256 devices in a mesh: shot: 8 (over y, core), rcv: 32 (over x, z).
Axes of the slice: x: 4, y: 4, z: 8, core: 2. Of those that a mesh axis runs over, the one named last changes fastest.
Arguments:
- blended: float32 [48, 512, 2048], P('shot', 'rcv'), may hold values from -60 to 60
- partners: int32 [48, 4], replicated, may hold values from -1 to 47, as said below
- offsets: int32 [48, 4], replicated, may hold values from -1024 to 1024
- fk_mask: int32 [2, 48, 1024], replicated, may hold values 0 or 1
Outputs:
- deblended: float32 [48, 512, 2048], P('shot', 'rcv')
- residual: float32 [48, 512, 2048], P('shot', 'rcv')
The draws below stay inside these ranges and needn't reach their ends.
Inputs may be any that keep to these rules, and one draw needn't show every extreme that they name: `partners`: entries -1 mark empty slots and come after the filled ones; every other entry names a shot other than the row's own, at most 3 shots away, and no shot twice in a row; some shot has all 4 slots filled; the last shot is always named.
All inputs are finite; a program needn't handle non-finite values.
Results may differ from the reference program's by a relative error of at most 0.0003.
Values sent between devices are 32-bit elements; how exact they have to be, the bound alone decides.
A program may use at most 64 MiB of HBM per device.

```python
import math
import jax
import jax.numpy as jnp
from jax import lax

RECV_DEV = 16
SAMPLES = 2048
ITERATIONS = 2
PARTNERS = 4
HALO_SHOTS = 3
FREQUENCIES = 1024
SHOT_TOTAL = 48
RECV_TOTAL = 512


def draw_blended(key, part):
    key = jax.random.fold_in(key, 11)
    key_shot, key_recv, key_base = jax.random.split(key, 3)
    shot_scale = jnp.exp(jax.random.uniform(key_shot, (SHOT_TOTAL,), jnp.float32, math.log(0.3), math.log(3.0)))
    position = jnp.arange(RECV_TOTAL, dtype=jnp.float32) / max(RECV_TOTAL - 1, 1)
    recv_scale = jnp.exp(jax.random.uniform(key_recv, (RECV_TOTAL,), jnp.float32, math.log(0.6), math.log(1.8)))
    recv_scale = recv_scale * (0.6 + 1.2 * position)
    shape = (SHOT_TOTAL, RECV_TOTAL, SAMPLES)
    base = jnp.clip(jax.random.normal(key_base, shape, jnp.float32), -6.0, 6.0)
    return (base * shot_scale[:, None, None] * recv_scale[None, :, None]).astype(jnp.float32)


def draw_partners(key, part):
    key = jax.random.fold_in(key, 5)
    key_score, key_count, key_forced = jax.random.split(key, 3)
    width = 2 * HALO_SHOTS
    shot_index = jnp.arange(SHOT_TOTAL, dtype=jnp.int32)
    candidate = jnp.concatenate([jnp.arange(-HALO_SHOTS, 0, dtype=jnp.int32), jnp.arange(1, HALO_SHOTS + 1, dtype=jnp.int32)])
    target = shot_index[:, None] + candidate[None, :]
    valid = (target >= 0) & (target < SHOT_TOTAL)
    score = jax.random.randint(key_score, (SHOT_TOTAL, width), 0, 1 << 20) * width + jnp.arange(width, dtype=jnp.int32)[None, :]
    favoured = (shot_index[:, None] == SHOT_TOTAL - 2) & (jnp.arange(width, dtype=jnp.int32)[None, :] == HALO_SHOTS)
    score = jnp.where(favoured, (1 << 21) * width, score)
    score = jnp.where(valid, score, -1)
    order = jnp.argsort(-score, axis=1, stable=True)[:, :PARTNERS]
    chosen = jnp.take_along_axis(target, order, axis=1)
    chosen_valid = jnp.take_along_axis(valid, order, axis=1)
    count = jax.random.randint(key_count, (SHOT_TOTAL,), 1, PARTNERS + 1)
    forced = jax.random.randint(key_forced, (), HALO_SHOTS, SHOT_TOTAL - HALO_SHOTS)
    count = jnp.where(shot_index == forced, PARTNERS, count)
    slot_index = jnp.arange(PARTNERS, dtype=jnp.int32)
    keep_slot = (slot_index[None, :] < count[:, None]) & chosen_valid
    return jnp.where(keep_slot, chosen, -1).astype(jnp.int32)


def place_ends(entries, rng, least, high):
    spot = [jax.random.randint(jax.random.fold_in(rng, axis), (), 0, length) for axis, length in enumerate(entries.shape)]
    main_axis = entries.shape.index(max(entries.shape))
    next_to = spot[:main_axis] + [(spot[main_axis] + 1) % entries.shape[main_axis]] + spot[main_axis + 1:]
    return entries.at[tuple(spot)].set(least).at[tuple(next_to)].set(high)


def setup_inputs(seed: int = 0) -> dict:
    arg_keys = jax.random.split(jax.random.key(seed), 5)
    blended = draw_blended(jax.random.fold_in(arg_keys[4], 71), 0)
    partners = draw_partners(jax.random.fold_in(arg_keys[4], 71), 0)
    offsets = place_ends(jax.random.randint(arg_keys[2], (SHOT_TOTAL, PARTNERS), 0 - SAMPLES // 2, SAMPLES // 2 + 1), jax.random.fold_in(arg_keys[2], 1), 0 - SAMPLES // 2, (SAMPLES // 2 + 1) - 1).astype(jnp.int32)
    fk_mask = place_ends((jax.random.randint(arg_keys[3], (ITERATIONS, SHOT_TOTAL, FREQUENCIES), 0, 2) < 1).astype(jnp.int32), jax.random.fold_in(arg_keys[3], 1), 0, 1)
    return {"blended": blended, "partners": partners, "offsets": offsets, "fk_mask": fk_mask}


HIGH = lax.Precision.HIGHEST


def angle_tables(sample_count, first_freq, freq_width):
    freq_index = first_freq + jnp.arange(freq_width, dtype=jnp.int32)
    sample_index = jnp.arange(sample_count, dtype=jnp.int32)
    phase = (sample_index[:, None] * freq_index[None, :]) % sample_count
    theta = phase.astype(jnp.float32) * (2.0 * math.pi / sample_count)
    return jnp.cos(theta), jnp.sin(theta)


def shot_tables(shot_count):
    shot_index = jnp.arange(shot_count, dtype=jnp.int32)
    phase = (shot_index[:, None] * shot_index[None, :]) % shot_count
    theta = phase.astype(jnp.float32) * (2.0 * math.pi / shot_count)
    return jnp.cos(theta), jnp.sin(theta)


def shot_mix(matrix, field):
    return jnp.einsum('ms,snf->mnf', matrix, field, precision=HIGH)


def wavenumber_mask(real_part, imag_part, kept_mask, cos_shot, sin_shot, shot_count):
    upper_re = shot_mix(cos_shot, real_part) + shot_mix(sin_shot, imag_part)
    upper_im = shot_mix(cos_shot, imag_part) - shot_mix(sin_shot, real_part)
    masked_re = kept_mask[:, None, :] * upper_re
    masked_im = kept_mask[:, None, :] * upper_im
    inverse_re = (shot_mix(cos_shot, masked_re) - shot_mix(sin_shot, masked_im)) / shot_count
    inverse_im = (shot_mix(cos_shot, masked_im) + shot_mix(sin_shot, masked_re)) / shot_count
    return inverse_re, inverse_im


def coherence_filter(field, kept_mask):
    shot_count, recv_piece, sample_count = field.shape
    freq_count = sample_count // 2
    traces = field.reshape(shot_count * recv_piece, sample_count)
    cos_time, sin_time = angle_tables(sample_count, 0, freq_count)
    cos_shot, sin_shot = shot_tables(shot_count)
    real_part = jnp.dot(traces, cos_time, precision=HIGH).reshape(shot_count, recv_piece, freq_count)
    imag_part = -jnp.dot(traces, sin_time, precision=HIGH).reshape(shot_count, recv_piece, freq_count)
    inverse_re, inverse_im = wavenumber_mask(real_part, imag_part, kept_mask, cos_shot, sin_shot, shot_count)
    summed = jnp.dot(inverse_re.reshape(-1, freq_count), cos_time.T, precision=HIGH)
    summed = summed - jnp.dot(inverse_im.reshape(-1, freq_count), sin_time.T, precision=HIGH)
    return (summed * (2.0 / sample_count)).reshape(shot_count, recv_piece, sample_count)


def shift_records(records, delays, sample_count):
    margin = sample_count // 2
    extended = jnp.pad(records, ((0, 0), (0, 0), (margin, margin)))

    def one_shift(padded_row, delay_one):
        return lax.dynamic_slice_in_dim(padded_row, (margin - delay_one).astype(jnp.int32), sample_count, 1)

    return jax.vmap(one_shift)(extended, delays)


def blend_image(own_field, source, where_rows, present, delays):
    summed = own_field
    for slot_index in range(PARTNERS):
        records = jnp.take(source, where_rows[:, slot_index], axis=0)
        shifted = shift_records(records, delays[:, slot_index], own_field.shape[2])
        summed = summed + present[:, slot_index][:, None, None] * shifted
    return summed


def reference(blended, partners, offsets, fk_mask):
    groups = RECV_TOTAL // RECV_DEV
    present = (partners >= 0).astype(jnp.float32)
    where_rows = jnp.maximum(partners, 0).astype(jnp.int32)
    estimate = jnp.zeros_like(blended)
    residual = blended
    for sweep in range(ITERATIONS):
        kept_mask = fk_mask[sweep].astype(jnp.float32)
        blocks = residual.reshape(SHOT_TOTAL, groups, RECV_DEV, SAMPLES).transpose(1, 0, 2, 3)
        filtered = lax.map(lambda block_field: coherence_filter(block_field, kept_mask), blocks)
        filtered = filtered.transpose(1, 0, 2, 3).reshape(SHOT_TOTAL, RECV_TOTAL, SAMPLES)
        image = blend_image(filtered, filtered, where_rows, present, offsets)
        step_length = jnp.sum(residual * image) / jnp.sum(image * image)
        estimate = estimate + step_length * filtered
        residual = residual - step_length * image
    return estimate, residual
```

```python
import math

import jax
import jax.numpy as jnp
import numpy as np
from jax import lax
from jax.experimental import pallas as pl
from jax.experimental.pallas import tpu as pltpu
from jax.sharding import PartitionSpec as P

ITERATIONS = 2
PARTNERS = 4
SHOTS = 48
SAMPLES = 2048
FREQS = 1024
ROWS = 16
GROUPS = 8
PITCH = 40
BASE = 16
TRACES = 2 * SHOTS

MESH = pl.DeviceIdType.MESH
BF16 = jnp.bfloat16
F32 = jnp.float32


def group_frequencies():
    j = np.arange(64)
    rows = [np.concatenate([16 * j, 8 + 16 * j])]
    for g in range(1, GROUPS):
        rows.append(np.concatenate([g + 16 * j, 16 - g + 16 * j]))
    return np.stack(rows)


def split_np(table):
    table = table.astype(np.float32)
    high = table.astype(jnp.bfloat16)
    low = (table - high.astype(np.float32)).astype(jnp.bfloat16)
    return high, low


def time_tables():
    kept = group_frequencies()
    n2 = np.arange(128)
    out = np.zeros((GROUPS, 256, 256))
    for g in range(GROUPS):
        phase = (n2[:, None] * kept[g][None, :]) % SAMPLES
        cos = np.cos(2 * np.pi * phase / SAMPLES)
        sin = np.sin(2 * np.pi * phase / SAMPLES)
        first = np.arange(128) < 64
        if g == 0:
            out[g, :128, :128] = np.where(first, cos, 0)
            out[g, :128, 128:] = np.where(first, -sin, 0)
            out[g, 128:, :128] = np.where(first, 0, cos)
            out[g, 128:, 128:] = np.where(first, 0, -sin)
        else:
            out[g, :128, :128] = cos
            out[g, :128, 128:] = -sin
            out[g, 128:, :128] = np.where(first, sin, -sin)
            out[g, 128:, 128:] = np.where(first, cos, -cos)
    return split_np(out)


def shot_tables():
    index = np.arange(SHOTS)
    phase = 2 * np.pi * ((index[:, None] * index[None, :]) % SHOTS) / SHOTS
    cos, sin = np.cos(phase), np.sin(phase)
    forward = np.block([[cos, sin], [-sin, cos]])
    inverse = np.block([[cos, -sin], [sin, cos]]) / (SHOTS * FREQS)
    return np.stack([forward, inverse])


def shot_operands():
    high, low = split_np(shot_tables())
    return np.concatenate([high, high], axis=2), low


def mask_order():
    order = group_frequencies().reshape(-1)
    out = np.zeros((FREQS, FREQS), np.float32)
    out[order, np.arange(FREQS)] = 1
    return out.astype(jnp.bfloat16)


C1, C2, C3 = (math.cos(math.pi * i / 8) for i in (1, 2, 3))


def radix16(x):
    a = [x[n] + x[n + 8] for n in range(8)]
    b = [x[n] - x[n + 8] for n in range(8)]
    e = [a[n] + a[n + 4] for n in range(4)]
    f = [a[n] - a[n + 4] for n in range(4)]
    p02, p13 = e[0] + e[2], e[1] + e[3]
    y0, y8 = p02 + p13, p02 - p13
    re4, im4 = e[0] - e[2], e[3] - e[1]
    m, q = C2 * (f[1] - f[3]), C2 * (f[1] + f[3])
    re2, re6 = f[0] + m, f[0] - m
    im2, im6 = -f[2] - q, f[2] - q
    c = [None] + [b[n] - b[8 - n] for n in (1, 2, 3)]
    d = [None] + [b[n] + b[8 - n] for n in (1, 2, 3)]
    up, down = b[0] + C2 * c[2], b[0] - C2 * c[2]
    v, w = C1 * c[1] + C3 * c[3], C3 * c[1] - C1 * c[3]
    re1, re7, re3, re5 = up + v, up - v, down + w, down - w
    p, t = C3 * d[1] + C1 * d[3], C2 * d[2] + b[4]
    q, u = C1 * d[1] - C3 * d[3], C2 * d[2] - b[4]
    im1, im7, im3, im5 = -p - t, t - p, -q - u, u - q
    return [(y0, y8), (re1, im1), (re2, im2), (re3, im3), (re4, im4), (re5, im5), (re6, im6), (re7, im7)]


def radix16_back(z):
    (w0, w8), (re1, im1), (re2, im2), (re3, im3), (re4, im4), (re5, im5), (re6, im6), (re7, im7) = z
    plus, minus = w0 + w8, w0 - w8
    ee = [plus + re4, minus - im4, plus - re4, minus + im4]
    m, q = C2 * (re2 - re6), C2 * (im2 + im6)
    eo = [re2 + re6, m - q, im6 - im2, -m - q]
    even = [ee[n] + eo[n] for n in range(4)] + [ee[n] - eo[n] for n in range(4)]
    s17, d17, s35, d35 = re1 + re7, re1 - re7, re3 + re5, re3 - re5
    t17, g17, t35, g35 = im1 + im7, im1 - im7, im3 + im5, im3 - im5
    pc = [None, C1 * d17 + C3 * d35, C2 * (s17 - s35), C3 * d17 - C1 * d35]
    ps = [None, C3 * t17 + C1 * t35, C2 * (g17 + g35), C1 * t17 - C3 * t35]
    odd = [None] * 8
    odd[0] = s17 + s35
    odd[4] = g35 - g17
    for n in (1, 2, 3):
        odd[n] = pc[n] - ps[n]
        odd[8 - n] = -pc[n] - ps[n]
    return [even[n] + odd[n] for n in range(8)] + [even[n] - odd[n] for n in range(8)]


def split(x):
    high = x.astype(BF16)
    return high, (x - high.astype(F32)).astype(BF16)


def dot(a, b):
    return lax.dot_general(a, b, (((1,), (0,)), ((), ())), preferred_element_type=F32)


def dot_t(a, b):
    return lax.dot_general(a, b, (((1,), (1,)), ((), ())), preferred_element_type=F32)


def fk_filter(sweep, res, out, kept, table_hi, table_lo, mix_hi, mix_lo, y_hi, y_lo, v, w, back):
    def forward_rows(block, _):
        recv, first = block // 3, (block % 3) * 256
        parts = []
        for half in range(2):
            x = [res[recv, pl.ds(first + half * 128 + n1, 8, stride=ROWS), :] for n1 in range(ROWS)]
            parts.append(radix16(x))
        row = pl.multiple_of(block * 16, 16)
        for g in range(GROUPS):
            for part in range(2):
                high, low = split(jnp.concatenate([parts[0][g][part], parts[1][g][part]], axis=0))
                y_hi[g, pl.ds(row, 16), part * 128:(part + 1) * 128] = high
                y_lo[g, pl.ds(row, 16), part * 128:(part + 1) * 128] = low
        return 0

    lax.fori_loop(0, TRACES // 16, forward_rows, 0)

    for g in range(GROUPS):
        z = dot(y_hi[g], table_hi[g]) + dot(y_lo[g], table_hi[g]) + dot(y_hi[g], table_lo[g])
        high, low = split(z)
        c = g * 256
        for source, at in ((high, 0), (low, 96)):
            v[at:at + 48, c:c + 128] = source[:48, :128]
            v[at:at + 48, c + 128:c + 256] = source[48:, :128]
            v[at + 48:at + 96, c:c + 128] = source[:48, 128:]
            v[at + 48:at + 96, c + 128:c + 256] = source[48:, 128:]

    for g in range(GROUPS):
        c = g * 256
        u = dot(mix_hi[0], v[:, c:c + 256]) + dot(mix_lo[0], v[:96, c:c + 256])
        keep = kept[sweep * SHOTS:(sweep + 1) * SHOTS, g * 128:(g + 1) * 128]
        keep = jnp.concatenate([keep, keep], axis=0)
        high, low = split(u * jnp.concatenate([keep, keep], axis=1))
        w[:96, c:c + 256] = high
        w[96:, c:c + 256] = low

    for g in range(GROUPS):
        c = g * 256
        z = dot(mix_hi[1], w[:, c:c + 256]) + dot(mix_lo[1], w[:96, c:c + 256])
        high, low = split(z)
        for source, at in ((high, y_hi), (low, y_lo)):
            at[g, :48, :128] = source[:48, :128]
            at[g, 48:, :128] = source[:48, 128:]
            at[g, :48, 128:] = source[48:, :128]
            at[g, 48:, 128:] = source[48:, 128:]

    for g in range(GROUPS):
        back[g] = (
            dot_t(y_hi[g], table_hi[g]) + dot_t(y_lo[g], table_hi[g]) + dot_t(y_hi[g], table_lo[g])
        )

    def inverse_rows(block, _):
        recv = block // 6
        shot = (block % 6) * 8
        row = pl.multiple_of(block * 8, 8)
        z = [
            (back[g, pl.ds(row, 8), 0:128], back[g, pl.ds(row, 8), 128:256])
            for g in range(GROUPS)
        ]
        x = radix16_back(z)
        for n1 in range(ROWS):
            out[recv, pl.ds(shot * PITCH + BASE + n1, 8, stride=PITCH), :] = x[n1]
        return 0

    lax.fori_loop(0, TRACES // 8, inverse_rows, 0)


def blend(partners, offsets, q, res, image):
    lane = lax.broadcasted_iota(jnp.int32, (ROWS, 128), 1)

    def one_shot(shot, sums):
        num, den = sums
        where = []
        for j in range(PARTNERS):
            partner, delay = partners[shot, j], offsets[shot, j]
            trace = jnp.where(partner >= 0, partner, SHOTS)
            rest = delay & 127
            where.append((trace * PITCH + BASE - (delay >> 7), rest, lane < 128 - rest))
        for recv in range(2):
            own = pl.multiple_of(shot * PITCH + BASE, 8)
            g = q[recv, pl.ds(own, ROWS), :]
            for start, rest, near in where:
                here = q[recv, pl.ds(start, ROWS), :]
                before = q[recv, pl.ds(start - 1, ROWS), :]
                g = g + pltpu.roll(jnp.where(near, here, before), rest, 1)
            at = pl.ds(pl.multiple_of(shot * ROWS, ROWS), ROWS)
            image[recv, at, :] = g
            num = num + res[recv, at, :] * g
            den = den + g * g
        return num, den

    zero = jnp.zeros((ROWS, 128), F32)
    return lax.fori_loop(0, SHOTS, one_shot, (zero, zero), unroll=2)


def kernel(
    groups, planes, columns,
    partners, offsets, blended, fk_mask, table_hi_h, table_lo_h, order_h, mix_hi, mix_lo,
    out_d, out_r,
    staged, res, q1, q2, image, send_d, send_r, y_hi, y_lo, v, w, back,
    table_hi, table_lo, order, kept, sums_mine, sums_got,
    load_sem, in_send, in_recv, out_send, out_recv, own_sem, sum_send, sum_recv,
):
    me = lax.axis_index("shot")
    place = lax.axis_index("rcv")
    plane, column = place // columns, place % columns

    loads = [
        pltpu.make_async_copy(table_hi_h, table_hi, load_sem.at[0]),
        pltpu.make_async_copy(table_lo_h, table_lo, load_sem.at[1]),
        pltpu.make_async_copy(order_h, order, load_sem.at[2]),
    ]
    for load in loads:
        load.start()

    shot_peers = [((lax.rem(me + k, groups), place)) for k in range(1, groups)]
    column_peers = [(me, plane * columns + lax.rem(column + k, columns)) for k in range(1, columns)]
    plane_peers = [(me, lax.rem(plane + k, planes) * columns + column) for k in range(1, planes)]
    peers = shot_peers + column_peers + plane_peers
    barrier = pltpu.get_barrier_semaphore()
    for peer in peers:
        pl.semaphore_signal(barrier, inc=1, device_id=peer, device_id_type=MESH)

    for shot in range(6):
        for half in range(2):
            for n1 in range(ROWS):
                at = half * 8 * 96 + shot * ROWS + n1
                staged[pl.ds(at, 8, stride=96), :] = blended[
                    shot, half * 8:(half + 1) * 8, n1 * 128:(n1 + 1) * 128
                ]

    pl.semaphore_wait(barrier, len(peers))

    mine = pl.ds(pl.multiple_of(me * 96, 8), 96)
    copies = []
    for k in range(1, groups):
        peer = shot_peers[k - 1]
        for recv in range(2):
            copies.append(pltpu.make_async_remote_copy(
                src_ref=staged.at[pl.ds(pl.multiple_of(peer[0] * 192 + recv * 96, 8), 96)],
                dst_ref=res.at[recv, mine],
                send_sem=in_send.at[k - 1, recv],
                recv_sem=in_recv.at[k - 1, recv],
                device_id=peer, device_id_type=MESH,
            ))
            copies[-1].start()
    own = []
    for recv in range(2):
        own.append(pltpu.make_async_copy(
            staged.at[pl.ds(pl.multiple_of(me * 192 + recv * 96, 8), 96)],
            res.at[recv, mine], own_sem.at[recv],
        ))
        own[-1].start()

    q1[...] = jnp.zeros_like(q1)
    q2[...] = jnp.zeros_like(q2)
    for load in loads:
        load.wait()
    kept[...] = dot(fk_mask[...].astype(F32).astype(BF16), order[...])

    for copy in own:
        copy.wait()
    for copy in copies:
        copy.wait()

    def all_sum(sweep, num, den):
        mine_sum = jnp.concatenate([num[:8] + num[8:], den[:8] + den[8:]], axis=0)
        slot = 0
        for stage, stage_peers in enumerate((shot_peers, column_peers, plane_peers)):
            sums_mine[sweep, stage] = mine_sum
            moves = []
            for peer in stage_peers:
                moves.append(pltpu.make_async_remote_copy(
                    src_ref=sums_mine.at[sweep, stage], dst_ref=sums_got.at[sweep, slot],
                    send_sem=sum_send.at[sweep, slot], recv_sem=sum_recv.at[sweep, slot],
                    device_id=peer, device_id_type=MESH,
                ))
                moves[-1].start()
                slot += 1
            for i, move in enumerate(moves):
                move.wait()
                mine_sum = mine_sum + sums_got[sweep, slot - len(moves) + i]
        return jnp.sum(mine_sum[:8], keepdims=True) / jnp.sum(mine_sum[8:], keepdims=True)

    common = (kept, table_hi, table_lo, mix_hi, mix_lo, y_hi, y_lo, v, w, back)
    fk_filter(0, res, q1, *common)
    step1 = all_sum(0, *blend(partners, offsets, q1, res, image))
    res[...] = res[...] - step1 * image[...]
    fk_filter(1, res, q2, *common)
    step2 = all_sum(1, *blend(partners, offsets, q2, res, image))

    def finish(first_shot):
        for recv in range(2):
            for i in range(6):
                shot = first_shot + i
                data = pl.ds(pl.multiple_of(shot * PITCH + BASE, 8), ROWS)
                at = pl.ds(pl.multiple_of(shot * ROWS, ROWS), ROWS)
                send_d[recv, shot] = step1 * q1[recv, data, :] + step2 * q2[recv, data, :]
                send_r[recv, shot] = res[recv, at, :] - step2 * image[recv, at, :]

    copies = []
    for k in range(1, groups):
        peer = shot_peers[k - 1]
        finish(peer[0] * 6)
        for recv in range(2):
            for which, (source, target) in enumerate(((send_d, out_d), (send_r, out_r))):
                copies.append(pltpu.make_async_remote_copy(
                    src_ref=source.at[recv, pl.ds(peer[0] * 6, 6)],
                    dst_ref=target.at[:, pl.ds(pl.multiple_of((me * 2 + recv) * ROWS, ROWS), ROWS)],
                    send_sem=out_send.at[k - 1, recv, which],
                    recv_sem=out_recv.at[k - 1, recv, which],
                    device_id=peer, device_id_type=MESH,
                ))
                copies[-1].start()
    finish(me * 6)
    own = []
    for recv in range(2):
        for which, (source, target) in enumerate(((send_d, out_d), (send_r, out_r))):
            own.append(pltpu.make_async_copy(
                source.at[recv, pl.ds(me * 6, 6)],
                target.at[:, pl.ds(pl.multiple_of((me * 2 + recv) * ROWS, ROWS), ROWS)],
                own_sem.at[2 + recv * 2 + which],
            ))
            own[-1].start()
    for copy in own:
        copy.wait()
    for copy in copies:
        copy.wait()


def natural(d_rows, r_rows, d_out, r_out):
    for source, target in ((d_rows, d_out), (r_rows, r_out)):
        for half in range(2):
            for n1 in range(ROWS):
                target[0, half * 8:(half + 1) * 8, n1 * 128:(n1 + 1) * 128] = source[
                    0, pl.ds(half * 128 + n1, 8, stride=ROWS), :
                ]


def solution(mesh):
    groups = mesh.shape["shot"]
    columns = 8 if mesh.shape["rcv"] % 8 == 0 else mesh.shape["rcv"]
    planes = mesh.shape["rcv"] // columns
    slots = groups - 1 + columns - 1 + planes - 1
    table_hi, table_lo = time_tables()
    mix_hi, mix_lo = shot_operands()
    order = mask_order()

    def body(blended, partners, offsets, fk_mask):
        vmem = pl.BlockSpec(memory_space=pltpu.VMEM)
        smem = pl.BlockSpec(memory_space=pltpu.SMEM)
        hbm = pl.BlockSpec(memory_space=pl.ANY)
        rows = jax.ShapeDtypeStruct((6, 16 * ROWS, 128), F32)
        d_rows, r_rows = pl.pallas_call(
            lambda *refs: kernel(groups, planes, columns, *refs),
            out_shape=(rows, rows),
            in_specs=[smem, smem, vmem, vmem, hbm, hbm, hbm, vmem, vmem],
            out_specs=(hbm, hbm),
            scratch_shapes=[
                pltpu.VMEM((16 * 96, 128), F32),
                pltpu.VMEM((2, SHOTS * ROWS, 128), F32),
                pltpu.VMEM((2, (SHOTS + 1) * PITCH, 128), F32),
                pltpu.VMEM((2, (SHOTS + 1) * PITCH, 128), F32),
                pltpu.VMEM((2, SHOTS * ROWS, 128), F32),
                pltpu.VMEM((2, SHOTS, ROWS, 128), F32),
                pltpu.VMEM((2, SHOTS, ROWS, 128), F32),
                pltpu.VMEM((GROUPS, TRACES, 256), BF16),
                pltpu.VMEM((GROUPS, TRACES, 256), BF16),
                pltpu.VMEM((192, 2 * FREQS), BF16),
                pltpu.VMEM((192, 2 * FREQS), BF16),
                pltpu.VMEM((GROUPS, TRACES, 256), F32),
                pltpu.VMEM((GROUPS, 256, 256), BF16),
                pltpu.VMEM((GROUPS, 256, 256), BF16),
                pltpu.VMEM((FREQS, FREQS), BF16),
                pltpu.VMEM((ITERATIONS * SHOTS, FREQS), F32),
                pltpu.VMEM((ITERATIONS, 3, 16, 128), F32),
                pltpu.VMEM((ITERATIONS, slots, 16, 128), F32),
                pltpu.SemaphoreType.DMA((3,)),
                pltpu.SemaphoreType.DMA((groups - 1, 2)),
                pltpu.SemaphoreType.DMA((groups - 1, 2)),
                pltpu.SemaphoreType.DMA((groups - 1, 2, 2)),
                pltpu.SemaphoreType.DMA((groups - 1, 2, 2)),
                pltpu.SemaphoreType.DMA((6,)),
                pltpu.SemaphoreType.DMA((ITERATIONS, slots)),
                pltpu.SemaphoreType.DMA((ITERATIONS, slots)),
            ],
            compiler_params=pltpu.CompilerParams(
                collective_id=0, has_side_effects=True, vmem_limit_bytes=48 * 2**20
            ),
            name="deblend",
        )(
            partners, offsets, blended, fk_mask.reshape(ITERATIONS * SHOTS, FREQS),
            jnp.asarray(table_hi), jnp.asarray(table_lo), jnp.asarray(order),
            jnp.asarray(mix_hi), jnp.asarray(mix_lo),
        )
        out = jax.ShapeDtypeStruct(blended.shape, F32)
        row_spec = pl.BlockSpec((1, 16 * ROWS, 128), lambda i: (i, 0, 0))
        out_spec = pl.BlockSpec((1, 16, SAMPLES), lambda i: (i, 0, 0))
        return pl.pallas_call(
            natural,
            grid=(6,),
            out_shape=(out, out),
            in_specs=[row_spec, row_spec],
            out_specs=(out_spec, out_spec),
            name="natural_order",
        )(d_rows, r_rows)

    in_specs = (P("shot", "rcv", None), P(), P(), P())
    out_specs = (P("shot", "rcv", None), P("shot", "rcv", None))
    return jax.shard_map(body, mesh=mesh, in_specs=in_specs, out_specs=out_specs, check_vma=False)
```

```python
import math

import jax
import jax.numpy as jnp
import numpy as np
from jax import lax
from jax.experimental import pallas as pl
from jax.experimental.pallas import tpu as pltpu
from jax.sharding import PartitionSpec as P

ITERATIONS = 2
PARTNERS = 4
SHOTS = 48
SAMPLES = 2048
FREQS = 1024
ROWS = 16
GROUPS = 8
PITCH = 40
BASE = 16
TRACES = 2 * SHOTS

MESH = pl.DeviceIdType.MESH
BF16 = jnp.bfloat16
F32 = jnp.float32


def group_frequencies():
    j = np.arange(64)
    rows = [np.concatenate([16 * j, 8 + 16 * j])]
    for g in range(1, GROUPS):
        rows.append(np.concatenate([g + 16 * j, 16 - g + 16 * j]))
    return np.stack(rows)


def split_np(table):
    table = table.astype(np.float32)
    high = table.astype(jnp.bfloat16)
    low = (table - high.astype(np.float32)).astype(jnp.bfloat16)
    return high, low


def time_tables():
    kept = group_frequencies()
    n2 = np.arange(128)
    out = np.zeros((GROUPS, 256, 256))
    for g in range(GROUPS):
        phase = (n2[:, None] * kept[g][None, :]) % SAMPLES
        cos = np.cos(2 * np.pi * phase / SAMPLES)
        sin = np.sin(2 * np.pi * phase / SAMPLES)
        first = np.arange(128) < 64
        if g == 0:
            out[g, :128, :128] = np.where(first, cos, 0)
            out[g, :128, 128:] = np.where(first, -sin, 0)
            out[g, 128:, :128] = np.where(first, 0, cos)
            out[g, 128:, 128:] = np.where(first, 0, -sin)
        else:
            out[g, :128, :128] = cos
            out[g, :128, 128:] = -sin
            out[g, 128:, :128] = np.where(first, sin, -sin)
            out[g, 128:, 128:] = np.where(first, cos, -cos)
    return split_np(out)


def shot_tables():
    index = np.arange(SHOTS)
    phase = 2 * np.pi * ((index[:, None] * index[None, :]) % SHOTS) / SHOTS
    cos, sin = np.cos(phase), np.sin(phase)
    forward = np.block([[cos, sin], [-sin, cos]])
    inverse = np.block([[cos, -sin], [sin, cos]]) / (SHOTS * FREQS)
    return np.stack([forward, inverse])


def shot_operands():
    high, low = split_np(shot_tables())
    return np.concatenate([high, high], axis=2), low


def mask_order():
    order = group_frequencies().reshape(-1)
    out = np.zeros((FREQS, FREQS), np.float32)
    out[order, np.arange(FREQS)] = 1
    return out.astype(jnp.bfloat16)


C1, C2, C3 = (math.cos(math.pi * i / 8) for i in (1, 2, 3))


def radix16(x):
    a = [x[n] + x[n + 8] for n in range(8)]
    b = [x[n] - x[n + 8] for n in range(8)]
    e = [a[n] + a[n + 4] for n in range(4)]
    f = [a[n] - a[n + 4] for n in range(4)]
    p02, p13 = e[0] + e[2], e[1] + e[3]
    y0, y8 = p02 + p13, p02 - p13
    re4, im4 = e[0] - e[2], e[3] - e[1]
    m, q = C2 * (f[1] - f[3]), C2 * (f[1] + f[3])
    re2, re6 = f[0] + m, f[0] - m
    im2, im6 = -f[2] - q, f[2] - q
    c = [None] + [b[n] - b[8 - n] for n in (1, 2, 3)]
    d = [None] + [b[n] + b[8 - n] for n in (1, 2, 3)]
    up, down = b[0] + C2 * c[2], b[0] - C2 * c[2]
    v, w = C1 * c[1] + C3 * c[3], C3 * c[1] - C1 * c[3]
    re1, re7, re3, re5 = up + v, up - v, down + w, down - w
    p, t = C3 * d[1] + C1 * d[3], C2 * d[2] + b[4]
    q, u = C1 * d[1] - C3 * d[3], C2 * d[2] - b[4]
    im1, im7, im3, im5 = -p - t, t - p, -q - u, u - q
    return [(y0, y8), (re1, im1), (re2, im2), (re3, im3), (re4, im4), (re5, im5), (re6, im6), (re7, im7)]


def radix16_back(z):
    (w0, w8), (re1, im1), (re2, im2), (re3, im3), (re4, im4), (re5, im5), (re6, im6), (re7, im7) = z
    plus, minus = w0 + w8, w0 - w8
    ee = [plus + re4, minus - im4, plus - re4, minus + im4]
    m, q = C2 * (re2 - re6), C2 * (im2 + im6)
    eo = [re2 + re6, m - q, im6 - im2, -m - q]
    even = [ee[n] + eo[n] for n in range(4)] + [ee[n] - eo[n] for n in range(4)]
    s17, d17, s35, d35 = re1 + re7, re1 - re7, re3 + re5, re3 - re5
    t17, g17, t35, g35 = im1 + im7, im1 - im7, im3 + im5, im3 - im5
    pc = [None, C1 * d17 + C3 * d35, C2 * (s17 - s35), C3 * d17 - C1 * d35]
    ps = [None, C3 * t17 + C1 * t35, C2 * (g17 + g35), C1 * t17 - C3 * t35]
    odd = [None] * 8
    odd[0] = s17 + s35
    odd[4] = g35 - g17
    for n in (1, 2, 3):
        odd[n] = pc[n] - ps[n]
        odd[8 - n] = -pc[n] - ps[n]
    return [even[n] + odd[n] for n in range(8)] + [even[n] - odd[n] for n in range(8)]


def split(x):
    high = x.astype(BF16)
    return high, (x - high.astype(F32)).astype(BF16)


def dot(a, b):
    return lax.dot_general(a, b, (((1,), (0,)), ((), ())), preferred_element_type=F32)


HALO = 3
SENT = 9 * ROWS
NEAR = 12
EARLY = 8


def forward(source, u, table_hi, table_lo, mix_hi, mix_lo, y_hi, y_lo, v):
    def forward_rows(block, _):
        recv, first = block // 3, (block % 3) * 256
        parts = []
        for half in range(2):
            x = [source[recv, pl.ds(first + half * 128 + n1, 8, stride=ROWS), :] for n1 in range(ROWS)]
            parts.append(radix16(x))
        row = pl.multiple_of(block * 16, 16)
        for g in range(GROUPS):
            for part in range(2):
                high, low = split(jnp.concatenate([parts[0][g][part], parts[1][g][part]], axis=0))
                y_hi[g, pl.ds(row, 16), part * 128:(part + 1) * 128] = high
                y_lo[g, pl.ds(row, 16), part * 128:(part + 1) * 128] = low
        return 0

    lax.fori_loop(0, TRACES // 16, forward_rows, 0)

    for g in range(GROUPS):
        z = dot(y_hi[g], table_hi[g]) + dot(y_lo[g], table_hi[g]) + dot(y_hi[g], table_lo[g])
        high, low = split(z)
        c = g * 256
        for source_rows, at in ((high, 0), (low, 96)):
            v[at:at + 48, c:c + 128] = source_rows[:48, :128]
            v[at:at + 48, c + 128:c + 256] = source_rows[48:, :128]
            v[at + 48:at + 96, c:c + 128] = source_rows[:48, 128:]
            v[at + 48:at + 96, c + 128:c + 256] = source_rows[48:, 128:]

    for g in range(GROUPS):
        c = g * 256
        u[g] = dot(mix_hi[0], v[:, c:c + 256]) + dot(mix_lo[0], v[:96, c:c + 256])


def inverse(spectrum, sweep, q, sent, kept, back_hi, back_lo, mix_hi, mix_lo, y_hi, y_lo, w, back):
    for g in range(GROUPS):
        c = g * 256
        keep = kept[sweep * SHOTS:(sweep + 1) * SHOTS, g * 128:(g + 1) * 128]
        keep = jnp.concatenate([keep, keep], axis=0)
        high, low = split(spectrum(g) * jnp.concatenate([keep, keep], axis=1))
        w[:96, c:c + 256] = high
        w[96:, c:c + 256] = low

    for g in range(GROUPS):
        c = g * 256
        z = dot(mix_hi[1], w[:, c:c + 256]) + dot(mix_lo[1], w[:96, c:c + 256])
        high, low = split(z)
        for source, at in ((high, y_hi), (low, y_lo)):
            at[g, :48, :128] = source[:48, :128]
            at[g, 48:, :128] = source[:48, 128:]
            at[g, :48, 128:] = source[48:, :128]
            at[g, 48:, 128:] = source[48:, 128:]

    for g in range(GROUPS):
        back[g] = dot(y_hi[g], back_hi[g]) + dot(y_lo[g], back_hi[g]) + dot(y_hi[g], back_lo[g])

    def inverse_rows(block, _):
        recv = block // 6
        shot = (block % 6) * 8
        row = pl.multiple_of(block * 8, 8)
        z = [
            (back[g, pl.ds(row, 8), 0:128], back[g, pl.ds(row, 8), 128:256])
            for g in range(GROUPS)
        ]
        x = radix16_back(z)
        for n1 in range(ROWS):
            q[recv, pl.ds(shot * PITCH + BASE + n1, 8, stride=PITCH), :] = x[n1]
            sent[recv, pl.ds((shot + HALO) * ROWS + n1, 8, stride=ROWS), :] = x[n1]
        return 0

    lax.fori_loop(0, TRACES // 8, inverse_rows, 0)


def shift_terms(lane, partners, offsets, shot, first, blank):
    terms = []
    for j in range(PARTNERS):
        partner, delay = partners[j, shot], offsets[j, shot]
        trace = jnp.where(partner >= 0, jnp.clip(partner - first, 0, blank - 1), blank)
        rest = delay & 127
        terms.append((trace * PITCH + BASE - (delay >> 7), rest, lane < 128 - rest))
    return terms


def shifted(q, recv, term):
    start, rest, near = term
    here = q[recv, pl.ds(start, ROWS), :]
    before = q[recv, pl.ds(start - 1, ROWS), :]
    return pltpu.roll(jnp.where(near, here, before), rest, 1)


def blend_sums(partners, offsets, q, residual, image):
    lane = lax.broadcasted_iota(jnp.int32, (ROWS, 128), 1)
    chunk = 8

    def shots(block, sums):
        num, den = sums
        terms = [
            shift_terms(lane, partners, offsets, block * chunk + i, 0, SHOTS) for i in range(chunk)
        ]
        for i in range(chunk):
            shot = block * chunk + i
            for recv in range(2):
                g = q[recv, pl.ds(pl.multiple_of(shot * PITCH + BASE, 8), ROWS), :]
                for term in terms[i]:
                    g = g + shifted(q, recv, term)
                at = pl.ds(pl.multiple_of(shot * ROWS, ROWS), ROWS)
                num = num + residual(recv, at) * g
                den = den + g * g
                if image is not None:
                    image[recv, at, :] = g
        return num, den

    zero = jnp.zeros((ROWS, 128), F32)
    num, den = lax.fori_loop(0, SHOTS // chunk, shots, (zero, zero))

    def fold(x):
        return x[:4] + x[4:8] + x[8:12] + x[12:]

    return jnp.concatenate([fold(num), fold(den)], axis=0)


def kernel(
    groups,
    partners, offsets, blended_h, fk_mask_h, order_h, tables_h, mix_hi, mix_lo,
    out_d, out_r,
    blended, fk_mask, staged, res, q, image, sent1, sent2, got1, got2, more1, more2, near_d, rows_r,
    y_hi, y_lo, v, w, back, u0, u1, tables, order, kept, sums_mine, sums_got,
    load_sem, in_send, in_recv, bulk_send, bulk_recv, more_send, more_recv, own_sem,
    sum_send, sum_recv,
):
    me = lax.axis_index("shot")
    place = lax.axis_index("rcv")
    places = lax.axis_size("rcv")
    core = lax.rem(me, 2)
    mate = (me + 1 - 2 * core, place)
    shot_peers = [(lax.rem(me + k, groups), place) for k in range(1, groups)]
    place_peers = [(me, lax.rem(place + k, places)) for k in range(1, places)]
    peers = shot_peers + place_peers

    first_load = pltpu.make_async_copy(blended_h, blended, load_sem.at[0])
    first_load.start()
    loads = [
        pltpu.make_async_copy(fk_mask_h, fk_mask, load_sem.at[1]),
        pltpu.make_async_copy(order_h, order, load_sem.at[2]),
        pltpu.make_async_copy(tables_h, tables, load_sem.at[3]),
    ]

    barrier = pltpu.get_barrier_semaphore()
    for peer in peers:
        pl.semaphore_signal(barrier, inc=1, device_id=peer, device_id_type=MESH)

    first_load.wait()
    for load in loads:
        load.start()
    for shot in range(6):
        for half in range(2):
            for n1 in range(ROWS):
                at = half * 8 * 96 + shot * ROWS + n1
                staged[pl.ds(at, 8, stride=96), :] = blended[
                    shot, half * 8:(half + 1) * 8, n1 * 128:(n1 + 1) * 128
                ]

    pl.semaphore_wait(barrier, len(peers))

    mine = pl.ds(pl.multiple_of(me * 96, 8), 96)
    copies = []
    for k in range(1, groups):
        peer = shot_peers[k - 1]
        for recv in range(2):
            copies.append(pltpu.make_async_remote_copy(
                src_ref=staged.at[pl.ds(pl.multiple_of(peer[0] * 192 + recv * 96, 8), 96)],
                dst_ref=res.at[recv, mine],
                send_sem=in_send.at[k - 1, recv],
                recv_sem=in_recv.at[k - 1, recv],
                device_id=peer, device_id_type=MESH,
            ))
            copies[-1].start()
    own = []
    for recv in range(2):
        own.append(pltpu.make_async_copy(
            staged.at[pl.ds(pl.multiple_of(me * 192 + recv * 96, 8), 96)],
            res.at[recv, mine], own_sem.at[recv],
        ))
        own[-1].start()

    q[...] = jnp.zeros_like(q)
    near_d[...] = jnp.zeros_like(near_d)
    for sent in (sent1, sent2):
        for recv in range(2):
            blank = jnp.zeros((HALO * ROWS, 128), F32)
            sent[recv, :HALO * ROWS, :] = blank
            sent[recv, (HALO + SHOTS) * ROWS:, :] = blank
    for load in loads:
        load.wait()
    kept[...] = dot(fk_mask[...].astype(F32).astype(BF16), order[...])

    for copy in own:
        copy.wait()
    for copy in copies:
        copy.wait()

    def bulk_copies(field, sent, got):
        moves = []
        for k in range(1, groups):
            peer = shot_peers[k - 1]
            for recv in range(2):
                start = (12 * (peer[0] // 2) + 9 * lax.rem(peer[0], 2)) * ROWS
                moves.append(pltpu.make_async_remote_copy(
                    src_ref=sent.at[recv, pl.ds(pl.multiple_of(start, 8), SENT)],
                    dst_ref=got.at[me * 2 + recv],
                    send_sem=bulk_send.at[field, k - 1, recv],
                    recv_sem=bulk_recv.at[field, k - 1, recv],
                    device_id=peer, device_id_type=MESH,
                ))
        return moves

    def own_copies(field, sent, got):
        moves = []
        for recv in range(2):
            start = (12 * (me // 2) + 9 * core) * ROWS
            moves.append(pltpu.make_async_copy(
                sent.at[recv, pl.ds(pl.multiple_of(start, 8), SENT)],
                got.at[me * 2 + recv], own_sem.at[2 + field * 2 + recv],
            ))
            moves[-1].start()
        return moves

    def sum_start(sweep, stage, value):
        sums_mine[sweep, stage] = value
        first = 0 if stage == 0 else len(place_peers)
        moves = []
        for i, peer in enumerate((place_peers, shot_peers)[stage]):
            moves.append(pltpu.make_async_remote_copy(
                src_ref=sums_mine.at[sweep, stage], dst_ref=sums_got.at[sweep, first + i],
                send_sem=sum_send.at[sweep, first + i], recv_sem=sum_recv.at[sweep, first + i],
                device_id=peer, device_id_type=MESH,
            ))
            moves[-1].start()
        return moves

    def sum_end(sweep, stage, value, moves):
        first = 0 if stage == 0 else len(place_peers)
        for i, move in enumerate(moves):
            move.wait_recv()
            value = value + sums_got[sweep, first + i]
        return value

    def ratio(value):
        return jnp.sum(value[:4], keepdims=True) / jnp.sum(value[4:], keepdims=True)

    def more_copy(field, got, more):
        at = pl.ds(pl.multiple_of(6 * (1 - core) * ROWS, 8), HALO * ROWS)
        move = pltpu.make_async_remote_copy(
            src_ref=got.at[:, at], dst_ref=more, send_sem=more_send.at[field],
            recv_sem=more_recv.at[field], device_id=mate, device_id_type=MESH,
        )
        move.start()
        return move

    ahead = (tables.at[0], tables.at[1], mix_hi, mix_lo, y_hi, y_lo, v)
    behind = (kept, tables.at[2], tables.at[3], mix_hi, mix_lo, y_hi, y_lo, w, back)

    forward(res, u0, *ahead)
    inverse(lambda g: u0[g], 0, q, sent1, *behind)
    bulk1 = bulk_copies(0, sent1, got1)
    for move in bulk1[:EARLY]:
        move.start()
    own1 = own_copies(0, sent1, got1)
    value = blend_sums(partners, offsets, q, lambda recv, at: res[recv, at, :], image)
    stage0 = sum_start(0, 0, value)
    forward(image, u1, *ahead)
    value = sum_end(0, 0, value, stage0)
    stage1 = sum_start(0, 1, value)
    for move in bulk1[EARLY:]:
        move.start()
    value = sum_end(0, 1, value, stage1)
    step1 = ratio(value)

    inverse(lambda g: u0[g] - step1 * u1[g], 1, q, sent2, *behind)
    bulk2 = bulk_copies(1, sent2, got2)
    for move in bulk2:
        move.start()
    own2 = own_copies(1, sent2, got2)
    value = blend_sums(
        partners, offsets, q, lambda recv, at: res[recv, at, :] - step1 * image[recv, at, :], None
    )
    stage2 = sum_start(1, 0, value)
    for move in own1:
        move.wait()
    for move in bulk1:
        move.wait()
    forward1 = more_copy(0, got1, more1)
    value = sum_end(1, 0, value, stage2)
    stage3 = sum_start(1, 1, value)
    for move in own2:
        move.wait()
    for move in bulk2:
        move.wait()
    forward2 = more_copy(1, got2, more2)
    value = sum_end(1, 1, value, stage3)
    step2 = ratio(value)

    def gather_direct(recv, _):
        for i in range(9):
            at = pl.ds(pl.multiple_of(recv * (NEAR + 1) * PITCH + (HALO * core + i) * PITCH + BASE, 8), ROWS)
            rows = slice(i * ROWS, (i + 1) * ROWS)
            near_d[0, at, :] = step1 * got1[recv, rows, :] + step2 * got2[recv, rows, :]
        return 0

    def gather_more(recv, _):
        for i in range(HALO):
            at = pl.ds(pl.multiple_of(recv * (NEAR + 1) * PITCH + (9 * (1 - core) + i) * PITCH + BASE, 8), ROWS)
            rows = slice(i * ROWS, (i + 1) * ROWS)
            near_d[0, at, :] = step1 * more1[recv, rows, :] + step2 * more2[recv, rows, :]
        return 0

    lax.fori_loop(0, 16, gather_direct, 0)
    forward1.wait()
    forward2.wait()
    lax.fori_loop(0, 16, gather_more, 0)

    lane = lax.broadcasted_iota(jnp.int32, (ROWS, 128), 1)
    first_shot = me * 6

    def finish(i, _):
        terms = shift_terms(lane, partners, offsets, first_shot + i, first_shot - HALO, NEAR)
        for recv in range(16):
            trace = recv * (NEAR + 1) * PITCH
            g = near_d[0, pl.ds(pl.multiple_of(trace + (HALO + i) * PITCH + BASE, 8), ROWS), :]
            for start, rest, near in terms:
                g = g + shifted(near_d, 0, (start + trace, rest, near))
            old = staged[pl.ds(pl.multiple_of(recv * 96 + i * ROWS, 8), ROWS), :]
            rows_r[recv * ROWS:(recv + 1) * ROWS, :] = old - g
        for half in range(2):
            for n1 in range(ROWS):
                at = (half * 8 * (NEAR + 1) + HALO + i) * PITCH + BASE + n1
                block = (i, slice(half * 8, (half + 1) * 8), slice(n1 * 128, (n1 + 1) * 128))
                out_d[block] = near_d[0, pl.ds(at, 8, stride=(NEAR + 1) * PITCH), :]
                out_r[block] = rows_r[pl.ds(half * 128 + n1, 8, stride=ROWS), :]
        return 0

    lax.fori_loop(0, 6, finish, 0)

    for move in stage0 + stage1 + stage2 + stage3:
        move.wait_send()


def solution(mesh):
    groups = mesh.shape["shot"]
    peers = groups - 1 + mesh.shape["rcv"] - 1
    table_hi, table_lo = time_tables()
    tables = np.stack([table_hi, table_lo, table_hi.swapaxes(1, 2), table_lo.swapaxes(1, 2)])
    mix_hi, mix_lo = shot_operands()
    order = mask_order()

    def body(blended, partners, offsets, fk_mask):
        vmem = pl.BlockSpec(memory_space=pltpu.VMEM)
        smem = pl.BlockSpec(memory_space=pltpu.SMEM)
        hbm = pl.BlockSpec(memory_space=pltpu.HBM)
        out = jax.ShapeDtypeStruct(blended.shape, F32)
        dma = pltpu.SemaphoreType.DMA
        return pl.pallas_call(
            lambda *refs: kernel(groups, *refs),
            out_shape=(out, out),
            in_specs=[smem, smem, hbm, hbm, hbm, hbm, vmem, vmem],
            out_specs=(vmem, vmem),
            scratch_shapes=[
                pltpu.VMEM(blended.shape, F32),
                pltpu.VMEM((ITERATIONS * SHOTS, FREQS), jnp.int32),
                pltpu.VMEM((16 * 96, 128), F32),
                pltpu.VMEM((2, SHOTS * ROWS, 128), F32),
                pltpu.VMEM((2, (SHOTS + 1) * PITCH, 128), F32),
                pltpu.VMEM((2, SHOTS * ROWS, 128), F32),
                pltpu.VMEM((2, (SHOTS + 2 * HALO) * ROWS, 128), F32),
                pltpu.VMEM((2, (SHOTS + 2 * HALO) * ROWS, 128), F32),
                pltpu.VMEM((16, SENT, 128), F32),
                pltpu.VMEM((16, SENT, 128), F32),
                pltpu.VMEM((16, HALO * ROWS, 128), F32),
                pltpu.VMEM((16, HALO * ROWS, 128), F32),
                pltpu.VMEM((1, 16 * (NEAR + 1) * PITCH, 128), F32),
                pltpu.VMEM((16 * ROWS, 128), F32),
                pltpu.VMEM((GROUPS, TRACES, 256), BF16),
                pltpu.VMEM((GROUPS, TRACES, 256), BF16),
                pltpu.VMEM((192, 2 * FREQS), BF16),
                pltpu.VMEM((192, 2 * FREQS), BF16),
                pltpu.VMEM((GROUPS, TRACES, 256), F32),
                pltpu.VMEM((GROUPS, TRACES, 256), F32),
                pltpu.VMEM((GROUPS, TRACES, 256), F32),
                pltpu.VMEM((4, GROUPS, 256, 256), BF16),
                pltpu.VMEM((FREQS, FREQS), BF16),
                pltpu.VMEM((ITERATIONS * SHOTS, FREQS), F32),
                pltpu.VMEM((ITERATIONS, 2, 8, 128), F32),
                pltpu.VMEM((ITERATIONS, peers, 8, 128), F32),
                dma((4,)),
                dma((groups - 1, 2)),
                dma((groups - 1, 2)),
                dma((ITERATIONS, groups - 1, 2)),
                dma((ITERATIONS, groups - 1, 2)),
                dma((ITERATIONS,)),
                dma((ITERATIONS,)),
                dma((6,)),
                dma((ITERATIONS, peers)),
                dma((ITERATIONS, peers)),
            ],
            compiler_params=pltpu.CompilerParams(
                collective_id=0, has_side_effects=True, vmem_limit_bytes=56 * 2**20
            ),
            name="deblend",
        )(
            partners.T, offsets.T, blended, fk_mask.reshape(ITERATIONS * SHOTS, FREQS),
            jnp.asarray(order), jnp.asarray(tables), jnp.asarray(mix_hi), jnp.asarray(mix_lo),
        )

    in_specs = (P("shot", "rcv", None), P(), P(), P())
    out_specs = (P("shot", "rcv", None), P("shot", "rcv", None))
    return jax.shard_map(body, mesh=mesh, in_specs=in_specs, out_specs=out_specs, check_vma=False)
```

```python
import math

import jax
import jax.numpy as jnp
import numpy as np
from jax import lax
from jax.experimental import pallas as pl
from jax.experimental.pallas import tpu as pltpu
from jax.sharding import PartitionSpec as P

ITERATIONS = 2
PARTNERS = 4
SHOTS = 48
SAMPLES = 2048
FREQS = 1024
ROWS = 16
GROUPS = 8
PITCH = 40
BASE = 16
TRACES = 2 * SHOTS

MESH = pl.DeviceIdType.MESH
BF16 = jnp.bfloat16
F32 = jnp.float32


def group_frequencies():
    j = np.arange(64)
    rows = [np.concatenate([16 * j, 8 + 16 * j])]
    for g in range(1, GROUPS):
        rows.append(np.concatenate([g + 16 * j, 16 - g + 16 * j]))
    return np.stack(rows)


def split_np(table):
    table = table.astype(np.float32)
    high = table.astype(jnp.bfloat16)
    low = (table - high.astype(np.float32)).astype(jnp.bfloat16)
    return high, low


def time_tables():
    kept = group_frequencies()
    n2 = np.arange(128)
    out = np.zeros((GROUPS, 256, 256))
    for g in range(GROUPS):
        phase = (n2[:, None] * kept[g][None, :]) % SAMPLES
        cos = np.cos(2 * np.pi * phase / SAMPLES)
        sin = np.sin(2 * np.pi * phase / SAMPLES)
        first = np.arange(128) < 64
        if g == 0:
            out[g, :128, :128] = np.where(first, cos, 0)
            out[g, :128, 128:] = np.where(first, -sin, 0)
            out[g, 128:, :128] = np.where(first, 0, cos)
            out[g, 128:, 128:] = np.where(first, 0, -sin)
        else:
            out[g, :128, :128] = cos
            out[g, :128, 128:] = -sin
            out[g, 128:, :128] = np.where(first, sin, -sin)
            out[g, 128:, 128:] = np.where(first, cos, -cos)
    return split_np(out)


def shot_tables():
    index = np.arange(SHOTS)
    phase = 2 * np.pi * ((index[:, None] * index[None, :]) % SHOTS) / SHOTS
    cos, sin = np.cos(phase), np.sin(phase)
    forward = np.block([[cos, sin], [-sin, cos]])
    inverse = np.block([[cos, -sin], [sin, cos]]) / (SHOTS * FREQS)
    return np.stack([forward, inverse])


def shot_operands():
    high, low = split_np(shot_tables())
    return np.concatenate([high, high], axis=2), low


def mask_order():
    order = group_frequencies().reshape(-1)
    out = np.zeros((FREQS, FREQS), np.float32)
    out[order, np.arange(FREQS)] = 1
    return out.astype(jnp.bfloat16)


C1, C2, C3 = (math.cos(math.pi * i / 8) for i in (1, 2, 3))


def radix16(x):
    a = [x[n] + x[n + 8] for n in range(8)]
    b = [x[n] - x[n + 8] for n in range(8)]
    e = [a[n] + a[n + 4] for n in range(4)]
    f = [a[n] - a[n + 4] for n in range(4)]
    p02, p13 = e[0] + e[2], e[1] + e[3]
    y0, y8 = p02 + p13, p02 - p13
    re4, im4 = e[0] - e[2], e[3] - e[1]
    m, q = C2 * (f[1] - f[3]), C2 * (f[1] + f[3])
    re2, re6 = f[0] + m, f[0] - m
    im2, im6 = -f[2] - q, f[2] - q
    c = [None] + [b[n] - b[8 - n] for n in (1, 2, 3)]
    d = [None] + [b[n] + b[8 - n] for n in (1, 2, 3)]
    up, down = b[0] + C2 * c[2], b[0] - C2 * c[2]
    v, w = C1 * c[1] + C3 * c[3], C3 * c[1] - C1 * c[3]
    re1, re7, re3, re5 = up + v, up - v, down + w, down - w
    p, t = C3 * d[1] + C1 * d[3], C2 * d[2] + b[4]
    q, u = C1 * d[1] - C3 * d[3], C2 * d[2] - b[4]
    im1, im7, im3, im5 = -p - t, t - p, -q - u, u - q
    return [(y0, y8), (re1, im1), (re2, im2), (re3, im3), (re4, im4), (re5, im5), (re6, im6), (re7, im7)]


def radix16_back(z):
    (w0, w8), (re1, im1), (re2, im2), (re3, im3), (re4, im4), (re5, im5), (re6, im6), (re7, im7) = z
    plus, minus = w0 + w8, w0 - w8
    ee = [plus + re4, minus - im4, plus - re4, minus + im4]
    m, q = C2 * (re2 - re6), C2 * (im2 + im6)
    eo = [re2 + re6, m - q, im6 - im2, -m - q]
    even = [ee[n] + eo[n] for n in range(4)] + [ee[n] - eo[n] for n in range(4)]
    s17, d17, s35, d35 = re1 + re7, re1 - re7, re3 + re5, re3 - re5
    t17, g17, t35, g35 = im1 + im7, im1 - im7, im3 + im5, im3 - im5
    pc = [None, C1 * d17 + C3 * d35, C2 * (s17 - s35), C3 * d17 - C1 * d35]
    ps = [None, C3 * t17 + C1 * t35, C2 * (g17 + g35), C1 * t17 - C3 * t35]
    odd = [None] * 8
    odd[0] = s17 + s35
    odd[4] = g35 - g17
    for n in (1, 2, 3):
        odd[n] = pc[n] - ps[n]
        odd[8 - n] = -pc[n] - ps[n]
    return [even[n] + odd[n] for n in range(8)] + [even[n] - odd[n] for n in range(8)]


def split(x):
    high = x.astype(BF16)
    return high, (x - high.astype(F32)).astype(BF16)


def dot(a, b):
    return lax.dot_general(a, b, (((1,), (0,)), ((), ())), preferred_element_type=F32)


HALO = 3
SENT = 9
NEAR = 12


def ring(offset, size):
    return min(offset, size - offset)


def forward(source, u, table_hi, table_lo, mix_hi, mix_lo, y, v):
    def forward_rows(block, _):
        parts = []
        for half in range(2):
            x = [source[pl.ds(block * 256 + half * 128 + n1, 8, stride=ROWS), :] for n1 in range(ROWS)]
            parts.append(radix16(x))
        row = pl.multiple_of(block * 16, 16)
        for g in range(GROUPS):
            for part in range(2):
                high, low = split(jnp.concatenate([parts[0][g][part], parts[1][g][part]], axis=0))
                y[g, pl.ds(row, 16), part * 128:(part + 1) * 128] = high
                y[g, pl.ds(row + SHOTS, 16), part * 128:(part + 1) * 128] = low
        return 0

    lax.fori_loop(0, SHOTS // 16, forward_rows, 0)

    for g in range(GROUPS):
        both = dot(y[g], table_hi[g])
        high, low = split(both[:SHOTS] + both[SHOTS:] + dot(y[g, :SHOTS], table_lo[g]))
        c = slice(g * 128, (g + 1) * 128)
        v[0:48, c] = high[:, :128]
        v[48:96, c] = high[:, 128:]
        v[96:144, c] = low[:, :128]
        v[144:192, c] = low[:, 128:]

    for b in range(FREQS // 256):
        c = slice(b * 256, (b + 1) * 256)
        u[:, c] = dot(mix_hi[0], v[:, c]) + dot(mix_lo[0], v[:96, c])


def inverse(u, sweep, q, kept, back_hi, back_lo, mix_hi, mix_lo, y, w, back):
    for b in range(FREQS // 256):
        c = slice(b * 256, (b + 1) * 256)
        keep = kept[sweep * SHOTS:(sweep + 1) * SHOTS, c]
        high, low = split(u[:, c] * jnp.concatenate([keep, keep], axis=0))
        w[:96, c] = high
        w[96:, c] = low

    for b in range(FREQS // 256):
        c = slice(b * 256, (b + 1) * 256)
        high, low = split(dot(mix_hi[1], w[:, c]) + dot(mix_lo[1], w[:96, c]))
        for i in range(2):
            d = slice(i * 128, (i + 1) * 128)
            for part, at in ((high, 0), (low, SHOTS)):
                y[b * 2 + i, at:at + SHOTS, :128] = part[:48, d]
                y[b * 2 + i, at:at + SHOTS, 128:] = part[48:, d]

    for g in range(GROUPS):
        both = dot(y[g], back_hi[g])
        back[g] = both[:SHOTS] + both[SHOTS:] + dot(y[g, :SHOTS], back_lo[g])

    def inverse_rows(block, _):
        row = pl.multiple_of(block * 8, 8)
        z = [
            (back[g, pl.ds(row, 8), 0:128], back[g, pl.ds(row, 8), 128:256])
            for g in range(GROUPS)
        ]
        x = radix16_back(z)
        for n1 in range(ROWS):
            q[pl.ds(row * PITCH + BASE + n1, 8, stride=PITCH), :] = x[n1]
        return 0

    lax.fori_loop(0, SHOTS // 8, inverse_rows, 0)


def fill(sent, record):
    def shots(block, _):
        for i in range(8):
            shot = block * 8 + i
            sent[HALO + shot] = record(pl.ds(pl.multiple_of(shot * PITCH + BASE, 8), ROWS))
        return 0

    lax.fori_loop(0, SHOTS // 8, shots, 0)


def shift_terms(lane, partners, offsets, shot, first, blank):
    terms = []
    for j in range(PARTNERS):
        partner, delay = partners[j, shot], offsets[j, shot]
        trace = jnp.where(partner >= 0, jnp.clip(partner - first, 0, blank - 1), blank)
        rest = delay & 127
        terms.append((trace, BASE - (delay >> 7), rest, lane < 128 - rest))
    return terms


def shifted(load, term):
    trace, start, rest, near = term
    return pltpu.roll(jnp.where(near, load(trace, start), load(trace, start - 1)), rest, 1)


def blend(partners, offsets, q, image, residual=None, sums=0):
    lane = lax.broadcasted_iota(jnp.int32, (ROWS, 128), 1)
    chunk = 8

    def load(trace, start):
        return q[pl.ds(trace * PITCH + start, ROWS), :]

    def shots(block, sums):
        terms = [
            shift_terms(lane, partners, offsets, block * chunk + i, 0, SHOTS) for i in range(chunk)
        ]
        for i in range(chunk):
            shot = block * chunk + i
            g = q[pl.ds(pl.multiple_of(shot * PITCH + BASE, 8), ROWS), :]
            for term in terms[i]:
                g = g + shifted(load, term)
            at = pl.ds(pl.multiple_of(shot * ROWS, ROWS), ROWS)
            image[at, :] = g
            if residual is not None:
                sums = (sums[0] + residual[at, :] * g, sums[1] + g * g)
        return sums

    return lax.fori_loop(0, SHOTS // chunk, shots, sums)


def fold(sums):
    return jnp.concatenate([x[:4] + x[4:8] + x[8:12] + x[12:] for x in sums], axis=0)


def kernel(
    groups,
    partners_h, offsets_h, blended_h, fk_mask_h, order_h, tables_h, mix_hi_h, mix_lo_h,
    out_d, out_r,
    partners, offsets, mix_hi, mix_lo,
    blended, fk_mask, staged, res, q, other, image, image_a, image_b, sent1, sent2, got10, got11, got20, got21,
    left, late, rows_d, rows_r, done_d, done_r,
    y, v, w, back, u0, u1, tables, order, kept, sums_mine, sums_got,
    load_sem, in_send, in_recv, bulk_send, bulk_recv, more_send, more_recv, own_sem, out_sem,
    sum_send, sum_recv,
):
    got1, got2 = (got10, got11), (got20, got21)
    me = lax.axis_index("shot")
    place = lax.axis_index("rcv")
    places = lax.axis_size("rcv")
    core = lax.rem(me, 2)
    mate = (me + 1 - 2 * core, place)
    shot_peers = [(lax.rem(me + k, groups), place) for k in range(1, groups)]
    columns = 8 if places % 8 == 0 else places
    planes = places // columns
    steps = [(i, j) for i in range(planes) for j in range(columns)][1:]
    steps.sort(key=lambda s: -(ring(s[0], planes) + ring(s[1], columns)))
    plane, column = place // columns, lax.rem(place, columns)
    place_peers = [
        (me, lax.rem(plane + i, planes) * columns + lax.rem(column + j, columns)) for i, j in steps
    ]
    peers = shot_peers + place_peers

    barrier = pltpu.get_barrier_semaphore()
    for peer in shot_peers:
        pl.semaphore_signal(barrier, inc=1, device_id=peer, device_id_type=MESH)
    loads = [
        pltpu.make_async_copy(source, target, load_sem.at[i])
        for i, (source, target) in enumerate((
            (blended_h, blended), (mix_hi_h, mix_hi), (mix_lo_h, mix_lo), (fk_mask_h, fk_mask),
            (partners_h, partners), (offsets_h, offsets), (order_h, order), (tables_h, tables),
        ))
    ]
    first_load = loads.pop(0)
    first_load.start()
    for peer in place_peers:
        pl.semaphore_signal(barrier, inc=1, device_id=peer, device_id_type=MESH)

    first_load.wait()
    for load in loads:
        load.start()
    for shot in range(6):
        for half in range(2):
            for n1 in range(ROWS):
                at = half * 8 * 96 + shot * ROWS + n1
                staged[pl.ds(at, 8, stride=96), :] = blended[
                    shot, half * 8:(half + 1) * 8, n1 * 128:(n1 + 1) * 128
                ]

    pl.semaphore_wait(barrier, len(peers))

    mine = pl.ds(pl.multiple_of(me * 96, 8), 96)
    copies = [[], []]
    own = []
    for recv in range(2):
        for k in range(1, groups):
            peer = shot_peers[k - 1]
            copies[recv].append(pltpu.make_async_remote_copy(
                src_ref=staged.at[pl.ds(pl.multiple_of(peer[0] * 192 + recv * 96, 8), 96)],
                dst_ref=res.at[recv, mine],
                send_sem=in_send.at[k - 1, recv],
                recv_sem=in_recv.at[k - 1, recv],
                device_id=peer, device_id_type=MESH,
            ))
            copies[recv][-1].start()
        own.append(pltpu.make_async_copy(
            staged.at[pl.ds(pl.multiple_of(me * 192 + recv * 96, 8), 96)],
            res.at[recv, mine], own_sem.at[recv],
        ))
        own[-1].start()

    q[...] = jnp.zeros_like(q)
    other[...] = jnp.zeros_like(other)
    for sent in (sent1, sent2):
        for recv in range(2):
            blank = jnp.zeros((HALO, ROWS, 128), F32)
            sent[recv, :HALO] = blank
            sent[recv, HALO + SHOTS:] = blank

    def clear(source, _):
        for got in (got1, got2):
            for recv in range(2):
                for trace in range(NEAR):
                    got[recv][source, trace, :BASE, :] = jnp.zeros((BASE, 128), F32)
                    got[recv][source, trace, BASE + ROWS:, :] = jnp.zeros((PITCH - BASE - ROWS, 128), F32)
                got[recv][source, NEAR] = jnp.zeros((PITCH, 128), F32)
        return 0

    lax.fori_loop(0, groups, clear, 0)
    for load in loads:
        load.wait()
    kept[...] = dot(fk_mask[...].astype(F32).astype(BF16), order[...])

    def bulk_start(field, recv, sent, got):
        moves = []
        for k in range(1, groups):
            peer = shot_peers[k - 1]
            there = lax.rem(peer[0], 2)
            moves.append(pltpu.make_async_remote_copy(
                src_ref=sent.at[recv, pl.ds(12 * (peer[0] // 2) + 9 * there, SENT)],
                dst_ref=got[recv].at[me, pl.ds(HALO * there, SENT), pl.ds(BASE, ROWS)],
                send_sem=bulk_send.at[field, k - 1, recv],
                recv_sem=bulk_recv.at[field, k - 1, recv],
                device_id=peer, device_id_type=MESH,
            ))
            moves[-1].start()
        moves.append(pltpu.make_async_copy(
            sent.at[recv, pl.ds(12 * (me // 2) + 9 * core, SENT)],
            got[recv].at[me, pl.ds(HALO * core, SENT), pl.ds(BASE, ROWS)],
            own_sem.at[2 + field * 2 + recv],
        ))
        moves[-1].start()
        return moves

    def more_start(field, recv, got):
        move = pltpu.make_async_remote_copy(
            src_ref=got[recv].at[:, pl.ds(6 - 3 * core, HALO), pl.ds(BASE, ROWS)],
            dst_ref=got[recv].at[:, pl.ds(9 * core, HALO), pl.ds(BASE, ROWS)],
            send_sem=more_send.at[field, recv], recv_sem=more_recv.at[field, recv],
            device_id=mate, device_id_type=MESH,
        )
        move.start()
        return move

    def sum_start(sweep, stage, value):
        sums_mine[sweep, stage] = value
        first = 0 if stage == 0 else len(place_peers)
        moves = []
        for i, peer in enumerate((place_peers, shot_peers)[stage]):
            moves.append(pltpu.make_async_remote_copy(
                src_ref=sums_mine.at[sweep, stage], dst_ref=sums_got.at[sweep, first + i],
                send_sem=sum_send.at[sweep, first + i], recv_sem=sum_recv.at[sweep, first + i],
                device_id=peer, device_id_type=MESH,
            ))
            moves[-1].start()
        return moves

    def sum_end(sweep, stage, value, moves):
        first = 0 if stage == 0 else len(place_peers)
        for i, move in enumerate(moves):
            move.wait_recv()
            value = value + sums_got[sweep, first + i]
        return value

    def ratio(value):
        return jnp.sum(value[:4], keepdims=True) / jnp.sum(value[4:], keepdims=True)

    lane = lax.broadcasted_iota(jnp.int32, (ROWS, 128), 1)
    first_shot = me * 6

    def blend_near(recv, got, put):
        def one_shot(i, _):
            terms = shift_terms(lane, partners, offsets, first_shot + i, first_shot - HALO, NEAR)
            for source in range(groups):
                g = got[recv][source, HALO + i, pl.ds(BASE, ROWS), :]
                for term in terms:
                    g = g + shifted(
                        lambda trace, start: got[recv][source, trace, pl.ds(start, ROWS), :], term
                    )
                put(i, source, g)
            return 0

        lax.fori_loop(0, 6, one_shot, 0)

    ahead = (tables.at[0], tables.at[1], mix_hi, mix_lo, y, v)
    behind = (kept, tables.at[2], tables.at[3], mix_hi, mix_lo, y, w, back)

    zero = jnp.zeros((ROWS, 128), F32)
    sums = (zero, zero)
    bulk1 = []
    for recv in range(2):
        own[recv].wait()
        for copy in copies[recv]:
            copy.wait()
        forward(res.at[recv], u0.at[recv], *ahead)
        inverse(u0.at[recv], 0, q.at[recv], *behind)
        fill(sent1.at[recv], lambda at: q[recv, at, :])
        bulk1.append(bulk_start(0, recv, sent1, got1))
        sums = blend(partners, offsets, q.at[recv], image.at[recv], res.at[recv], sums)
    value = fold(sums)
    stage0 = sum_start(0, 0, value)

    for recv in range(2):
        inverse(u0.at[recv], 1, q.at[recv], *behind)
        blend(partners, offsets, q.at[recv], image_a.at[recv])
    for recv in range(2):
        forward(image.at[recv], u1.at[recv], *ahead)
        inverse(u1.at[recv], 1, other.at[recv], *behind)
    value = sum_end(0, 0, value, stage0)
    stage1 = sum_start(0, 1, value)
    for recv in range(2):
        blend(partners, offsets, other.at[recv], image_b.at[recv])
    value = sum_end(0, 1, value, stage1)
    step1 = ratio(value)

    bulk2 = []
    for recv in range(2):
        fill(sent2.at[recv], lambda at: q[recv, at, :] - step1 * other[recv, at, :])
        bulk2.append(bulk_start(1, recv, sent2, got2))
        if recv == 0:

            def second(block, sums):
                num, den = sums
                for i in range(8):
                    at = pl.ds(pl.multiple_of((block * 8 + i) * ROWS, ROWS), ROWS)
                    for r in range(2):
                        g = image_a[r, at, :] - step1 * image_b[r, at, :]
                        num = num + (res[r, at, :] - step1 * image[r, at, :]) * g
                        den = den + g * g
                return num, den

            value = fold(lax.fori_loop(0, SHOTS // 8, second, (zero, zero)))
            stage2 = sum_start(1, 0, value)

    more1 = []
    for recv in range(2):
        for move in bulk1[recv]:
            move.wait()
        more1.append(more_start(0, recv, got1))
    for recv in range(2):
        more1[recv].wait()

        def put_left(i, source, g):
            old = staged[pl.ds(pl.multiple_of((source * 2 + recv) * 96 + i * ROWS, 8), ROWS), :]
            left[recv, i, source] = old - step1 * g

        blend_near(recv, got1, put_left)

    value = sum_end(1, 0, value, stage2)
    stage3 = sum_start(1, 1, value)

    for move in bulk2[0]:
        move.wait()
    more = more_start(1, 0, got2)
    more.wait()

    def put_late(i, source, g):
        late[i, source] = g

    blend_near(0, got2, put_late)
    for move in bulk2[1]:
        move.wait()
    more = more_start(1, 1, got2)
    value = sum_end(1, 1, value, stage3)
    step2 = ratio(value)

    def rows_of(recv, source):
        return slice((source * 2 + recv) * ROWS, (source * 2 + recv + 1) * ROWS)

    def combine(i, _):
        data = pl.ds(BASE, ROWS)
        for source in range(groups):
            for recv in range(2):
                rows_d[i, rows_of(recv, source), :] = (
                    step1 * got1[recv][source, HALO + i, data, :]
                    + step2 * got2[recv][source, HALO + i, data, :]
                )
            rows_r[i, rows_of(0, source), :] = left[0, i, source] - step2 * late[i, source]
        return 0

    def natural(source, target):
        def one_shot(i, _):
            for half in range(2):
                for n1 in range(ROWS):
                    target[i, half * 8:(half + 1) * 8, n1 * 128:(n1 + 1) * 128] = source[
                        i, pl.ds(half * 128 + n1, 8, stride=ROWS), :
                    ]
            return 0

        lax.fori_loop(0, 6, one_shot, 0)

    lax.fori_loop(0, 6, combine, 0)
    natural(rows_d, done_d)
    write_d = pltpu.make_async_copy(done_d, out_d, out_sem.at[0])
    write_d.start()
    more.wait()

    def put_rest(i, source, g):
        rows_r[i, rows_of(1, source), :] = left[1, i, source] - step2 * g

    blend_near(1, got2, put_rest)
    natural(rows_r, done_r)
    write_r = pltpu.make_async_copy(done_r, out_r, out_sem.at[1])
    write_r.start()
    write_d.wait()
    write_r.wait()

    for move in stage0 + stage1 + stage2 + stage3:
        move.wait_send()


def write_out(d, r, out_d, out_r, held_d, held_r, sem):
    parts = [
        (source.at[i], held.at[i], target.at[i])
        for source, held, target in ((d, held_d, out_d), (r, held_r, out_r))
        for i in range(6)
    ]
    loads = [pltpu.make_async_copy(p[0], p[1], sem.at[0, i]) for i, p in enumerate(parts)]
    stores = [pltpu.make_async_copy(p[1], p[2], sem.at[1, i]) for i, p in enumerate(parts)]
    for load in loads:
        load.start()
    for load, store in zip(loads, stores):
        load.wait()
        store.start()
    for store in stores:
        store.wait()


def solution(mesh):
    groups = mesh.shape["shot"]
    peers = groups - 1 + mesh.shape["rcv"] - 1
    table_hi, table_lo = time_tables()
    tables = np.stack([table_hi, table_lo, table_hi.swapaxes(1, 2), table_lo.swapaxes(1, 2)])
    mix_hi, mix_lo = shot_operands()
    order = mask_order()

    def body(blended, partners, offsets, fk_mask):
        hbm = pl.BlockSpec(memory_space=pltpu.HBM)
        out = jax.ShapeDtypeStruct(blended.shape, F32)
        dma = pltpu.SemaphoreType.DMA
        d, r = pl.pallas_call(
            lambda *refs: kernel(groups, *refs),
            out_shape=(out, out),
            in_specs=[hbm] * 8,
            out_specs=(hbm, hbm),
            scratch_shapes=[
                pltpu.SMEM((PARTNERS, SHOTS), jnp.int32),
                pltpu.SMEM((PARTNERS, SHOTS), jnp.int32),
                pltpu.VMEM(mix_hi.shape, BF16),
                pltpu.VMEM(mix_lo.shape, BF16),
                pltpu.VMEM(blended.shape, F32),
                pltpu.VMEM((ITERATIONS * SHOTS, FREQS), jnp.int32),
                pltpu.VMEM((16 * 96, 128), F32),
                pltpu.VMEM((2, SHOTS * ROWS, 128), F32),
                pltpu.VMEM((2, (SHOTS + 1) * PITCH, 128), F32),
                pltpu.VMEM((2, (SHOTS + 1) * PITCH, 128), F32),
                pltpu.VMEM((2, SHOTS * ROWS, 128), F32),
                pltpu.VMEM((2, SHOTS * ROWS, 128), F32),
                pltpu.VMEM((2, SHOTS * ROWS, 128), F32),
                pltpu.VMEM((2, SHOTS + 2 * HALO, ROWS, 128), F32),
                pltpu.VMEM((2, SHOTS + 2 * HALO, ROWS, 128), F32),
                *[pltpu.VMEM((groups, NEAR + 1, PITCH, 128), F32)] * 4,
                pltpu.VMEM((2, 6, groups, ROWS, 128), F32),
                pltpu.VMEM((6, groups, ROWS, 128), F32),
                pltpu.VMEM((6, 16 * ROWS, 128), F32),
                pltpu.VMEM((6, 16 * ROWS, 128), F32),
                pltpu.VMEM(blended.shape, F32),
                pltpu.VMEM(blended.shape, F32),
                pltpu.VMEM((GROUPS, TRACES, 256), BF16),
                pltpu.VMEM((192, FREQS), BF16),
                pltpu.VMEM((192, FREQS), BF16),
                pltpu.VMEM((GROUPS, SHOTS, 256), F32),
                pltpu.VMEM((2, 96, FREQS), F32),
                pltpu.VMEM((2, 96, FREQS), F32),
                pltpu.VMEM((4, GROUPS, 256, 256), BF16),
                pltpu.VMEM((FREQS, FREQS), BF16),
                pltpu.VMEM((ITERATIONS * SHOTS, FREQS), F32),
                pltpu.VMEM((ITERATIONS, 2, 8, 128), F32),
                pltpu.VMEM((ITERATIONS, peers, 8, 128), F32),
                dma((8,)),
                dma((groups - 1, 2)),
                dma((groups - 1, 2)),
                dma((ITERATIONS, groups - 1, 2)),
                dma((ITERATIONS, groups - 1, 2)),
                dma((ITERATIONS, 2)),
                dma((ITERATIONS, 2)),
                dma((6,)),
                dma((2,)),
                dma((ITERATIONS, peers)),
                dma((ITERATIONS, peers)),
            ],
            compiler_params=pltpu.CompilerParams(
                collective_id=0, has_side_effects=True, vmem_limit_bytes=56 * 2**20
            ),
            name="deblend",
        )(
            partners.T, offsets.T, blended, fk_mask.reshape(ITERATIONS * SHOTS, FREQS),
            jnp.asarray(order), jnp.asarray(tables), jnp.asarray(mix_hi), jnp.asarray(mix_lo),
        )
        return pl.pallas_call(
            write_out,
            out_shape=(out, out),
            in_specs=[hbm, hbm],
            out_specs=(hbm, hbm),
            scratch_shapes=[pltpu.VMEM(blended.shape, F32), pltpu.VMEM(blended.shape, F32), dma((2, 12))],
            compiler_params=pltpu.CompilerParams(vmem_limit_bytes=56 * 2**20),
            name="write_out",
        )(d, r)

    in_specs = (P("shot", "rcv", None), P(), P(), P())
    out_specs = (P("shot", "rcv", None), P("shot", "rcv", None))
    return jax.shard_map(body, mesh=mesh, in_specs=in_specs, out_specs=out_specs, check_vma=False)
```

```python
import math

import jax
import jax.numpy as jnp
import numpy as np
from jax import lax
from jax.experimental import pallas as pl
from jax.experimental.pallas import tpu as pltpu
from jax.sharding import PartitionSpec as P

ITERATIONS = 2
PARTNERS = 4
SHOTS = 48
SAMPLES = 2048
FREQS = 1024
ROWS = 16
GROUPS = 8
PITCH = 40
BASE = 16
TRACES = 2 * SHOTS

MESH = pl.DeviceIdType.MESH
BF16 = jnp.bfloat16
F32 = jnp.float32


def group_frequencies():
    j = np.arange(64)
    rows = [np.concatenate([16 * j, 8 + 16 * j])]
    for g in range(1, GROUPS):
        rows.append(np.concatenate([g + 16 * j, 16 - g + 16 * j]))
    return np.stack(rows)


def split_np(table):
    table = table.astype(np.float32)
    high = table.astype(jnp.bfloat16)
    low = (table - high.astype(np.float32)).astype(jnp.bfloat16)
    return high, low


def time_tables():
    kept = group_frequencies()
    n2 = np.arange(128)
    out = np.zeros((GROUPS, 256, 256))
    for g in range(GROUPS):
        phase = (n2[:, None] * kept[g][None, :]) % SAMPLES
        cos = np.cos(2 * np.pi * phase / SAMPLES)
        sin = np.sin(2 * np.pi * phase / SAMPLES)
        first = np.arange(128) < 64
        if g == 0:
            out[g, :128, :128] = np.where(first, cos, 0)
            out[g, :128, 128:] = np.where(first, -sin, 0)
            out[g, 128:, :128] = np.where(first, 0, cos)
            out[g, 128:, 128:] = np.where(first, 0, -sin)
        else:
            out[g, :128, :128] = cos
            out[g, :128, 128:] = -sin
            out[g, 128:, :128] = np.where(first, sin, -sin)
            out[g, 128:, 128:] = np.where(first, cos, -cos)
    return split_np(out)


def shot_tables():
    index = np.arange(SHOTS)
    phase = 2 * np.pi * ((index[:, None] * index[None, :]) % SHOTS) / SHOTS
    cos, sin = np.cos(phase), np.sin(phase)
    forward = np.block([[cos, sin], [-sin, cos]])
    inverse = np.block([[cos, -sin], [sin, cos]]) / (SHOTS * FREQS)
    return np.stack([forward, inverse])


def shot_operands():
    high, low = split_np(shot_tables())
    return np.concatenate([high, high], axis=2), low


def mask_order():
    order = group_frequencies().reshape(-1)
    out = np.zeros((FREQS, FREQS), np.float32)
    out[order, np.arange(FREQS)] = 1
    return out.astype(jnp.bfloat16)


C1, C2, C3 = (math.cos(math.pi * i / 8) for i in (1, 2, 3))


def radix16(x):
    a = [x[n] + x[n + 8] for n in range(8)]
    b = [x[n] - x[n + 8] for n in range(8)]
    e = [a[n] + a[n + 4] for n in range(4)]
    f = [a[n] - a[n + 4] for n in range(4)]
    p02, p13 = e[0] + e[2], e[1] + e[3]
    y0, y8 = p02 + p13, p02 - p13
    re4, im4 = e[0] - e[2], e[3] - e[1]
    m, q = C2 * (f[1] - f[3]), C2 * (f[1] + f[3])
    re2, re6 = f[0] + m, f[0] - m
    im2, im6 = -f[2] - q, f[2] - q
    c = [None] + [b[n] - b[8 - n] for n in (1, 2, 3)]
    d = [None] + [b[n] + b[8 - n] for n in (1, 2, 3)]
    up, down = b[0] + C2 * c[2], b[0] - C2 * c[2]
    v, w = C1 * c[1] + C3 * c[3], C3 * c[1] - C1 * c[3]
    re1, re7, re3, re5 = up + v, up - v, down + w, down - w
    p, t = C3 * d[1] + C1 * d[3], C2 * d[2] + b[4]
    q, u = C1 * d[1] - C3 * d[3], C2 * d[2] - b[4]
    im1, im7, im3, im5 = -p - t, t - p, -q - u, u - q
    return [(y0, y8), (re1, im1), (re2, im2), (re3, im3), (re4, im4), (re5, im5), (re6, im6), (re7, im7)]


def radix16_back(z):
    (w0, w8), (re1, im1), (re2, im2), (re3, im3), (re4, im4), (re5, im5), (re6, im6), (re7, im7) = z
    plus, minus = w0 + w8, w0 - w8
    ee = [plus + re4, minus - im4, plus - re4, minus + im4]
    m, q = C2 * (re2 - re6), C2 * (im2 + im6)
    eo = [re2 + re6, m - q, im6 - im2, -m - q]
    even = [ee[n] + eo[n] for n in range(4)] + [ee[n] - eo[n] for n in range(4)]
    s17, d17, s35, d35 = re1 + re7, re1 - re7, re3 + re5, re3 - re5
    t17, g17, t35, g35 = im1 + im7, im1 - im7, im3 + im5, im3 - im5
    pc = [None, C1 * d17 + C3 * d35, C2 * (s17 - s35), C3 * d17 - C1 * d35]
    ps = [None, C3 * t17 + C1 * t35, C2 * (g17 + g35), C1 * t17 - C3 * t35]
    odd = [None] * 8
    odd[0] = s17 + s35
    odd[4] = g35 - g17
    for n in (1, 2, 3):
        odd[n] = pc[n] - ps[n]
        odd[8 - n] = -pc[n] - ps[n]
    return [even[n] + odd[n] for n in range(8)] + [even[n] - odd[n] for n in range(8)]


def split(x):
    high = x.astype(BF16)
    return high, (x - high.astype(F32)).astype(BF16)


def dot(a, b):
    return lax.dot_general(a, b, (((1,), (0,)), ((), ())), preferred_element_type=F32)


HALO = 3
SUM_ORDER = ((0, 1), (1, 0))
SENT = 9
NEAR = 12


def ring(offset, size):
    return min(offset, size - offset)


def forward(source, u, table_hi, table_lo, mix_hi, mix_lo, y, v):
    def forward_rows(block, _):
        parts = []
        for half in range(2):
            x = [source[pl.ds(block * 256 + half * 128 + n1, 8, stride=ROWS), :] for n1 in range(ROWS)]
            parts.append(radix16(x))
        row = pl.multiple_of(block * 16, 16)
        for g in range(GROUPS):
            for part in range(2):
                high, low = split(jnp.concatenate([parts[0][g][part], parts[1][g][part]], axis=0))
                y[g, pl.ds(row, 16), part * 128:(part + 1) * 128] = high
                y[g, pl.ds(row + SHOTS, 16), part * 128:(part + 1) * 128] = low
        return 0

    lax.fori_loop(0, SHOTS // 16, forward_rows, 0)

    for g in range(GROUPS):
        both = dot(y[g], table_hi[g])
        high, low = split(both[:SHOTS] + both[SHOTS:] + dot(y[g, :SHOTS], table_lo[g]))
        c = slice(g * 128, (g + 1) * 128)
        v[0:48, c] = high[:, :128]
        v[48:96, c] = high[:, 128:]
        v[96:144, c] = low[:, :128]
        v[144:192, c] = low[:, 128:]

    for b in range(FREQS // 256):
        c = slice(b * 256, (b + 1) * 256)
        u[:, c] = dot(mix_hi[0], v[:, c]) + dot(mix_lo[0], v[:96, c])


def inverse(u, sweep, q, kept, back_hi, back_lo, mix_hi, mix_lo, y, w, back):
    for b in range(FREQS // 256):
        c = slice(b * 256, (b + 1) * 256)
        keep = kept[sweep * SHOTS:(sweep + 1) * SHOTS, c]
        high, low = split(u[:, c] * jnp.concatenate([keep, keep], axis=0))
        w[:96, c] = high
        w[96:, c] = low

    for b in range(FREQS // 256):
        c = slice(b * 256, (b + 1) * 256)
        high, low = split(dot(mix_hi[1], w[:, c]) + dot(mix_lo[1], w[:96, c]))
        for i in range(2):
            d = slice(i * 128, (i + 1) * 128)
            for part, at in ((high, 0), (low, SHOTS)):
                y[b * 2 + i, at:at + SHOTS, :128] = part[:48, d]
                y[b * 2 + i, at:at + SHOTS, 128:] = part[48:, d]

    for g in range(GROUPS):
        both = dot(y[g], back_hi[g])
        back[g] = both[:SHOTS] + both[SHOTS:] + dot(y[g, :SHOTS], back_lo[g])

    def inverse_rows(block, _):
        row = pl.multiple_of(block * 8, 8)
        z = [
            (back[g, pl.ds(row, 8), 0:128], back[g, pl.ds(row, 8), 128:256])
            for g in range(GROUPS)
        ]
        x = radix16_back(z)
        for n1 in range(ROWS):
            q[pl.ds(row * PITCH + BASE + n1, 8, stride=PITCH), :] = x[n1]
        return 0

    lax.fori_loop(0, SHOTS // 8, inverse_rows, 0)


def fill(sent, record):
    def shots(block, _):
        for i in range(8):
            shot = block * 8 + i
            sent[HALO + shot] = record(pl.ds(pl.multiple_of(shot * PITCH + BASE, 8), ROWS))
        return 0

    lax.fori_loop(0, SHOTS // 8, shots, 0)


def shift_tables(partners, offsets, traces, rows, rests, count, first_shot, first, blank):
    def one_shot(i, _):
        for j in range(PARTNERS):
            partner, delay = partners[j, first_shot + i], offsets[j, first_shot + i]
            trace = jnp.where(partner >= 0, jnp.clip(partner - first, 0, blank - 1), blank)
            if traces is None:
                rows[j, i] = trace * PITCH + BASE - (delay >> 7)
            else:
                traces[j, i] = trace
                rows[j, i] = BASE - (delay >> 7)
            rests[j, i] = delay & 127
        return 0

    lax.fori_loop(0, count, one_shot, 0)


def shift_terms(lane, rows, rests, i):
    return [(rows[j, i], rests[j, i], lane < 128 - rests[j, i]) for j in range(PARTNERS)]


def blended_record(own, load, terms):
    g = own
    for j, (row, rest, near) in enumerate(terms):
        g = g + pltpu.roll(jnp.where(near, load(j, row), load(j, row - 1)), rest, 1)
    return g


def blend(tables, fields, residual=None, sums=0, chunk=16):
    lane = lax.broadcasted_iota(jnp.int32, (ROWS, 128), 1)

    def shots(block, sums):
        terms = [shift_terms(lane, *tables, block * chunk + i) for i in range(chunk)]
        for i in range(chunk):
            shot = block * chunk + i
            at = pl.ds(pl.multiple_of(shot * ROWS, ROWS), ROWS)
            for q, image in fields:
                own = q[pl.ds(pl.multiple_of(shot * PITCH + BASE, 8), ROWS), :]
                g = blended_record(own, lambda j, row: q[pl.ds(row, ROWS), :], terms[i])
                image[at, :] = g
                if residual is not None:
                    sums = (sums[0] + residual[at, :] * g, sums[1] + g * g)
        return sums

    return lax.fori_loop(0, SHOTS // chunk, shots, sums)


def fold(sums):
    return jnp.concatenate([x[:4] + x[4:8] + x[8:12] + x[12:] for x in sums], axis=0)


def kernel(
    groups,
    partners_h, offsets_h, blended_h, fk_mask_h, order_h, tables_h, mix_hi_h, mix_lo_h,
    out_d, out_r,
    partners, offsets, rows_all, rests_all, traces_near, rows_near, rests_near, mix_hi, mix_lo,
    blended, fk_mask, staged, res, q, other, image, image_a, image_b, sent1, sent2, raw_a, raw_b, got_a, got_b, got10, got11, got20, got21,
    left, late, rows_d, rows_r, done_d, done_r,
    y, v, w, back, u0, u1, tables, order, kept, sums_mine, sums_got,
    load_sem, in_send, in_recv, bulk_send, bulk_recv, raw_send, raw_recv, more_send, more_recv, own_sem, out_sem,
    sum_send, sum_recv,
):
    got1, got2 = (got10, got11), (got20, got21)
    me = lax.axis_index("shot")
    place = lax.axis_index("rcv")
    places = lax.axis_size("rcv")
    core = lax.rem(me, 2)
    mate = (me + 1 - 2 * core, place)
    shot_peers = [(lax.rem(me + k, groups), place) for k in range(1, groups)]
    columns = 8 if places % 8 == 0 else places
    planes = places // columns
    steps = [(i, j) for i in range(planes) for j in range(columns)][1:]
    steps.sort(key=lambda s: -(ring(s[0], planes) + ring(s[1], columns)))
    plane, column = place // columns, lax.rem(place, columns)
    place_peers = [
        (me, lax.rem(plane + i, planes) * columns + lax.rem(column + j, columns)) for i, j in steps
    ]
    peers = shot_peers + place_peers

    barrier = pltpu.get_barrier_semaphore()
    for peer in shot_peers:
        pl.semaphore_signal(barrier, inc=1, device_id=peer, device_id_type=MESH)
    loads = [
        pltpu.make_async_copy(source, target, load_sem.at[i])
        for i, (source, target) in enumerate((
            (blended_h, blended), (mix_hi_h, mix_hi), (mix_lo_h, mix_lo), (fk_mask_h, fk_mask),
            (partners_h, partners), (offsets_h, offsets), (order_h, order), (tables_h, tables),
        ))
    ]
    first_load = loads.pop(0)
    first_load.start()
    for peer in place_peers:
        pl.semaphore_signal(barrier, inc=1, device_id=peer, device_id_type=MESH)

    first_load.wait()
    for load in loads:
        load.start()
    for shot in range(6):
        for half in range(2):
            for n1 in range(ROWS):
                at = half * 8 * 96 + shot * ROWS + n1
                staged[pl.ds(at, 8, stride=96), :] = blended[
                    shot, half * 8:(half + 1) * 8, n1 * 128:(n1 + 1) * 128
                ]

    pl.semaphore_wait(barrier, len(peers))

    mine = pl.ds(pl.multiple_of(me * 96, 8), 96)
    copies = [[], []]
    own = []
    for recv in range(2):
        for k in range(1, groups):
            peer = shot_peers[k - 1]
            copies[recv].append(pltpu.make_async_remote_copy(
                src_ref=staged.at[pl.ds(pl.multiple_of(peer[0] * 192 + recv * 96, 8), 96)],
                dst_ref=res.at[recv, mine],
                send_sem=in_send.at[k - 1, recv],
                recv_sem=in_recv.at[k - 1, recv],
                device_id=peer, device_id_type=MESH,
            ))
            copies[recv][-1].start()
        own.append(pltpu.make_async_copy(
            staged.at[pl.ds(pl.multiple_of(me * 192 + recv * 96, 8), 96)],
            res.at[recv, mine], own_sem.at[recv],
        ))
        own[-1].start()

    q[...] = jnp.zeros_like(q)
    other[...] = jnp.zeros_like(other)
    for sent in (sent1, sent2):
        for recv in range(2):
            blank = jnp.zeros((HALO, ROWS, 128), F32)
            sent[recv, :HALO] = blank
            sent[recv, HALO + SHOTS:] = blank

    def clear(source, _):
        for got in (got1, got2):
            for recv in range(2):
                for trace in range(NEAR):
                    got[recv][source, trace, :BASE, :] = jnp.zeros((BASE, 128), F32)
                    got[recv][source, trace, BASE + ROWS:, :] = jnp.zeros((PITCH - BASE - ROWS, 128), F32)
                got[recv][source, NEAR] = jnp.zeros((PITCH, 128), F32)
        return 0

    lax.fori_loop(0, groups, clear, 0)
    for load in loads:
        load.wait()
    first_shot = me * 6
    shift_tables(partners, offsets, None, rows_all, rests_all, SHOTS, 0, 0, SHOTS)
    shift_tables(partners, offsets, traces_near, rows_near, rests_near, 6, first_shot, first_shot - HALO, NEAR)
    kept[...] = dot(fk_mask[...].astype(F32).astype(BF16), order[...])

    def bulk_start(field, recv, sent, got, part=0):
        count = (SENT, HALO, SENT - HALO)[part]

        def range_of(device):
            pair, there = device // 2, lax.rem(device, 2)
            start = (9 * there, 6 + 3 * there, 12 * there)[part]
            near = (HALO * there, 6 - 3 * there, 6 * there)[part]
            return pl.ds(12 * pair + start, count), pl.ds(near, count)

        slot = 2 if part == 1 else recv
        moves = []
        for k in range(1, groups):
            peer = shot_peers[k - 1]
            source, target = range_of(peer[0])
            moves.append(pltpu.make_async_remote_copy(
                src_ref=sent.at[recv, source],
                dst_ref=got[recv].at[me, target, pl.ds(BASE, ROWS)],
                send_sem=bulk_send.at[field, k - 1, slot],
                recv_sem=bulk_recv.at[field, k - 1, slot],
                device_id=peer, device_id_type=MESH,
            ))
            moves[-1].start()
        source, target = range_of(me)
        moves.append(pltpu.make_async_copy(
            sent.at[recv, source],
            got[recv].at[me, target, pl.ds(BASE, ROWS)],
            own_sem.at[2 + field * 3 + slot],
        ))
        moves[-1].start()
        return moves

    def raw_start():
        moves = []
        for which, (source, target) in enumerate(((raw_a, got_a), (raw_b, got_b))):
            for k in range(1, groups):
                peer = shot_peers[k - 1]
                start = 12 * (peer[0] // 2) + 6 + 3 * lax.rem(peer[0], 2)
                moves.append(pltpu.make_async_remote_copy(
                    src_ref=source.at[pl.ds(start, HALO)], dst_ref=target.at[me],
                    send_sem=raw_send.at[which, k - 1], recv_sem=raw_recv.at[which, k - 1],
                    device_id=peer, device_id_type=MESH,
                ))
                moves[-1].start()
            moves.append(pltpu.make_async_copy(
                source.at[pl.ds(12 * (me // 2) + 6 + 3 * core, HALO)], target.at[me],
                own_sem.at[8 + which],
            ))
            moves[-1].start()
        return moves

    def more_start(field, recv, got):
        move = pltpu.make_async_remote_copy(
            src_ref=got[recv].at[:, pl.ds(6 - 3 * core, HALO), pl.ds(BASE, ROWS)],
            dst_ref=got[recv].at[:, pl.ds(9 * core, HALO), pl.ds(BASE, ROWS)],
            send_sem=more_send.at[field, recv], recv_sem=more_recv.at[field, recv],
            device_id=mate, device_id_type=MESH,
        )
        move.start()
        return move

    def sum_start(sweep, stage, value):
        sums_mine[sweep, stage] = value
        group = SUM_ORDER[sweep][stage]
        first = group * len(place_peers)
        moves = []
        for i, peer in enumerate((place_peers, shot_peers)[group]):
            moves.append(pltpu.make_async_remote_copy(
                src_ref=sums_mine.at[sweep, stage], dst_ref=sums_got.at[sweep, first + i],
                send_sem=sum_send.at[sweep, first + i], recv_sem=sum_recv.at[sweep, first + i],
                device_id=peer, device_id_type=MESH,
            ))
            moves[-1].start()
        return moves

    def sum_end(sweep, stage, value, moves):
        first = SUM_ORDER[sweep][stage] * len(place_peers)
        for i, move in enumerate(moves):
            move.wait_recv()
            value = value + sums_got[sweep, first + i]
        return value

    def ratio(value):
        return jnp.sum(value[:4], keepdims=True) / jnp.sum(value[4:], keepdims=True)

    lane = lax.broadcasted_iota(jnp.int32, (ROWS, 128), 1)

    def blend_near(recv, got, put, after=None):
        def shots(block, _):
            for i in (block * 2, block * 2 + 1):
                terms = shift_terms(lane, rows_near, rests_near, i)
                traces = [traces_near[j, i] for j in range(PARTNERS)]
                for source in range(groups):
                    own = got[recv][source, HALO + i, pl.ds(BASE, ROWS), :]

                    def load(j, row):
                        return got[recv][source, traces[j], pl.ds(row, ROWS), :]

                    put(i, source, blended_record(own, load, terms))
            if after is not None:
                after(block)
            return 0

        lax.fori_loop(0, 3, shots, 0)

    ahead = (tables.at[0], tables.at[1], mix_hi, mix_lo, y, v)
    behind = (kept, tables.at[2], tables.at[3], mix_hi, mix_lo, y, w, back)

    zero = jnp.zeros((ROWS, 128), F32)
    shifts = (rows_all, rests_all)
    sums = (zero, zero)
    bulk1 = []
    for recv in range(2):
        own[recv].wait()
        for copy in copies[recv]:
            copy.wait()
        forward(res.at[recv], u0.at[recv], *ahead)
        inverse(u0.at[recv], 0, q.at[recv], *behind)
        fill(sent1.at[recv], lambda at: q[recv, at, :])
        if recv == 0:
            bulk1.append(bulk_start(0, 0, sent1, got1))
        sums = blend(shifts, [(q.at[recv], image.at[recv])], res.at[recv], sums)
    value = fold(sums)
    stage0 = sum_start(0, 0, value)
    bulk1.append(bulk_start(0, 1, sent1, got1))

    for recv in range(2):
        inverse(u0.at[recv], 1, q.at[recv], *behind)
        forward(image.at[recv], u1.at[recv], *ahead)
        inverse(u1.at[recv], 1, other.at[recv], *behind)
    fill(raw_a, lambda at: q[0, at, :])
    fill(raw_b, lambda at: other[0, at, :])
    pairs = ((q, image_a), (other, image_b))
    blend(shifts, [(f.at[recv], g.at[recv]) for f, g in pairs for recv in range(2)], chunk=4)
    value = sum_end(0, 0, value, stage0)
    stage1 = sum_start(0, 1, value)
    raw = raw_start()
    value = sum_end(0, 1, value, stage1)
    step1 = ratio(value)

    def second(block, sums):
        num, den = sums
        for i in range(8):
            at = pl.ds(pl.multiple_of((block * 8 + i) * ROWS, ROWS), ROWS)
            for r in range(2):
                g = image_a[r, at, :] - step1 * image_b[r, at, :]
                num = num + (res[r, at, :] - step1 * image[r, at, :]) * g
                den = den + g * g
        return num, den

    value = fold(lax.fori_loop(0, SHOTS // 8, second, (zero, zero)))
    stage2 = sum_start(1, 0, value)
    bulk2 = []
    for recv in range(2):
        fill(sent2.at[recv], lambda at: q[recv, at, :] - step1 * other[recv, at, :])
        if recv == 1:
            bulk2_mate = bulk_start(1, 1, sent2, got2, 1)
        bulk2.append(bulk_start(1, recv, sent2, got2, 2))

    for move in raw:
        move.wait()
    for source in range(groups):
        for i in range(HALO):
            got20[source, 6 - 3 * core + i, BASE:BASE + ROWS, :] = (
                got_a[source, i] - step1 * got_b[source, i]
            )
    more2 = more_start(1, 0, got2)

    more1 = []
    for recv in range(2):
        for move in bulk1[recv]:
            move.wait()
        more1.append(more_start(0, recv, got1))
    for recv in range(2):
        more1[recv].wait()

        def put_left(i, source, g):
            old = staged[pl.ds(pl.multiple_of((source * 2 + recv) * 96 + i * ROWS, 8), ROWS), :]
            left[recv, i, source] = old - step1 * g

        blend_near(recv, got1, put_left)

    value = sum_end(1, 0, value, stage2)
    stage3 = sum_start(1, 1, value)

    for move in bulk2[0]:
        move.wait()
    more2.wait()

    def put_late(i, source, g):
        late[i, source] = g

    blend_near(0, got2, put_late)
    for move in bulk2_mate:
        move.wait()
    more = more_start(1, 1, got2)
    value = sum_end(1, 1, value, stage3)
    step2 = ratio(value)

    def rows_of(recv, source):
        return slice((source * 2 + recv) * ROWS, (source * 2 + recv + 1) * ROWS)

    def combine(i, _):
        data = pl.ds(BASE, ROWS)
        for source in range(groups):
            for recv in range(2):
                rows_d[i, rows_of(recv, source), :] = (
                    step1 * got1[recv][source, HALO + i, data, :]
                    + step2 * got2[recv][source, HALO + i, data, :]
                )
            rows_r[i, rows_of(0, source), :] = left[0, i, source] - step2 * late[i, source]
        return 0

    def natural(source, target, i):
        for half in range(2):
            for n1 in range(ROWS):
                target[i, half * 8:(half + 1) * 8, n1 * 128:(n1 + 1) * 128] = source[
                    i, pl.ds(half * 128 + n1, 8, stride=ROWS), :
                ]

    def natural_d(i, _):
        natural(rows_d, done_d, i)
        return 0

    def write_r(block):
        two = pl.ds(block * 2, 2)
        return pltpu.make_async_copy(done_r.at[two], out_r.at[two], out_sem.at[1 + block])

    def put_rest(i, source, g):
        rows_r[i, rows_of(1, source), :] = left[1, i, source] - step2 * g

    def finish_r(block):
        for i in (block * 2, block * 2 + 1):
            natural(rows_r, done_r, i)
        write_r(block).start()

    for move in bulk2[1]:
        move.wait()
    lax.fori_loop(0, 6, combine, 0)
    more.wait()
    lax.fori_loop(0, 6, natural_d, 0)
    write_d = pltpu.make_async_copy(done_d, out_d, out_sem.at[0])
    write_d.start()
    blend_near(1, got2, put_rest, finish_r)
    for block in range(3):
        write_r(block).wait()
    write_d.wait()

    for move in stage0 + stage1 + stage2 + stage3:
        move.wait_send()


def write_out(d, r, out_d, out_r, held_d, held_r, sem):
    parts = [
        (source.at[i], held.at[i], target.at[i])
        for source, held, target in ((d, held_d, out_d), (r, held_r, out_r))
        for i in range(6)
    ]
    loads = [pltpu.make_async_copy(p[0], p[1], sem.at[0, i]) for i, p in enumerate(parts)]
    stores = [pltpu.make_async_copy(p[1], p[2], sem.at[1, i]) for i, p in enumerate(parts)]
    for load in loads:
        load.start()
    for load, store in zip(loads, stores):
        load.wait()
        store.start()
    for store in stores:
        store.wait()


def solution(mesh):
    groups = mesh.shape["shot"]
    peers = groups - 1 + mesh.shape["rcv"] - 1
    table_hi, table_lo = time_tables()
    tables = np.stack([table_hi, table_lo, table_hi.swapaxes(1, 2), table_lo.swapaxes(1, 2)])
    mix_hi, mix_lo = shot_operands()
    order = mask_order()

    def body(blended, partners, offsets, fk_mask):
        hbm = pl.BlockSpec(memory_space=pltpu.HBM)
        out = jax.ShapeDtypeStruct(blended.shape, F32)
        dma = pltpu.SemaphoreType.DMA
        d, r = pl.pallas_call(
            lambda *refs: kernel(groups, *refs),
            out_shape=(out, out),
            in_specs=[hbm] * 8,
            out_specs=(hbm, hbm),
            scratch_shapes=[
                *[pltpu.SMEM((PARTNERS, SHOTS), jnp.int32)] * 4,
                *[pltpu.SMEM((PARTNERS, 6), jnp.int32)] * 3,
                pltpu.VMEM(mix_hi.shape, BF16),
                pltpu.VMEM(mix_lo.shape, BF16),
                pltpu.VMEM(blended.shape, F32),
                pltpu.VMEM((ITERATIONS * SHOTS, FREQS), jnp.int32),
                pltpu.VMEM((16 * 96, 128), F32),
                pltpu.VMEM((2, SHOTS * ROWS, 128), F32),
                pltpu.VMEM((2, (SHOTS + 1) * PITCH, 128), F32),
                pltpu.VMEM((2, (SHOTS + 1) * PITCH, 128), F32),
                pltpu.VMEM((2, SHOTS * ROWS, 128), F32),
                pltpu.VMEM((2, SHOTS * ROWS, 128), F32),
                pltpu.VMEM((2, SHOTS * ROWS, 128), F32),
                pltpu.VMEM((2, SHOTS + 2 * HALO, ROWS, 128), F32),
                pltpu.VMEM((2, SHOTS + 2 * HALO, ROWS, 128), F32),
                *[pltpu.VMEM((SHOTS + 2 * HALO, ROWS, 128), F32)] * 2,
                *[pltpu.VMEM((groups, HALO, ROWS, 128), F32)] * 2,
                *[pltpu.VMEM((groups, NEAR + 1, PITCH, 128), F32)] * 4,
                pltpu.VMEM((2, 6, groups, ROWS, 128), F32),
                pltpu.VMEM((6, groups, ROWS, 128), F32),
                pltpu.VMEM((6, 16 * ROWS, 128), F32),
                pltpu.VMEM((6, 16 * ROWS, 128), F32),
                pltpu.VMEM(blended.shape, F32),
                pltpu.VMEM(blended.shape, F32),
                pltpu.VMEM((GROUPS, TRACES, 256), BF16),
                pltpu.VMEM((192, FREQS), BF16),
                pltpu.VMEM((192, FREQS), BF16),
                pltpu.VMEM((GROUPS, SHOTS, 256), F32),
                pltpu.VMEM((2, 96, FREQS), F32),
                pltpu.VMEM((2, 96, FREQS), F32),
                pltpu.VMEM((4, GROUPS, 256, 256), BF16),
                pltpu.VMEM((FREQS, FREQS), BF16),
                pltpu.VMEM((ITERATIONS * SHOTS, FREQS), F32),
                pltpu.VMEM((ITERATIONS, 2, 8, 128), F32),
                pltpu.VMEM((ITERATIONS, peers, 8, 128), F32),
                dma((8,)),
                dma((groups - 1, 2)),
                dma((groups - 1, 2)),
                dma((ITERATIONS, groups - 1, 3)),
                dma((ITERATIONS, groups - 1, 3)),
                dma((2, groups - 1)),
                dma((2, groups - 1)),
                dma((ITERATIONS, 2)),
                dma((ITERATIONS, 2)),
                dma((10,)),
                dma((4,)),
                dma((ITERATIONS, peers)),
                dma((ITERATIONS, peers)),
            ],
            compiler_params=pltpu.CompilerParams(
                collective_id=0, has_side_effects=True, vmem_limit_bytes=56 * 2**20
            ),
            name="deblend",
        )(
            partners.T, offsets.T, blended, fk_mask.reshape(ITERATIONS * SHOTS, FREQS),
            jnp.asarray(order), jnp.asarray(tables), jnp.asarray(mix_hi), jnp.asarray(mix_lo),
        )
        return pl.pallas_call(
            write_out,
            out_shape=(out, out),
            in_specs=[hbm, hbm],
            out_specs=(hbm, hbm),
            scratch_shapes=[pltpu.VMEM(blended.shape, F32), pltpu.VMEM(blended.shape, F32), dma((2, 12))],
            compiler_params=pltpu.CompilerParams(vmem_limit_bytes=56 * 2**20),
            name="write_out",
        )(d, r)

    in_specs = (P("shot", "rcv", None), P(), P(), P())
    out_specs = (P("shot", "rcv", None), P("shot", "rcv", None))
    return jax.shard_map(body, mesh=mesh, in_specs=in_specs, out_specs=out_specs, check_vma=False)
```

```python
import math

import jax
import jax.numpy as jnp
import numpy as np
from jax import lax
from jax.experimental import pallas as pl
from jax.experimental.pallas import tpu as pltpu
from jax.sharding import PartitionSpec as P

ITERATIONS = 2
PARTNERS = 4
SHOTS = 48
SAMPLES = 2048
FREQS = 1024
ROWS = 16
GROUPS = 8
PITCH = 40
BASE = 16
TRACES = 2 * SHOTS

MESH = pl.DeviceIdType.MESH
BF16 = jnp.bfloat16
F32 = jnp.float32


def group_frequencies():
    j = np.arange(64)
    rows = [np.concatenate([16 * j, 8 + 16 * j])]
    for g in range(1, GROUPS):
        rows.append(np.concatenate([g + 16 * j, 16 - g + 16 * j]))
    return np.stack(rows)


def split_np(table):
    table = table.astype(np.float32)
    high = table.astype(jnp.bfloat16)
    low = (table - high.astype(np.float32)).astype(jnp.bfloat16)
    return high, low


def time_tables():
    kept = group_frequencies()
    n2 = np.arange(128)
    out = np.zeros((GROUPS, 256, 256))
    for g in range(GROUPS):
        phase = (n2[:, None] * kept[g][None, :]) % SAMPLES
        cos = np.cos(2 * np.pi * phase / SAMPLES)
        sin = np.sin(2 * np.pi * phase / SAMPLES)
        first = np.arange(128) < 64
        if g == 0:
            out[g, :128, :128] = np.where(first, cos, 0)
            out[g, :128, 128:] = np.where(first, -sin, 0)
            out[g, 128:, :128] = np.where(first, 0, cos)
            out[g, 128:, 128:] = np.where(first, 0, -sin)
        else:
            out[g, :128, :128] = cos
            out[g, :128, 128:] = -sin
            out[g, 128:, :128] = np.where(first, sin, -sin)
            out[g, 128:, 128:] = np.where(first, cos, -cos)
    return split_np(out)


def shot_tables():
    index = np.arange(SHOTS)
    phase = 2 * np.pi * ((index[:, None] * index[None, :]) % SHOTS) / SHOTS
    cos, sin = np.cos(phase), np.sin(phase)
    forward = np.block([[cos, sin], [-sin, cos]])
    inverse = np.block([[cos, -sin], [sin, cos]]) / (SHOTS * FREQS)
    return np.stack([forward, inverse])


def shot_operands():
    high, low = split_np(shot_tables())
    return np.concatenate([high, high], axis=2), low


def mask_order():
    order = group_frequencies().reshape(-1)
    out = np.zeros((FREQS, FREQS), np.float32)
    out[order, np.arange(FREQS)] = 1
    return out.astype(jnp.bfloat16)


C1, C2, C3 = (math.cos(math.pi * i / 8) for i in (1, 2, 3))


def radix16(x):
    a = [x[n] + x[n + 8] for n in range(8)]
    b = [x[n] - x[n + 8] for n in range(8)]
    e = [a[n] + a[n + 4] for n in range(4)]
    f = [a[n] - a[n + 4] for n in range(4)]
    p02, p13 = e[0] + e[2], e[1] + e[3]
    y0, y8 = p02 + p13, p02 - p13
    re4, im4 = e[0] - e[2], e[3] - e[1]
    m, q = C2 * (f[1] - f[3]), C2 * (f[1] + f[3])
    re2, re6 = f[0] + m, f[0] - m
    im2, im6 = -f[2] - q, f[2] - q
    c = [None] + [b[n] - b[8 - n] for n in (1, 2, 3)]
    d = [None] + [b[n] + b[8 - n] for n in (1, 2, 3)]
    up, down = b[0] + C2 * c[2], b[0] - C2 * c[2]
    v, w = C1 * c[1] + C3 * c[3], C3 * c[1] - C1 * c[3]
    re1, re7, re3, re5 = up + v, up - v, down + w, down - w
    p, t = C3 * d[1] + C1 * d[3], C2 * d[2] + b[4]
    q, u = C1 * d[1] - C3 * d[3], C2 * d[2] - b[4]
    im1, im7, im3, im5 = -p - t, t - p, -q - u, u - q
    return [(y0, y8), (re1, im1), (re2, im2), (re3, im3), (re4, im4), (re5, im5), (re6, im6), (re7, im7)]


def radix16_back(z):
    (w0, w8), (re1, im1), (re2, im2), (re3, im3), (re4, im4), (re5, im5), (re6, im6), (re7, im7) = z
    plus, minus = w0 + w8, w0 - w8
    ee = [plus + re4, minus - im4, plus - re4, minus + im4]
    m, q = C2 * (re2 - re6), C2 * (im2 + im6)
    eo = [re2 + re6, m - q, im6 - im2, -m - q]
    even = [ee[n] + eo[n] for n in range(4)] + [ee[n] - eo[n] for n in range(4)]
    s17, d17, s35, d35 = re1 + re7, re1 - re7, re3 + re5, re3 - re5
    t17, g17, t35, g35 = im1 + im7, im1 - im7, im3 + im5, im3 - im5
    pc = [None, C1 * d17 + C3 * d35, C2 * (s17 - s35), C3 * d17 - C1 * d35]
    ps = [None, C3 * t17 + C1 * t35, C2 * (g17 + g35), C1 * t17 - C3 * t35]
    odd = [None] * 8
    odd[0] = s17 + s35
    odd[4] = g35 - g17
    for n in (1, 2, 3):
        odd[n] = pc[n] - ps[n]
        odd[8 - n] = -pc[n] - ps[n]
    return [even[n] + odd[n] for n in range(8)] + [even[n] - odd[n] for n in range(8)]


def split(x):
    high = x.astype(BF16)
    return high, (x - high.astype(F32)).astype(BF16)


def dot(a, b):
    return lax.dot_general(a, b, (((1,), (0,)), ((), ())), preferred_element_type=F32)


HALO = 3
SUM_ORDER = ((0, 1), (1, 0))
SENT = 9
NEAR = 12


def ring(offset, size):
    return min(offset, size - offset)


def forward(source, u, table_hi, table_lo, mix_hi, mix_lo, y, v):
    def forward_rows(block, _):
        parts = []
        for half in range(2):
            x = [source[pl.ds(block * 256 + half * 128 + n1, 8, stride=ROWS), :] for n1 in range(ROWS)]
            parts.append(radix16(x))
        row = pl.multiple_of(block * 16, 16)
        for g in range(GROUPS):
            for part in range(2):
                high, low = split(jnp.concatenate([parts[0][g][part], parts[1][g][part]], axis=0))
                y[g, pl.ds(row, 16), part * 128:(part + 1) * 128] = high
                y[g, pl.ds(row + SHOTS, 16), part * 128:(part + 1) * 128] = low
        return 0

    lax.fori_loop(0, SHOTS // 16, forward_rows, 0)

    for g in range(GROUPS):
        both = dot(y[g], table_hi[g])
        high, low = split(both[:SHOTS] + both[SHOTS:] + dot(y[g, :SHOTS], table_lo[g]))
        c = slice(g * 128, (g + 1) * 128)
        v[0:48, c] = high[:, :128]
        v[48:96, c] = high[:, 128:]
        v[96:144, c] = low[:, :128]
        v[144:192, c] = low[:, 128:]

    for b in range(FREQS // 256):
        c = slice(b * 256, (b + 1) * 256)
        u[:, c] = dot(mix_hi[0], v[:, c]) + dot(mix_lo[0], v[:96, c])


def inverse(u, sweep, q, kept, back_hi, back_lo, mix_hi, mix_lo, y, w, back):
    for b in range(FREQS // 256):
        c = slice(b * 256, (b + 1) * 256)
        keep = kept[sweep * SHOTS:(sweep + 1) * SHOTS, c]
        high, low = split(u[:, c] * jnp.concatenate([keep, keep], axis=0))
        w[:96, c] = high
        w[96:, c] = low

    for b in range(FREQS // 256):
        c = slice(b * 256, (b + 1) * 256)
        high, low = split(dot(mix_hi[1], w[:, c]) + dot(mix_lo[1], w[:96, c]))
        for i in range(2):
            d = slice(i * 128, (i + 1) * 128)
            for part, at in ((high, 0), (low, SHOTS)):
                y[b * 2 + i, at:at + SHOTS, :128] = part[:48, d]
                y[b * 2 + i, at:at + SHOTS, 128:] = part[48:, d]

    for g in range(GROUPS):
        both = dot(y[g], back_hi[g])
        back[g] = both[:SHOTS] + both[SHOTS:] + dot(y[g, :SHOTS], back_lo[g])

    def inverse_rows(block, _):
        row = pl.multiple_of(block * 8, 8)
        z = [
            (back[g, pl.ds(row, 8), 0:128], back[g, pl.ds(row, 8), 128:256])
            for g in range(GROUPS)
        ]
        x = radix16_back(z)
        for n1 in range(ROWS):
            q[pl.ds(row * PITCH + BASE + n1, 8, stride=PITCH), :] = x[n1]
        return 0

    lax.fori_loop(0, SHOTS // 8, inverse_rows, 0)


def fill(sent, record):
    def shots(block, _):
        for i in range(8):
            shot = block * 8 + i
            sent[HALO + shot] = record(pl.ds(pl.multiple_of(shot * PITCH + BASE, 8), ROWS))
        return 0

    lax.fori_loop(0, SHOTS // 8, shots, 0)


def shift_tables(partners, offsets, traces, rows, rests, count, first_shot, first, blank):
    def one_shot(i, _):
        for j in range(PARTNERS):
            partner, delay = partners[j, first_shot + i], offsets[j, first_shot + i]
            trace = jnp.where(partner >= 0, jnp.clip(partner - first, 0, blank - 1), blank)
            if traces is None:
                rows[j, i] = trace * PITCH + BASE - (delay >> 7)
            else:
                traces[j, i] = trace
                rows[j, i] = BASE - (delay >> 7)
            rests[j, i] = delay & 127
        return 0

    lax.fori_loop(0, count, one_shot, 0)


def shift_terms(lane, rows, rests, i):
    return [(rows[j, i], rests[j, i], lane < 128 - rests[j, i]) for j in range(PARTNERS)]


def blended_record(own, load, terms):
    g = own
    for j, (row, rest, near) in enumerate(terms):
        g = g + pltpu.roll(jnp.where(near, load(j, row), load(j, row - 1)), rest, 1)
    return g


def blend(tables, fields, residual=None, sums=0, chunk=16):
    lane = lax.broadcasted_iota(jnp.int32, (ROWS, 128), 1)

    def shots(block, sums):
        terms = [shift_terms(lane, *tables, block * chunk + i) for i in range(chunk)]
        for i in range(chunk):
            shot = block * chunk + i
            at = pl.ds(pl.multiple_of(shot * ROWS, ROWS), ROWS)
            for q, image in fields:
                own = q[pl.ds(pl.multiple_of(shot * PITCH + BASE, 8), ROWS), :]
                g = blended_record(own, lambda j, row: q[pl.ds(row, ROWS), :], terms[i])
                image[at, :] = g
                if residual is not None:
                    sums = (sums[0] + residual[at, :] * g, sums[1] + g * g)
        return sums

    return lax.fori_loop(0, SHOTS // chunk, shots, sums)


def fold(sums):
    return jnp.concatenate([x[:4] + x[4:8] + x[8:12] + x[12:] for x in sums], axis=0)


def kernel(
    groups,
    partners_h, offsets_h, blended_h, fk_mask_h, order_h, tables_h, mix_hi_h, mix_lo_h,
    out_d, out_r,
    partners, offsets, rows_all, rests_all, traces_near, rows_near, rests_near, mix_hi, mix_lo,
    blended, fk_mask, staged, res, q, other, image, image_a, image_b, sent1, sent2, raw_a, raw_b, got_a, got_b, got10, got11, got20, got21,
    left, late, rows_d, rows_r, done_d, done_r,
    y, v, w, back, u0, u1, tables, order, kept, sums_mine, sums_got,
    load_sem, in_send, in_recv, bulk_send, bulk_recv, raw_send, raw_recv, more_send, more_recv, own_sem, out_sem,
    sum_send, sum_recv,
):
    got1, got2 = (got10, got11), (got20, got21)
    me = lax.axis_index("shot")
    place = lax.axis_index("rcv")
    places = lax.axis_size("rcv")
    core = lax.rem(me, 2)
    mate = (me + 1 - 2 * core, place)
    shot_peers = [(lax.rem(me + k, groups), place) for k in range(1, groups)]
    columns = 8 if places % 8 == 0 else places
    planes = places // columns
    steps = [(i, j) for i in range(planes) for j in range(columns)][1:]
    steps.sort(key=lambda s: -(ring(s[0], planes) + ring(s[1], columns)))
    plane, column = place // columns, lax.rem(place, columns)
    place_peers = [
        (me, lax.rem(plane + i, planes) * columns + lax.rem(column + j, columns)) for i, j in steps
    ]
    peers = shot_peers + place_peers

    barrier = pltpu.get_barrier_semaphore()
    for peer in shot_peers:
        pl.semaphore_signal(barrier, inc=1, device_id=peer, device_id_type=MESH)
    loads = [
        pltpu.make_async_copy(source, target, load_sem.at[i])
        for i, (source, target) in enumerate((
            (blended_h, blended), (mix_hi_h, mix_hi), (mix_lo_h, mix_lo), (fk_mask_h, fk_mask),
            (partners_h, partners), (offsets_h, offsets), (order_h, order), (tables_h, tables),
        ))
    ]
    first_load = loads.pop(0)
    first_load.start()
    for peer in place_peers:
        pl.semaphore_signal(barrier, inc=1, device_id=peer, device_id_type=MESH)

    first_load.wait()
    for load in loads:
        load.start()
    for shot in range(6):
        for half in range(2):
            for n1 in range(ROWS):
                at = half * 8 * 96 + shot * ROWS + n1
                staged[pl.ds(at, 8, stride=96), :] = blended[
                    shot, half * 8:(half + 1) * 8, n1 * 128:(n1 + 1) * 128
                ]

    pl.semaphore_wait(barrier, len(peers))

    mine = pl.ds(pl.multiple_of(me * 96, 8), 96)
    copies = [[], []]
    own = []
    for recv in range(2):
        for k in range(1, groups):
            peer = shot_peers[k - 1]
            copies[recv].append(pltpu.make_async_remote_copy(
                src_ref=staged.at[pl.ds(pl.multiple_of(peer[0] * 192 + recv * 96, 8), 96)],
                dst_ref=res.at[recv, mine],
                send_sem=in_send.at[k - 1, recv],
                recv_sem=in_recv.at[k - 1, recv],
                device_id=peer, device_id_type=MESH,
            ))
            copies[recv][-1].start()
        own.append(pltpu.make_async_copy(
            staged.at[pl.ds(pl.multiple_of(me * 192 + recv * 96, 8), 96)],
            res.at[recv, mine], own_sem.at[recv],
        ))
        own[-1].start()

    q[...] = jnp.zeros_like(q)
    other[...] = jnp.zeros_like(other)
    for sent in (sent1, sent2):
        for recv in range(2):
            blank = jnp.zeros((HALO, ROWS, 128), F32)
            sent[recv, :HALO] = blank
            sent[recv, HALO + SHOTS:] = blank

    def clear(source, _):
        for got in (got1, got2):
            for recv in range(2):
                for trace in range(NEAR):
                    got[recv][source, trace, :BASE, :] = jnp.zeros((BASE, 128), F32)
                    got[recv][source, trace, BASE + ROWS:, :] = jnp.zeros((PITCH - BASE - ROWS, 128), F32)
                got[recv][source, NEAR] = jnp.zeros((PITCH, 128), F32)
        return 0

    lax.fori_loop(0, groups, clear, 0)
    for load in loads:
        load.wait()
    first_shot = me * 6
    shift_tables(partners, offsets, None, rows_all, rests_all, SHOTS, 0, 0, SHOTS)
    shift_tables(partners, offsets, traces_near, rows_near, rests_near, 6, first_shot, first_shot - HALO, NEAR)
    kept[...] = dot(fk_mask[...].astype(F32).astype(BF16), order[...])

    def bulk_start(field, recv, sent, got, part=0):
        count = (SENT, HALO, SENT - HALO)[part]

        def range_of(device):
            pair, there = device // 2, lax.rem(device, 2)
            start = (9 * there, 6 + 3 * there, 12 * there)[part]
            near = (HALO * there, 6 - 3 * there, 6 * there)[part]
            return pl.ds(12 * pair + start, count), pl.ds(near, count)

        slot = 2 if part == 1 else recv
        moves = []
        for k in range(1, groups):
            peer = shot_peers[k - 1]
            source, target = range_of(peer[0])
            moves.append(pltpu.make_async_remote_copy(
                src_ref=sent.at[recv, source],
                dst_ref=got[recv].at[me, target, pl.ds(BASE, ROWS)],
                send_sem=bulk_send.at[field, k - 1, slot],
                recv_sem=bulk_recv.at[field, k - 1, slot],
                device_id=peer, device_id_type=MESH,
            ))
            moves[-1].start()
        source, target = range_of(me)
        moves.append(pltpu.make_async_copy(
            sent.at[recv, source],
            got[recv].at[me, target, pl.ds(BASE, ROWS)],
            own_sem.at[2 + field * 3 + slot],
        ))
        moves[-1].start()
        return moves

    def raw_start():
        moves = []
        for which, (source, target) in enumerate(((raw_a, got_a), (raw_b, got_b))):
            for k in range(1, groups):
                peer = shot_peers[k - 1]
                start = 12 * (peer[0] // 2) + 6 + 3 * lax.rem(peer[0], 2)
                moves.append(pltpu.make_async_remote_copy(
                    src_ref=source.at[pl.ds(start, HALO)], dst_ref=target.at[me],
                    send_sem=raw_send.at[which, k - 1], recv_sem=raw_recv.at[which, k - 1],
                    device_id=peer, device_id_type=MESH,
                ))
                moves[-1].start()
            moves.append(pltpu.make_async_copy(
                source.at[pl.ds(12 * (me // 2) + 6 + 3 * core, HALO)], target.at[me],
                own_sem.at[8 + which],
            ))
            moves[-1].start()
        return moves

    def more_start(field, recv, got):
        move = pltpu.make_async_remote_copy(
            src_ref=got[recv].at[:, pl.ds(6 - 3 * core, HALO), pl.ds(BASE, ROWS)],
            dst_ref=got[recv].at[:, pl.ds(9 * core, HALO), pl.ds(BASE, ROWS)],
            send_sem=more_send.at[field, recv], recv_sem=more_recv.at[field, recv],
            device_id=mate, device_id_type=MESH,
        )
        move.start()
        return move

    def sum_start(sweep, stage, value):
        sums_mine[sweep, stage] = value
        group = SUM_ORDER[sweep][stage]
        first = group * len(place_peers)
        moves = []
        for i, peer in enumerate((place_peers, shot_peers)[group]):
            moves.append(pltpu.make_async_remote_copy(
                src_ref=sums_mine.at[sweep, stage], dst_ref=sums_got.at[sweep, first + i],
                send_sem=sum_send.at[sweep, first + i], recv_sem=sum_recv.at[sweep, first + i],
                device_id=peer, device_id_type=MESH,
            ))
            moves[-1].start()
        return moves

    def sum_end(sweep, stage, value, moves):
        first = SUM_ORDER[sweep][stage] * len(place_peers)
        for i, move in enumerate(moves):
            move.wait_recv()
            value = value + sums_got[sweep, first + i]
        return value

    def ratio(value):
        return jnp.sum(value[:4], keepdims=True) / jnp.sum(value[4:], keepdims=True)

    lane = lax.broadcasted_iota(jnp.int32, (ROWS, 128), 1)

    def blend_near(recv, got, put, after=None):
        def shots(block, _):
            for i in (block * 2, block * 2 + 1):
                terms = shift_terms(lane, rows_near, rests_near, i)
                traces = [traces_near[j, i] for j in range(PARTNERS)]
                for source in range(groups):
                    own = got[recv][source, HALO + i, pl.ds(BASE, ROWS), :]

                    def load(j, row):
                        return got[recv][source, traces[j], pl.ds(row, ROWS), :]

                    put(i, source, blended_record(own, load, terms))
            if after is not None:
                after(block)
            return 0

        lax.fori_loop(0, 3, shots, 0)

    ahead = (tables.at[0], tables.at[1], mix_hi, mix_lo, y, v)
    behind = (kept, tables.at[2], tables.at[3], mix_hi, mix_lo, y, w, back)

    zero = jnp.zeros((ROWS, 128), F32)
    shifts = (rows_all, rests_all)
    sums = (zero, zero)
    bulk1 = []
    for recv in range(2):
        own[recv].wait()
        for copy in copies[recv]:
            copy.wait()
        forward(res.at[recv], u0.at[recv], *ahead)
        inverse(u0.at[recv], 0, q.at[recv], *behind)
        fill(sent1.at[recv], lambda at: q[recv, at, :])
        if recv == 0:
            bulk1.append(bulk_start(0, 0, sent1, got1))
        sums = blend(shifts, [(q.at[recv], image.at[recv])], res.at[recv], sums)
    value = fold(sums)
    stage0 = sum_start(0, 0, value)
    bulk1.append(bulk_start(0, 1, sent1, got1))

    for recv in range(2):
        inverse(u0.at[recv], 1, q.at[recv], *behind)
        forward(image.at[recv], u1.at[recv], *ahead)
        inverse(u1.at[recv], 1, other.at[recv], *behind)
    fill(raw_a, lambda at: q[0, at, :])
    fill(raw_b, lambda at: other[0, at, :])
    pairs = ((q, image_a), (other, image_b))
    value = sum_end(0, 0, value, stage0)
    stage1 = sum_start(0, 1, value)
    raw = raw_start()
    blend(shifts, [(f.at[recv], g.at[recv]) for f, g in pairs for recv in range(2)], chunk=4)
    value = sum_end(0, 1, value, stage1)
    step1 = ratio(value)

    def second(block, sums):
        num, den = sums
        for i in range(8):
            at = pl.ds(pl.multiple_of((block * 8 + i) * ROWS, ROWS), ROWS)
            for r in range(2):
                g = image_a[r, at, :] - step1 * image_b[r, at, :]
                num = num + (res[r, at, :] - step1 * image[r, at, :]) * g
                den = den + g * g
        return num, den

    value = fold(lax.fori_loop(0, SHOTS // 8, second, (zero, zero)))
    stage2 = sum_start(1, 0, value)
    bulk2 = []
    for recv in range(2):
        fill(sent2.at[recv], lambda at: q[recv, at, :] - step1 * other[recv, at, :])
        if recv == 1:
            bulk2_mate = bulk_start(1, 1, sent2, got2, 1)
        bulk2.append(bulk_start(1, recv, sent2, got2, 2))

    for move in raw:
        move.wait()
    for source in range(groups):
        for i in range(HALO):
            got20[source, 6 - 3 * core + i, BASE:BASE + ROWS, :] = (
                got_a[source, i] - step1 * got_b[source, i]
            )
    more2 = more_start(1, 0, got2)

    more1 = []
    for recv in range(2):
        for move in bulk1[recv]:
            move.wait()
        more1.append(more_start(0, recv, got1))
    for recv in range(2):
        more1[recv].wait()

        def put_left(i, source, g):
            old = staged[pl.ds(pl.multiple_of((source * 2 + recv) * 96 + i * ROWS, 8), ROWS), :]
            left[recv, i, source] = old - step1 * g

        blend_near(recv, got1, put_left)
        if recv == 0:
            value = sum_end(1, 0, value, stage2)
            stage3 = sum_start(1, 1, value)

    for move in bulk2[0]:
        move.wait()
    more2.wait()

    def put_late(i, source, g):
        late[i, source] = g

    blend_near(0, got2, put_late)
    for move in bulk2_mate:
        move.wait()
    more = more_start(1, 1, got2)
    value = sum_end(1, 1, value, stage3)
    step2 = ratio(value)

    def rows_of(recv, source):
        return slice((source * 2 + recv) * ROWS, (source * 2 + recv + 1) * ROWS)

    def combine(i, _):
        data = pl.ds(BASE, ROWS)
        for source in range(groups):
            at = rows_of(0, source)
            rows_d[i, at, :] = (
                step1 * got10[source, HALO + i, data, :] + step2 * got20[source, HALO + i, data, :]
            )
            rows_r[i, at, :] = left[0, i, source] - step2 * late[i, source]
        return 0

    def natural(source, target, i):
        for half in range(2):
            for n1 in range(ROWS):
                target[i, half * 8:(half + 1) * 8, n1 * 128:(n1 + 1) * 128] = source[
                    i, pl.ds(half * 128 + n1, 8, stride=ROWS), :
                ]

    def writes(block):
        two = pl.ds(block * 2, 2)
        return (
            pltpu.make_async_copy(done_d.at[two], out_d.at[two], out_sem.at[block]),
            pltpu.make_async_copy(done_r.at[two], out_r.at[two], out_sem.at[3 + block]),
        )

    def put_rest(i, source, g):
        at = rows_of(1, source)
        data = pl.ds(BASE, ROWS)
        rows_r[i, at, :] = left[1, i, source] - step2 * g
        rows_d[i, at, :] = (
            step1 * got11[source, HALO + i, data, :] + step2 * got21[source, HALO + i, data, :]
        )

    def finish_two(block):
        for i in (block * 2, block * 2 + 1):
            natural(rows_d, done_d, i)
            natural(rows_r, done_r, i)
        for write in writes(block):
            write.start()

    lax.fori_loop(0, 6, combine, 0)
    for move in bulk2[1]:
        move.wait()
    more.wait()
    blend_near(1, got2, put_rest, finish_two)
    for block in range(3):
        for write in writes(block):
            write.wait()

    for move in stage0 + stage1 + stage2 + stage3:
        move.wait_send()


def write_out(d, r, out_d, out_r, held_d, held_r, sem):
    parts = [
        (source.at[i], held.at[i], target.at[i])
        for source, held, target in ((d, held_d, out_d), (r, held_r, out_r))
        for i in range(6)
    ]
    loads = [pltpu.make_async_copy(p[0], p[1], sem.at[0, i]) for i, p in enumerate(parts)]
    stores = [pltpu.make_async_copy(p[1], p[2], sem.at[1, i]) for i, p in enumerate(parts)]
    for load in loads:
        load.start()
    for load, store in zip(loads, stores):
        load.wait()
        store.start()
    for store in stores:
        store.wait()


def solution(mesh):
    groups = mesh.shape["shot"]
    peers = groups - 1 + mesh.shape["rcv"] - 1
    table_hi, table_lo = time_tables()
    tables = np.stack([table_hi, table_lo, table_hi.swapaxes(1, 2), table_lo.swapaxes(1, 2)])
    mix_hi, mix_lo = shot_operands()
    order = mask_order()

    def body(blended, partners, offsets, fk_mask):
        hbm = pl.BlockSpec(memory_space=pltpu.HBM)
        out = jax.ShapeDtypeStruct(blended.shape, F32)
        dma = pltpu.SemaphoreType.DMA
        d, r = pl.pallas_call(
            lambda *refs: kernel(groups, *refs),
            out_shape=(out, out),
            in_specs=[hbm] * 8,
            out_specs=(hbm, hbm),
            scratch_shapes=[
                *[pltpu.SMEM((PARTNERS, SHOTS), jnp.int32)] * 4,
                *[pltpu.SMEM((PARTNERS, 6), jnp.int32)] * 3,
                pltpu.VMEM(mix_hi.shape, BF16),
                pltpu.VMEM(mix_lo.shape, BF16),
                pltpu.VMEM(blended.shape, F32),
                pltpu.VMEM((ITERATIONS * SHOTS, FREQS), jnp.int32),
                pltpu.VMEM((16 * 96, 128), F32),
                pltpu.VMEM((2, SHOTS * ROWS, 128), F32),
                pltpu.VMEM((2, (SHOTS + 1) * PITCH, 128), F32),
                pltpu.VMEM((2, (SHOTS + 1) * PITCH, 128), F32),
                pltpu.VMEM((2, SHOTS * ROWS, 128), F32),
                pltpu.VMEM((2, SHOTS * ROWS, 128), F32),
                pltpu.VMEM((2, SHOTS * ROWS, 128), F32),
                pltpu.VMEM((2, SHOTS + 2 * HALO, ROWS, 128), F32),
                pltpu.VMEM((2, SHOTS + 2 * HALO, ROWS, 128), F32),
                *[pltpu.VMEM((SHOTS + 2 * HALO, ROWS, 128), F32)] * 2,
                *[pltpu.VMEM((groups, HALO, ROWS, 128), F32)] * 2,
                *[pltpu.VMEM((groups, NEAR + 1, PITCH, 128), F32)] * 4,
                pltpu.VMEM((2, 6, groups, ROWS, 128), F32),
                pltpu.VMEM((6, groups, ROWS, 128), F32),
                pltpu.VMEM((6, 16 * ROWS, 128), F32),
                pltpu.VMEM((6, 16 * ROWS, 128), F32),
                pltpu.VMEM(blended.shape, F32),
                pltpu.VMEM(blended.shape, F32),
                pltpu.VMEM((GROUPS, TRACES, 256), BF16),
                pltpu.VMEM((192, FREQS), BF16),
                pltpu.VMEM((192, FREQS), BF16),
                pltpu.VMEM((GROUPS, SHOTS, 256), F32),
                pltpu.VMEM((2, 96, FREQS), F32),
                pltpu.VMEM((2, 96, FREQS), F32),
                pltpu.VMEM((4, GROUPS, 256, 256), BF16),
                pltpu.VMEM((FREQS, FREQS), BF16),
                pltpu.VMEM((ITERATIONS * SHOTS, FREQS), F32),
                pltpu.VMEM((ITERATIONS, 2, 8, 128), F32),
                pltpu.VMEM((ITERATIONS, peers, 8, 128), F32),
                dma((8,)),
                dma((groups - 1, 2)),
                dma((groups - 1, 2)),
                dma((ITERATIONS, groups - 1, 3)),
                dma((ITERATIONS, groups - 1, 3)),
                dma((2, groups - 1)),
                dma((2, groups - 1)),
                dma((ITERATIONS, 2)),
                dma((ITERATIONS, 2)),
                dma((10,)),
                dma((6,)),
                dma((ITERATIONS, peers)),
                dma((ITERATIONS, peers)),
            ],
            compiler_params=pltpu.CompilerParams(
                collective_id=0, has_side_effects=True, vmem_limit_bytes=56 * 2**20
            ),
            name="deblend",
        )(
            partners.T, offsets.T, blended, fk_mask.reshape(ITERATIONS * SHOTS, FREQS),
            jnp.asarray(order), jnp.asarray(tables), jnp.asarray(mix_hi), jnp.asarray(mix_lo),
        )
        return pl.pallas_call(
            write_out,
            out_shape=(out, out),
            in_specs=[hbm, hbm],
            out_specs=(hbm, hbm),
            scratch_shapes=[pltpu.VMEM(blended.shape, F32), pltpu.VMEM(blended.shape, F32), dma((2, 12))],
            compiler_params=pltpu.CompilerParams(vmem_limit_bytes=56 * 2**20),
            name="write_out",
        )(d, r)

    in_specs = (P("shot", "rcv", None), P(), P(), P())
    out_specs = (P("shot", "rcv", None), P("shot", "rcv", None))
    return jax.shard_map(body, mesh=mesh, in_specs=in_specs, out_specs=out_specs, check_vma=False)
```

```python
import math

import jax
import jax.numpy as jnp
import numpy as np
from jax import lax
from jax.experimental import pallas as pl
from jax.experimental.pallas import tpu as pltpu
from jax.sharding import PartitionSpec as P

ITERATIONS = 2
PARTNERS = 4
SHOTS = 48
SAMPLES = 2048
FREQS = 1024
ROWS = 16
GROUPS = 8
PITCH = 40
BASE = 16
TRACES = 2 * SHOTS

MESH = pl.DeviceIdType.MESH
BF16 = jnp.bfloat16
F32 = jnp.float32


def group_frequencies():
    j = np.arange(64)
    rows = [np.concatenate([16 * j, 8 + 16 * j])]
    for g in range(1, GROUPS):
        rows.append(np.concatenate([g + 16 * j, 16 - g + 16 * j]))
    return np.stack(rows)


def split_np(table):
    table = table.astype(np.float32)
    high = table.astype(jnp.bfloat16)
    low = (table - high.astype(np.float32)).astype(jnp.bfloat16)
    return high, low


def time_tables():
    kept = group_frequencies()
    n2 = np.arange(128)
    out = np.zeros((GROUPS, 256, 256))
    for g in range(GROUPS):
        phase = (n2[:, None] * kept[g][None, :]) % SAMPLES
        cos = np.cos(2 * np.pi * phase / SAMPLES)
        sin = np.sin(2 * np.pi * phase / SAMPLES)
        first = np.arange(128) < 64
        if g == 0:
            out[g, :128, :128] = np.where(first, cos, 0)
            out[g, :128, 128:] = np.where(first, -sin, 0)
            out[g, 128:, :128] = np.where(first, 0, cos)
            out[g, 128:, 128:] = np.where(first, 0, -sin)
        else:
            out[g, :128, :128] = cos
            out[g, :128, 128:] = -sin
            out[g, 128:, :128] = np.where(first, sin, -sin)
            out[g, 128:, 128:] = np.where(first, cos, -cos)
    return split_np(out)


def shot_tables():
    index = np.arange(SHOTS)
    phase = 2 * np.pi * ((index[:, None] * index[None, :]) % SHOTS) / SHOTS
    cos, sin = np.cos(phase), np.sin(phase)
    forward = np.block([[cos, sin], [-sin, cos]])
    inverse = np.block([[cos, -sin], [sin, cos]]) / (SHOTS * FREQS)
    return np.stack([forward, inverse])


def shot_operands():
    high, low = split_np(shot_tables())
    return np.concatenate([high, high], axis=2), low


def mask_order():
    order = group_frequencies().reshape(-1)
    out = np.zeros((FREQS, FREQS), np.float32)
    out[order, np.arange(FREQS)] = 1
    return out.astype(jnp.bfloat16)


C1, C2, C3 = (math.cos(math.pi * i / 8) for i in (1, 2, 3))


def radix16(x):
    a = [x[n] + x[n + 8] for n in range(8)]
    b = [x[n] - x[n + 8] for n in range(8)]
    e = [a[n] + a[n + 4] for n in range(4)]
    f = [a[n] - a[n + 4] for n in range(4)]
    p02, p13 = e[0] + e[2], e[1] + e[3]
    y0, y8 = p02 + p13, p02 - p13
    re4, im4 = e[0] - e[2], e[3] - e[1]
    m, q = C2 * (f[1] - f[3]), C2 * (f[1] + f[3])
    re2, re6 = f[0] + m, f[0] - m
    im2, im6 = -f[2] - q, f[2] - q
    c = [None] + [b[n] - b[8 - n] for n in (1, 2, 3)]
    d = [None] + [b[n] + b[8 - n] for n in (1, 2, 3)]
    up, down = b[0] + C2 * c[2], b[0] - C2 * c[2]
    v, w = C1 * c[1] + C3 * c[3], C3 * c[1] - C1 * c[3]
    re1, re7, re3, re5 = up + v, up - v, down + w, down - w
    p, t = C3 * d[1] + C1 * d[3], C2 * d[2] + b[4]
    q, u = C1 * d[1] - C3 * d[3], C2 * d[2] - b[4]
    im1, im7, im3, im5 = -p - t, t - p, -q - u, u - q
    return [(y0, y8), (re1, im1), (re2, im2), (re3, im3), (re4, im4), (re5, im5), (re6, im6), (re7, im7)]


def radix16_back(z):
    (w0, w8), (re1, im1), (re2, im2), (re3, im3), (re4, im4), (re5, im5), (re6, im6), (re7, im7) = z
    plus, minus = w0 + w8, w0 - w8
    ee = [plus + re4, minus - im4, plus - re4, minus + im4]
    m, q = C2 * (re2 - re6), C2 * (im2 + im6)
    eo = [re2 + re6, m - q, im6 - im2, -m - q]
    even = [ee[n] + eo[n] for n in range(4)] + [ee[n] - eo[n] for n in range(4)]
    s17, d17, s35, d35 = re1 + re7, re1 - re7, re3 + re5, re3 - re5
    t17, g17, t35, g35 = im1 + im7, im1 - im7, im3 + im5, im3 - im5
    pc = [None, C1 * d17 + C3 * d35, C2 * (s17 - s35), C3 * d17 - C1 * d35]
    ps = [None, C3 * t17 + C1 * t35, C2 * (g17 + g35), C1 * t17 - C3 * t35]
    odd = [None] * 8
    odd[0] = s17 + s35
    odd[4] = g35 - g17
    for n in (1, 2, 3):
        odd[n] = pc[n] - ps[n]
        odd[8 - n] = -pc[n] - ps[n]
    return [even[n] + odd[n] for n in range(8)] + [even[n] - odd[n] for n in range(8)]


def split(x):
    high = x.astype(BF16)
    return high, (x - high.astype(F32)).astype(BF16)


def dot(a, b):
    return lax.dot_general(a, b, (((1,), (0,)), ((), ())), preferred_element_type=F32)


HALO = 3
FAR_FIRST = (4, 3, 5, 2, 6, 1, 7)
SUM_ORDER = ((0, 1), (1, 0))
SENT = 9
NEAR = 12


def ring(offset, size):
    return min(offset, size - offset)


def forward(source, u, table_hi, table_lo, mix_hi, mix_lo, y, v):
    def forward_rows(block, _):
        parts = []
        for half in range(2):
            x = [source[pl.ds(block * 256 + half * 128 + n1, 8, stride=ROWS), :] for n1 in range(ROWS)]
            parts.append(radix16(x))
        row = pl.multiple_of(block * 16, 16)
        for g in range(GROUPS):
            for part in range(2):
                high, low = split(jnp.concatenate([parts[0][g][part], parts[1][g][part]], axis=0))
                y[g, pl.ds(row, 16), part * 128:(part + 1) * 128] = high
                y[g, pl.ds(row + SHOTS, 16), part * 128:(part + 1) * 128] = low
        return 0

    lax.fori_loop(0, SHOTS // 16, forward_rows, 0)

    for g in range(GROUPS):
        both = dot(y[g], table_hi[g])
        high, low = split(both[:SHOTS] + both[SHOTS:] + dot(y[g, :SHOTS], table_lo[g]))
        c = slice(g * 128, (g + 1) * 128)
        v[0:48, c] = high[:, :128]
        v[48:96, c] = high[:, 128:]
        v[96:144, c] = low[:, :128]
        v[144:192, c] = low[:, 128:]

    for b in range(FREQS // 256):
        c = slice(b * 256, (b + 1) * 256)
        u[:, c] = dot(mix_hi[0], v[:, c]) + dot(mix_lo[0], v[:96, c])


def inverse(u, sweep, q, kept, back_hi, back_lo, mix_hi, mix_lo, y, w, back):
    for b in range(FREQS // 256):
        c = slice(b * 256, (b + 1) * 256)
        keep = kept[sweep * SHOTS:(sweep + 1) * SHOTS, c]
        high, low = split(u[:, c] * jnp.concatenate([keep, keep], axis=0))
        w[:96, c] = high
        w[96:, c] = low

    for b in range(FREQS // 256):
        c = slice(b * 256, (b + 1) * 256)
        high, low = split(dot(mix_hi[1], w[:, c]) + dot(mix_lo[1], w[:96, c]))
        for i in range(2):
            d = slice(i * 128, (i + 1) * 128)
            for part, at in ((high, 0), (low, SHOTS)):
                y[b * 2 + i, at:at + SHOTS, :128] = part[:48, d]
                y[b * 2 + i, at:at + SHOTS, 128:] = part[48:, d]

    for g in range(GROUPS):
        both = dot(y[g], back_hi[g])
        back[g] = both[:SHOTS] + both[SHOTS:] + dot(y[g, :SHOTS], back_lo[g])

    def inverse_rows(block, _):
        row = pl.multiple_of(block * 8, 8)
        z = [
            (back[g, pl.ds(row, 8), 0:128], back[g, pl.ds(row, 8), 128:256])
            for g in range(GROUPS)
        ]
        x = radix16_back(z)
        for n1 in range(ROWS):
            q[pl.ds(row * PITCH + BASE + n1, 8, stride=PITCH), :] = x[n1]
        return 0

    lax.fori_loop(0, SHOTS // 8, inverse_rows, 0)


def fill(sent, record):
    def shots(block, _):
        for i in range(8):
            shot = block * 8 + i
            sent[HALO + shot] = record(pl.ds(pl.multiple_of(shot * PITCH + BASE, 8), ROWS))
        return 0

    lax.fori_loop(0, SHOTS // 8, shots, 0)


def shift_tables(partners, offsets, traces, rows, rests, count, first_shot, first, blank):
    def one_shot(i, _):
        for j in range(PARTNERS):
            partner, delay = partners[j, first_shot + i], offsets[j, first_shot + i]
            trace = jnp.where(partner >= 0, jnp.clip(partner - first, 0, blank - 1), blank)
            if traces is None:
                rows[j, i] = trace * PITCH + BASE - (delay >> 7)
            else:
                traces[j, i] = trace
                rows[j, i] = BASE - (delay >> 7)
            rests[j, i] = delay & 127
        return 0

    lax.fori_loop(0, count, one_shot, 0)


def shift_terms(lane, rows, rests, i):
    return [(rows[j, i], rests[j, i], lane < 128 - rests[j, i]) for j in range(PARTNERS)]


def blended_record(own, load, terms):
    g = own
    for j, (row, rest, near) in enumerate(terms):
        g = g + pltpu.roll(jnp.where(near, load(j, row), load(j, row - 1)), rest, 1)
    return g


def blend(tables, fields, residual=None, sums=0, chunk=16):
    lane = lax.broadcasted_iota(jnp.int32, (ROWS, 128), 1)

    def shots(block, sums):
        terms = [shift_terms(lane, *tables, block * chunk + i) for i in range(chunk)]
        for i in range(chunk):
            shot = block * chunk + i
            at = pl.ds(pl.multiple_of(shot * ROWS, ROWS), ROWS)
            for q, image in fields:
                own = q[pl.ds(pl.multiple_of(shot * PITCH + BASE, 8), ROWS), :]
                g = blended_record(own, lambda j, row: q[pl.ds(row, ROWS), :], terms[i])
                image[at, :] = g
                if residual is not None:
                    sums = (sums[0] + residual[at, :] * g, sums[1] + g * g)
        return sums

    return lax.fori_loop(0, SHOTS // chunk, shots, sums)


def fold(sums):
    return jnp.concatenate([x[:4] + x[4:8] + x[8:12] + x[12:] for x in sums], axis=0)


def kernel(
    groups,
    partners_h, offsets_h, blended_h, fk_mask_h, order_h, tables_h, mix_hi_h, mix_lo_h,
    out_d, out_r,
    partners, offsets, rows_all, rests_all, traces_near, rows_near, rests_near, mix_hi, mix_lo,
    blended, fk_mask, staged, res, q, other, image, image_a, image_b, sent1, sent2, raw_a, raw_b, got_a, got_b, got10, got11, got20, got21,
    left, late, rows_d, rows_r, done_d, done_r,
    y, v, w, back, u0, u1, tables, order, kept, sums_mine, sums_got,
    load_sem, in_send, in_recv, bulk_send, bulk_recv, raw_send, raw_recv, more_send, more_recv, own_sem, out_sem,
    sum_send, sum_recv,
):
    got1, got2 = (got10, got11), (got20, got21)
    me = lax.axis_index("shot")
    place = lax.axis_index("rcv")
    places = lax.axis_size("rcv")
    core = lax.rem(me, 2)
    mate = (me + 1 - 2 * core, place)
    shot_peers = [(lax.rem(me + k, groups), place) for k in range(1, groups)]
    columns = 8 if places % 8 == 0 else places
    planes = places // columns
    steps = [(i, j) for i in range(planes) for j in range(columns)][1:]
    steps.sort(key=lambda s: -(ring(s[0], planes) + ring(s[1], columns)))
    plane, column = place // columns, lax.rem(place, columns)
    place_peers = [
        (me, lax.rem(plane + i, planes) * columns + lax.rem(column + j, columns)) for i, j in steps
    ]
    peers = shot_peers + place_peers

    barrier = pltpu.get_barrier_semaphore()
    for peer in shot_peers:
        pl.semaphore_signal(barrier, inc=1, device_id=peer, device_id_type=MESH)
    loads = [
        pltpu.make_async_copy(source, target, load_sem.at[i])
        for i, (source, target) in enumerate((
            (blended_h, blended), (mix_hi_h, mix_hi), (mix_lo_h, mix_lo), (fk_mask_h, fk_mask),
            (partners_h, partners), (offsets_h, offsets), (order_h, order), (tables_h, tables),
        ))
    ]
    first_load = loads.pop(0)
    first_load.start()
    for peer in place_peers:
        pl.semaphore_signal(barrier, inc=1, device_id=peer, device_id_type=MESH)

    first_load.wait()
    for load in loads:
        load.start()
    for shot in range(6):
        for half in range(2):
            for n1 in range(ROWS):
                at = half * 8 * 96 + shot * ROWS + n1
                staged[pl.ds(at, 8, stride=96), :] = blended[
                    shot, half * 8:(half + 1) * 8, n1 * 128:(n1 + 1) * 128
                ]

    pl.semaphore_wait(barrier, len(peers))

    mine = pl.ds(pl.multiple_of(me * 96, 8), 96)
    copies = [[], []]
    own = []
    for recv in range(2):
        for k in range(1, groups):
            peer = shot_peers[k - 1]
            copies[recv].append(pltpu.make_async_remote_copy(
                src_ref=staged.at[pl.ds(pl.multiple_of(peer[0] * 192 + recv * 96, 8), 96)],
                dst_ref=res.at[recv, mine],
                send_sem=in_send.at[k - 1, recv],
                recv_sem=in_recv.at[k - 1, recv],
                device_id=peer, device_id_type=MESH,
            ))
            copies[recv][-1].start()
        own.append(pltpu.make_async_copy(
            staged.at[pl.ds(pl.multiple_of(me * 192 + recv * 96, 8), 96)],
            res.at[recv, mine], own_sem.at[recv],
        ))
        own[-1].start()

    q[...] = jnp.zeros_like(q)
    other[...] = jnp.zeros_like(other)
    for sent in (sent1, sent2):
        for recv in range(2):
            blank = jnp.zeros((HALO, ROWS, 128), F32)
            sent[recv, :HALO] = blank
            sent[recv, HALO + SHOTS:] = blank

    def clear(source, _):
        for got in (got1, got2):
            for recv in range(2):
                for trace in range(NEAR):
                    got[recv][source, trace, :BASE, :] = jnp.zeros((BASE, 128), F32)
                    got[recv][source, trace, BASE + ROWS:, :] = jnp.zeros((PITCH - BASE - ROWS, 128), F32)
                got[recv][source, NEAR] = jnp.zeros((PITCH, 128), F32)
        return 0

    lax.fori_loop(0, groups, clear, 0)
    for load in loads:
        load.wait()
    first_shot = me * 6
    shift_tables(partners, offsets, None, rows_all, rests_all, SHOTS, 0, 0, SHOTS)
    shift_tables(partners, offsets, traces_near, rows_near, rests_near, 6, first_shot, first_shot - HALO, NEAR)
    kept[...] = dot(fk_mask[...].astype(F32).astype(BF16), order[...])

    def bulk_start(field, recv, sent, got, part=0):
        count = (SENT, HALO, SENT - HALO)[part]

        def range_of(device):
            pair, there = device // 2, lax.rem(device, 2)
            start = (9 * there, 6 + 3 * there, 12 * there)[part]
            near = (HALO * there, 6 - 3 * there, 6 * there)[part]
            return pl.ds(12 * pair + start, count), pl.ds(near, count)

        slot = 2 if part == 1 else recv
        moves = []
        for k in FAR_FIRST:
            peer = shot_peers[k - 1]
            source, target = range_of(peer[0])
            moves.append(pltpu.make_async_remote_copy(
                src_ref=sent.at[recv, source],
                dst_ref=got[recv].at[me, target, pl.ds(BASE, ROWS)],
                send_sem=bulk_send.at[field, k - 1, slot],
                recv_sem=bulk_recv.at[field, k - 1, slot],
                device_id=peer, device_id_type=MESH,
            ))
            moves[-1].start()
        source, target = range_of(me)
        moves.append(pltpu.make_async_copy(
            sent.at[recv, source],
            got[recv].at[me, target, pl.ds(BASE, ROWS)],
            own_sem.at[2 + field * 3 + slot],
        ))
        moves[-1].start()
        return moves

    def raw_start():
        moves = []
        for which, (source, target) in enumerate(((raw_a, got_a), (raw_b, got_b))):
            for k in range(1, groups):
                peer = shot_peers[k - 1]
                start = 12 * (peer[0] // 2) + 6 + 3 * lax.rem(peer[0], 2)
                moves.append(pltpu.make_async_remote_copy(
                    src_ref=source.at[pl.ds(start, HALO)], dst_ref=target.at[me],
                    send_sem=raw_send.at[which, k - 1], recv_sem=raw_recv.at[which, k - 1],
                    device_id=peer, device_id_type=MESH,
                ))
                moves[-1].start()
            moves.append(pltpu.make_async_copy(
                source.at[pl.ds(12 * (me // 2) + 6 + 3 * core, HALO)], target.at[me],
                own_sem.at[8 + which],
            ))
            moves[-1].start()
        return moves

    def more_start(field, recv, got):
        move = pltpu.make_async_remote_copy(
            src_ref=got[recv].at[:, pl.ds(6 - 3 * core, HALO), pl.ds(BASE, ROWS)],
            dst_ref=got[recv].at[:, pl.ds(9 * core, HALO), pl.ds(BASE, ROWS)],
            send_sem=more_send.at[field, recv], recv_sem=more_recv.at[field, recv],
            device_id=mate, device_id_type=MESH,
        )
        move.start()
        return move

    def sum_start(sweep, stage, value):
        sums_mine[sweep, stage] = value
        group = SUM_ORDER[sweep][stage]
        first = group * len(place_peers)
        moves = []
        for i, peer in enumerate((place_peers, shot_peers)[group]):
            moves.append(pltpu.make_async_remote_copy(
                src_ref=sums_mine.at[sweep, stage], dst_ref=sums_got.at[sweep, first + i],
                send_sem=sum_send.at[sweep, first + i], recv_sem=sum_recv.at[sweep, first + i],
                device_id=peer, device_id_type=MESH,
            ))
            moves[-1].start()
        return moves

    def sum_end(sweep, stage, value, moves):
        first = SUM_ORDER[sweep][stage] * len(place_peers)
        for i, move in enumerate(moves):
            move.wait_recv()
            value = value + sums_got[sweep, first + i]
        return value

    def ratio(value):
        return jnp.sum(value[:4], keepdims=True) / jnp.sum(value[4:], keepdims=True)

    lane = lax.broadcasted_iota(jnp.int32, (ROWS, 128), 1)

    def blend_near(recv, got, put, after=None):
        def shots(block, _):
            for i in (block * 2, block * 2 + 1):
                terms = shift_terms(lane, rows_near, rests_near, i)
                traces = [traces_near[j, i] for j in range(PARTNERS)]
                for source in range(groups):
                    own = got[recv][source, HALO + i, pl.ds(BASE, ROWS), :]

                    def load(j, row):
                        return got[recv][source, traces[j], pl.ds(row, ROWS), :]

                    put(i, source, blended_record(own, load, terms))
            if after is not None:
                after(block)
            return 0

        lax.fori_loop(0, 3, shots, 0)

    ahead = (tables.at[0], tables.at[1], mix_hi, mix_lo, y, v)
    behind = (kept, tables.at[2], tables.at[3], mix_hi, mix_lo, y, w, back)

    zero = jnp.zeros((ROWS, 128), F32)
    shifts = (rows_all, rests_all)
    sums = (zero, zero)
    bulk1 = []
    for recv in range(2):
        own[recv].wait()
        for copy in copies[recv]:
            copy.wait()
        forward(res.at[recv], u0.at[recv], *ahead)
        inverse(u0.at[recv], 0, q.at[recv], *behind)
        fill(sent1.at[recv], lambda at: q[recv, at, :])
        if recv == 0:
            bulk1.append(bulk_start(0, 0, sent1, got1))
        sums = blend(shifts, [(q.at[recv], image.at[recv])], res.at[recv], sums)
    value = fold(sums)
    stage0 = sum_start(0, 0, value)
    bulk1.append(bulk_start(0, 1, sent1, got1))

    for recv in range(2):
        inverse(u0.at[recv], 1, q.at[recv], *behind)
        forward(image.at[recv], u1.at[recv], *ahead)
        inverse(u1.at[recv], 1, other.at[recv], *behind)
    fill(raw_a, lambda at: q[0, at, :])
    fill(raw_b, lambda at: other[0, at, :])
    pairs = ((q, image_a), (other, image_b))
    value = sum_end(0, 0, value, stage0)
    stage1 = sum_start(0, 1, value)
    raw = raw_start()
    blend(shifts, [(f.at[recv], g.at[recv]) for f, g in pairs for recv in range(2)], chunk=4)
    value = sum_end(0, 1, value, stage1)
    step1 = ratio(value)

    def second(block, sums):
        num, den = sums
        for i in range(8):
            at = pl.ds(pl.multiple_of((block * 8 + i) * ROWS, ROWS), ROWS)
            for r in range(2):
                g = image_a[r, at, :] - step1 * image_b[r, at, :]
                num = num + (res[r, at, :] - step1 * image[r, at, :]) * g
                den = den + g * g
        return num, den

    value = fold(lax.fori_loop(0, SHOTS // 8, second, (zero, zero)))
    stage2 = sum_start(1, 0, value)
    bulk2 = []
    for recv in range(2):
        fill(sent2.at[recv], lambda at: q[recv, at, :] - step1 * other[recv, at, :])
        if recv == 1:
            bulk2_mate = bulk_start(1, 1, sent2, got2, 1)
        bulk2.append(bulk_start(1, recv, sent2, got2, 2))

    for move in raw:
        move.wait()
    for source in range(groups):
        for i in range(HALO):
            got20[source, 6 - 3 * core + i, BASE:BASE + ROWS, :] = (
                got_a[source, i] - step1 * got_b[source, i]
            )
    more2 = more_start(1, 0, got2)

    more1 = []
    for recv in range(2):
        for move in bulk1[recv]:
            move.wait()
        more1.append(more_start(0, recv, got1))
    for recv in range(2):
        more1[recv].wait()

        def put_left(i, source, g):
            old = staged[pl.ds(pl.multiple_of((source * 2 + recv) * 96 + i * ROWS, 8), ROWS), :]
            left[recv, i, source] = old - step1 * g

        blend_near(recv, got1, put_left)
        if recv == 0:
            value = sum_end(1, 0, value, stage2)
            stage3 = sum_start(1, 1, value)

    for move in bulk2[0]:
        move.wait()
    more2.wait()

    def put_late(i, source, g):
        late[i, source] = g

    blend_near(0, got2, put_late)
    for move in bulk2_mate:
        move.wait()
    more = more_start(1, 1, got2)
    value = sum_end(1, 1, value, stage3)
    step2 = ratio(value)

    def rows_of(recv, source):
        return slice((source * 2 + recv) * ROWS, (source * 2 + recv + 1) * ROWS)

    def combine(i, _):
        data = pl.ds(BASE, ROWS)
        for source in range(groups):
            at = rows_of(0, source)
            rows_d[i, at, :] = (
                step1 * got10[source, HALO + i, data, :] + step2 * got20[source, HALO + i, data, :]
            )
            rows_r[i, at, :] = left[0, i, source] - step2 * late[i, source]
        return 0

    def natural(source, target, i):
        for half in range(2):
            for n1 in range(ROWS):
                target[i, half * 8:(half + 1) * 8, n1 * 128:(n1 + 1) * 128] = source[
                    i, pl.ds(half * 128 + n1, 8, stride=ROWS), :
                ]

    def writes(block):
        two = pl.ds(block * 2, 2)
        return (
            pltpu.make_async_copy(done_d.at[two], out_d.at[two], out_sem.at[block]),
            pltpu.make_async_copy(done_r.at[two], out_r.at[two], out_sem.at[3 + block]),
        )

    def put_rest(i, source, g):
        at = rows_of(1, source)
        data = pl.ds(BASE, ROWS)
        rows_r[i, at, :] = left[1, i, source] - step2 * g
        rows_d[i, at, :] = (
            step1 * got11[source, HALO + i, data, :] + step2 * got21[source, HALO + i, data, :]
        )

    def finish_two(block):
        for i in (block * 2, block * 2 + 1):
            natural(rows_d, done_d, i)
            natural(rows_r, done_r, i)
        for write in writes(block):
            write.start()

    lax.fori_loop(0, 6, combine, 0)
    for move in bulk2[1]:
        move.wait()
    more.wait()
    blend_near(1, got2, put_rest, finish_two)
    for block in range(3):
        for write in writes(block):
            write.wait()

    for move in stage0 + stage1 + stage2 + stage3:
        move.wait_send()


def write_out(d, r, out_d, out_r, held_d, held_r, sem):
    parts = [
        (source.at[i], held.at[i], target.at[i])
        for source, held, target in ((d, held_d, out_d), (r, held_r, out_r))
        for i in range(6)
    ]
    loads = [pltpu.make_async_copy(p[0], p[1], sem.at[0, i]) for i, p in enumerate(parts)]
    stores = [pltpu.make_async_copy(p[1], p[2], sem.at[1, i]) for i, p in enumerate(parts)]
    for load in loads:
        load.start()
    for load, store in zip(loads, stores):
        load.wait()
        store.start()
    for store in stores:
        store.wait()


def solution(mesh):
    groups = mesh.shape["shot"]
    peers = groups - 1 + mesh.shape["rcv"] - 1
    table_hi, table_lo = time_tables()
    tables = np.stack([table_hi, table_lo, table_hi.swapaxes(1, 2), table_lo.swapaxes(1, 2)])
    mix_hi, mix_lo = shot_operands()
    order = mask_order()

    def body(blended, partners, offsets, fk_mask):
        hbm = pl.BlockSpec(memory_space=pltpu.HBM)
        out = jax.ShapeDtypeStruct(blended.shape, F32)
        dma = pltpu.SemaphoreType.DMA
        d, r = pl.pallas_call(
            lambda *refs: kernel(groups, *refs),
            out_shape=(out, out),
            in_specs=[hbm] * 8,
            out_specs=(hbm, hbm),
            scratch_shapes=[
                *[pltpu.SMEM((PARTNERS, SHOTS), jnp.int32)] * 4,
                *[pltpu.SMEM((PARTNERS, 6), jnp.int32)] * 3,
                pltpu.VMEM(mix_hi.shape, BF16),
                pltpu.VMEM(mix_lo.shape, BF16),
                pltpu.VMEM(blended.shape, F32),
                pltpu.VMEM((ITERATIONS * SHOTS, FREQS), jnp.int32),
                pltpu.VMEM((16 * 96, 128), F32),
                pltpu.VMEM((2, SHOTS * ROWS, 128), F32),
                pltpu.VMEM((2, (SHOTS + 1) * PITCH, 128), F32),
                pltpu.VMEM((2, (SHOTS + 1) * PITCH, 128), F32),
                pltpu.VMEM((2, SHOTS * ROWS, 128), F32),
                pltpu.VMEM((2, SHOTS * ROWS, 128), F32),
                pltpu.VMEM((2, SHOTS * ROWS, 128), F32),
                pltpu.VMEM((2, SHOTS + 2 * HALO, ROWS, 128), F32),
                pltpu.VMEM((2, SHOTS + 2 * HALO, ROWS, 128), F32),
                *[pltpu.VMEM((SHOTS + 2 * HALO, ROWS, 128), F32)] * 2,
                *[pltpu.VMEM((groups, HALO, ROWS, 128), F32)] * 2,
                *[pltpu.VMEM((groups, NEAR + 1, PITCH, 128), F32)] * 4,
                pltpu.VMEM((2, 6, groups, ROWS, 128), F32),
                pltpu.VMEM((6, groups, ROWS, 128), F32),
                pltpu.VMEM((6, 16 * ROWS, 128), F32),
                pltpu.VMEM((6, 16 * ROWS, 128), F32),
                pltpu.VMEM(blended.shape, F32),
                pltpu.VMEM(blended.shape, F32),
                pltpu.VMEM((GROUPS, TRACES, 256), BF16),
                pltpu.VMEM((192, FREQS), BF16),
                pltpu.VMEM((192, FREQS), BF16),
                pltpu.VMEM((GROUPS, SHOTS, 256), F32),
                pltpu.VMEM((2, 96, FREQS), F32),
                pltpu.VMEM((2, 96, FREQS), F32),
                pltpu.VMEM((4, GROUPS, 256, 256), BF16),
                pltpu.VMEM((FREQS, FREQS), BF16),
                pltpu.VMEM((ITERATIONS * SHOTS, FREQS), F32),
                pltpu.VMEM((ITERATIONS, 2, 8, 128), F32),
                pltpu.VMEM((ITERATIONS, peers, 8, 128), F32),
                dma((8,)),
                dma((groups - 1, 2)),
                dma((groups - 1, 2)),
                dma((ITERATIONS, groups - 1, 3)),
                dma((ITERATIONS, groups - 1, 3)),
                dma((2, groups - 1)),
                dma((2, groups - 1)),
                dma((ITERATIONS, 2)),
                dma((ITERATIONS, 2)),
                dma((10,)),
                dma((6,)),
                dma((ITERATIONS, peers)),
                dma((ITERATIONS, peers)),
            ],
            compiler_params=pltpu.CompilerParams(
                collective_id=0, has_side_effects=True, vmem_limit_bytes=56 * 2**20
            ),
            name="deblend",
        )(
            partners.T, offsets.T, blended, fk_mask.reshape(ITERATIONS * SHOTS, FREQS),
            jnp.asarray(order), jnp.asarray(tables), jnp.asarray(mix_hi), jnp.asarray(mix_lo),
        )
        return pl.pallas_call(
            write_out,
            out_shape=(out, out),
            in_specs=[hbm, hbm],
            out_specs=(hbm, hbm),
            scratch_shapes=[pltpu.VMEM(blended.shape, F32), pltpu.VMEM(blended.shape, F32), dma((2, 12))],
            compiler_params=pltpu.CompilerParams(vmem_limit_bytes=56 * 2**20),
            name="write_out",
        )(d, r)

    in_specs = (P("shot", "rcv", None), P(), P(), P())
    out_specs = (P("shot", "rcv", None), P("shot", "rcv", None))
    return jax.shard_map(body, mesh=mesh, in_specs=in_specs, out_specs=out_specs, check_vma=False)
```

```python
import math

import jax
import jax.numpy as jnp
import numpy as np
from jax import lax
from jax.experimental import pallas as pl
from jax.experimental.pallas import tpu as pltpu
from jax.sharding import PartitionSpec as P

ITERATIONS = 2
PARTNERS = 4
SHOTS = 48
SAMPLES = 2048
FREQS = 1024
ROWS = 16
GROUPS = 8
PITCH = 40
BASE = 16
TRACES = 2 * SHOTS

MESH = pl.DeviceIdType.MESH
BF16 = jnp.bfloat16
F32 = jnp.float32


def group_frequencies():
    j = np.arange(64)
    rows = [np.concatenate([16 * j, 8 + 16 * j])]
    for g in range(1, GROUPS):
        rows.append(np.concatenate([g + 16 * j, 16 - g + 16 * j]))
    return np.stack(rows)


def split_np(table):
    table = table.astype(np.float32)
    high = table.astype(jnp.bfloat16)
    low = (table - high.astype(np.float32)).astype(jnp.bfloat16)
    return high, low


def time_tables():
    kept = group_frequencies()
    n2 = np.arange(128)
    out = np.zeros((GROUPS, 256, 256))
    for g in range(GROUPS):
        phase = (n2[:, None] * kept[g][None, :]) % SAMPLES
        cos = np.cos(2 * np.pi * phase / SAMPLES)
        sin = np.sin(2 * np.pi * phase / SAMPLES)
        first = np.arange(128) < 64
        if g == 0:
            out[g, :128, :128] = np.where(first, cos, 0)
            out[g, :128, 128:] = np.where(first, -sin, 0)
            out[g, 128:, :128] = np.where(first, 0, cos)
            out[g, 128:, 128:] = np.where(first, 0, -sin)
        else:
            out[g, :128, :128] = cos
            out[g, :128, 128:] = -sin
            out[g, 128:, :128] = np.where(first, sin, -sin)
            out[g, 128:, 128:] = np.where(first, cos, -cos)
    return split_np(out)


def shot_tables():
    index = np.arange(SHOTS)
    phase = 2 * np.pi * ((index[:, None] * index[None, :]) % SHOTS) / SHOTS
    cos, sin = np.cos(phase), np.sin(phase)
    forward = np.block([[cos, sin], [-sin, cos]])
    inverse = np.block([[cos, -sin], [sin, cos]]) / (SHOTS * FREQS)
    return np.stack([forward, inverse])


def shot_operands():
    high, low = split_np(shot_tables())
    return np.concatenate([high, high], axis=2), low


def mask_order():
    order = group_frequencies().reshape(-1)
    out = np.zeros((FREQS, FREQS), np.float32)
    out[order, np.arange(FREQS)] = 1
    return out.astype(jnp.bfloat16)


C1, C2, C3 = (math.cos(math.pi * i / 8) for i in (1, 2, 3))


def radix16(x):
    a = [x[n] + x[n + 8] for n in range(8)]
    b = [x[n] - x[n + 8] for n in range(8)]
    e = [a[n] + a[n + 4] for n in range(4)]
    f = [a[n] - a[n + 4] for n in range(4)]
    p02, p13 = e[0] + e[2], e[1] + e[3]
    y0, y8 = p02 + p13, p02 - p13
    re4, im4 = e[0] - e[2], e[3] - e[1]
    m, q = C2 * (f[1] - f[3]), C2 * (f[1] + f[3])
    re2, re6 = f[0] + m, f[0] - m
    im2, im6 = -f[2] - q, f[2] - q
    c = [None] + [b[n] - b[8 - n] for n in (1, 2, 3)]
    d = [None] + [b[n] + b[8 - n] for n in (1, 2, 3)]
    up, down = b[0] + C2 * c[2], b[0] - C2 * c[2]
    v, w = C1 * c[1] + C3 * c[3], C3 * c[1] - C1 * c[3]
    re1, re7, re3, re5 = up + v, up - v, down + w, down - w
    p, t = C3 * d[1] + C1 * d[3], C2 * d[2] + b[4]
    q, u = C1 * d[1] - C3 * d[3], C2 * d[2] - b[4]
    im1, im7, im3, im5 = -p - t, t - p, -q - u, u - q
    return [(y0, y8), (re1, im1), (re2, im2), (re3, im3), (re4, im4), (re5, im5), (re6, im6), (re7, im7)]


def radix16_back(z):
    (w0, w8), (re1, im1), (re2, im2), (re3, im3), (re4, im4), (re5, im5), (re6, im6), (re7, im7) = z
    plus, minus = w0 + w8, w0 - w8
    ee = [plus + re4, minus - im4, plus - re4, minus + im4]
    m, q = C2 * (re2 - re6), C2 * (im2 + im6)
    eo = [re2 + re6, m - q, im6 - im2, -m - q]
    even = [ee[n] + eo[n] for n in range(4)] + [ee[n] - eo[n] for n in range(4)]
    s17, d17, s35, d35 = re1 + re7, re1 - re7, re3 + re5, re3 - re5
    t17, g17, t35, g35 = im1 + im7, im1 - im7, im3 + im5, im3 - im5
    pc = [None, C1 * d17 + C3 * d35, C2 * (s17 - s35), C3 * d17 - C1 * d35]
    ps = [None, C3 * t17 + C1 * t35, C2 * (g17 + g35), C1 * t17 - C3 * t35]
    odd = [None] * 8
    odd[0] = s17 + s35
    odd[4] = g35 - g17
    for n in (1, 2, 3):
        odd[n] = pc[n] - ps[n]
        odd[8 - n] = -pc[n] - ps[n]
    return [even[n] + odd[n] for n in range(8)] + [even[n] - odd[n] for n in range(8)]


def split(x):
    high = x.astype(BF16)
    return high, (x - high.astype(F32)).astype(BF16)


def dot(a, b):
    return lax.dot_general(a, b, (((1,), (0,)), ((), ())), preferred_element_type=F32)


HALO = 3
FAR_FIRST = (4, 3, 5, 2, 6, 1, 7)
SUM_ORDER = ((0, 1), (1, 0))
SENT = 9
NEAR = 12


def ring(offset, size):
    return min(offset, size - offset)


def forward(source, u, table_hi, table_lo, mix_hi, mix_lo, y, v):
    def forward_rows(block, _):
        parts = []
        for half in range(2):
            x = [source[pl.ds(block * 256 + half * 128 + n1, 8, stride=ROWS), :] for n1 in range(ROWS)]
            parts.append(radix16(x))
        row = pl.multiple_of(block * 16, 16)
        for g in range(GROUPS):
            for part in range(2):
                high, low = split(jnp.concatenate([parts[0][g][part], parts[1][g][part]], axis=0))
                y[g, pl.ds(row, 16), part * 128:(part + 1) * 128] = high
                y[g, pl.ds(row + SHOTS, 16), part * 128:(part + 1) * 128] = low
        return 0

    lax.fori_loop(0, SHOTS // 16, forward_rows, 0)

    for g in range(GROUPS):
        both = dot(y[g], table_hi[g])
        high, low = split(both[:SHOTS] + both[SHOTS:] + dot(y[g, :SHOTS], table_lo[g]))
        c = slice(g * 128, (g + 1) * 128)
        v[0:48, c] = high[:, :128]
        v[48:96, c] = high[:, 128:]
        v[96:144, c] = low[:, :128]
        v[144:192, c] = low[:, 128:]

    for b in range(FREQS // 256):
        c = slice(b * 256, (b + 1) * 256)
        u[:, c] = dot(mix_hi[0], v[:, c]) + dot(mix_lo[0], v[:96, c])


def inverse(u, sweep, q, kept, back_hi, back_lo, mix_hi, mix_lo, y, w, back):
    for b in range(FREQS // 256):
        c = slice(b * 256, (b + 1) * 256)
        keep = kept[sweep * SHOTS:(sweep + 1) * SHOTS, c]
        high, low = split(u[:, c] * jnp.concatenate([keep, keep], axis=0))
        w[:96, c] = high
        w[96:, c] = low

    for b in range(FREQS // 256):
        c = slice(b * 256, (b + 1) * 256)
        high, low = split(dot(mix_hi[1], w[:, c]) + dot(mix_lo[1], w[:96, c]))
        for i in range(2):
            d = slice(i * 128, (i + 1) * 128)
            for part, at in ((high, 0), (low, SHOTS)):
                y[b * 2 + i, at:at + SHOTS, :128] = part[:48, d]
                y[b * 2 + i, at:at + SHOTS, 128:] = part[48:, d]

    for g in range(GROUPS):
        both = dot(y[g], back_hi[g])
        back[g] = both[:SHOTS] + both[SHOTS:] + dot(y[g, :SHOTS], back_lo[g])

    def inverse_rows(block, _):
        row = pl.multiple_of(block * 8, 8)
        z = [
            (back[g, pl.ds(row, 8), 0:128], back[g, pl.ds(row, 8), 128:256])
            for g in range(GROUPS)
        ]
        x = radix16_back(z)
        for n1 in range(ROWS):
            q[pl.ds(row * PITCH + BASE + n1, 8, stride=PITCH), :] = x[n1]
        return 0

    lax.fori_loop(0, SHOTS // 8, inverse_rows, 0)


def fill(sent, record):
    def shots(block, _):
        for i in range(8):
            shot = block * 8 + i
            sent[HALO + shot] = record(pl.ds(pl.multiple_of(shot * PITCH + BASE, 8), ROWS))
        return 0

    lax.fori_loop(0, SHOTS // 8, shots, 0)


def shift_tables(partners, offsets, traces, rows, rests, count, first_shot, first, blank):
    def one_shot(i, _):
        for j in range(PARTNERS):
            partner, delay = partners[j, first_shot + i], offsets[j, first_shot + i]
            trace = jnp.where(partner >= 0, jnp.clip(partner - first, 0, blank - 1), blank)
            if traces is None:
                rows[j, i] = trace * PITCH + BASE - (delay >> 7)
            else:
                traces[j, i] = trace
                rows[j, i] = BASE - (delay >> 7)
            rests[j, i] = delay & 127
        return 0

    lax.fori_loop(0, count, one_shot, 0)


def shift_terms(lane, rows, rests, i):
    return [(rows[j, i], rests[j, i], lane < 128 - rests[j, i]) for j in range(PARTNERS)]


def blended_record(own, load, terms):
    g = own
    for j, (row, rest, near) in enumerate(terms):
        g = g + pltpu.roll(jnp.where(near, load(j, row), load(j, row - 1)), rest, 1)
    return g


def blend(tables, fields, residual=None, sums=0, chunk=16):
    lane = lax.broadcasted_iota(jnp.int32, (ROWS, 128), 1)

    def shots(block, sums):
        terms = [shift_terms(lane, *tables, block * chunk + i) for i in range(chunk)]
        for i in range(chunk):
            shot = block * chunk + i
            at = pl.ds(pl.multiple_of(shot * ROWS, ROWS), ROWS)
            for q, image in fields:
                own = q[pl.ds(pl.multiple_of(shot * PITCH + BASE, 8), ROWS), :]
                g = blended_record(own, lambda j, row: q[pl.ds(row, ROWS), :], terms[i])
                image[at, :] = g
                if residual is not None:
                    sums = (sums[0] + residual[at, :] * g, sums[1] + g * g)
        return sums

    return lax.fori_loop(0, SHOTS // chunk, shots, sums)


def fold(sums):
    return jnp.concatenate([x[:4] + x[4:8] + x[8:12] + x[12:] for x in sums], axis=0)


def kernel(
    groups,
    partners_h, offsets_h, blended_h, fk_mask_h, order_h, tables_h, mix_hi_h, mix_lo_h,
    out_d, out_r,
    partners, offsets, rows_all, rests_all, traces_near, rows_near, rests_near, mix_hi, mix_lo,
    blended, fk_mask, staged, res, q, other, image, image_a, image_b, sent1, sent2, raw_a, raw_b, got_a, got_b, got10, got11, got20, got21,
    left, late, rows_d, rows_r, done_d, done_r,
    y, v, w, back, u0, u1, tables, order, kept, sums_mine, sums_got,
    load_sem, in_send, in_recv, bulk_send, bulk_recv, raw_send, raw_recv, more_send, more_recv, own_sem, out_sem,
    sum_send, sum_recv,
):
    got1, got2 = (got10, got11), (got20, got21)
    me = lax.axis_index("shot")
    place = lax.axis_index("rcv")
    places = lax.axis_size("rcv")
    core = lax.rem(me, 2)
    mate = (me + 1 - 2 * core, place)
    shot_peers = [(lax.rem(me + k, groups), place) for k in range(1, groups)]
    columns = 8 if places % 8 == 0 else places
    planes = places // columns
    steps = [(i, j) for i in range(planes) for j in range(columns)][1:]
    steps.sort(key=lambda s: -(ring(s[0], planes) + ring(s[1], columns)))
    plane, column = place // columns, lax.rem(place, columns)
    place_peers = [
        (me, lax.rem(plane + i, planes) * columns + lax.rem(column + j, columns)) for i, j in steps
    ]
    peers = shot_peers + place_peers

    barrier = pltpu.get_barrier_semaphore()
    for peer in shot_peers:
        pl.semaphore_signal(barrier, inc=1, device_id=peer, device_id_type=MESH)
    loads = [
        pltpu.make_async_copy(source, target, load_sem.at[i])
        for i, (source, target) in enumerate((
            (blended_h, blended), (mix_hi_h, mix_hi), (mix_lo_h, mix_lo), (fk_mask_h, fk_mask),
            (partners_h, partners), (offsets_h, offsets), (order_h, order), (tables_h, tables),
        ))
    ]
    first_load = loads.pop(0)
    first_load.start()
    for peer in place_peers:
        pl.semaphore_signal(barrier, inc=1, device_id=peer, device_id_type=MESH)

    first_load.wait()
    for load in loads:
        load.start()
    for shot in range(6):
        for half in range(2):
            for n1 in range(ROWS):
                at = half * 8 * 96 + shot * ROWS + n1
                staged[pl.ds(at, 8, stride=96), :] = blended[
                    shot, half * 8:(half + 1) * 8, n1 * 128:(n1 + 1) * 128
                ]

    pl.semaphore_wait(barrier, len(peers))

    mine = pl.ds(pl.multiple_of(me * 96, 8), 96)
    copies = [[], []]
    own = []
    for recv in range(2):
        for k in range(1, groups):
            peer = shot_peers[k - 1]
            copies[recv].append(pltpu.make_async_remote_copy(
                src_ref=staged.at[pl.ds(pl.multiple_of(peer[0] * 192 + recv * 96, 8), 96)],
                dst_ref=res.at[recv, mine],
                send_sem=in_send.at[k - 1, recv],
                recv_sem=in_recv.at[k - 1, recv],
                device_id=peer, device_id_type=MESH,
            ))
            copies[recv][-1].start()
        own.append(pltpu.make_async_copy(
            staged.at[pl.ds(pl.multiple_of(me * 192 + recv * 96, 8), 96)],
            res.at[recv, mine], own_sem.at[recv],
        ))
        own[-1].start()

    q[...] = jnp.zeros_like(q)
    other[...] = jnp.zeros_like(other)
    for sent in (sent1, sent2):
        for recv in range(2):
            blank = jnp.zeros((HALO, ROWS, 128), F32)
            sent[recv, :HALO] = blank
            sent[recv, HALO + SHOTS:] = blank

    def clear(source, _):
        for got in (got1, got2):
            for recv in range(2):
                for trace in range(NEAR):
                    got[recv][source, trace, :BASE, :] = jnp.zeros((BASE, 128), F32)
                    got[recv][source, trace, BASE + ROWS:, :] = jnp.zeros((PITCH - BASE - ROWS, 128), F32)
                got[recv][source, NEAR] = jnp.zeros((PITCH, 128), F32)
        return 0

    lax.fori_loop(0, groups, clear, 0)
    for load in loads:
        load.wait()
    first_shot = me * 6
    shift_tables(partners, offsets, None, rows_all, rests_all, SHOTS, 0, 0, SHOTS)
    shift_tables(partners, offsets, traces_near, rows_near, rests_near, 6, first_shot, first_shot - HALO, NEAR)
    kept[...] = dot(fk_mask[...].astype(F32).astype(BF16), order[...])

    def bulk_start(field, recv, sent, got, part=0):
        count = (SENT, HALO, SENT - HALO)[part]

        def range_of(device):
            pair, there = device // 2, lax.rem(device, 2)
            start = (9 * there, 6 + 3 * there, 12 * there)[part]
            near = (HALO * there, 6 - 3 * there, 6 * there)[part]
            return pl.ds(12 * pair + start, count), pl.ds(near, count)

        slot = 2 if part == 1 else recv
        moves = []
        for k in FAR_FIRST:
            peer = shot_peers[k - 1]
            source, target = range_of(peer[0])
            moves.append(pltpu.make_async_remote_copy(
                src_ref=sent.at[recv, source],
                dst_ref=got[recv].at[me, target, pl.ds(BASE, ROWS)],
                send_sem=bulk_send.at[field, k - 1, slot],
                recv_sem=bulk_recv.at[field, k - 1, slot],
                device_id=peer, device_id_type=MESH,
            ))
            moves[-1].start()
        source, target = range_of(me)
        moves.append(pltpu.make_async_copy(
            sent.at[recv, source],
            got[recv].at[me, target, pl.ds(BASE, ROWS)],
            own_sem.at[2 + field * 3 + slot],
        ))
        moves[-1].start()
        return moves

    def raw_start():
        moves = []
        for which, (source, target) in enumerate(((raw_a, got_a), (raw_b, got_b))):
            for k in FAR_FIRST:
                peer = shot_peers[k - 1]
                start = 12 * (peer[0] // 2) + 6 + 3 * lax.rem(peer[0], 2)
                moves.append(pltpu.make_async_remote_copy(
                    src_ref=source.at[pl.ds(start, HALO)], dst_ref=target.at[me],
                    send_sem=raw_send.at[which, k - 1], recv_sem=raw_recv.at[which, k - 1],
                    device_id=peer, device_id_type=MESH,
                ))
                moves[-1].start()
            moves.append(pltpu.make_async_copy(
                source.at[pl.ds(12 * (me // 2) + 6 + 3 * core, HALO)], target.at[me],
                own_sem.at[8 + which],
            ))
            moves[-1].start()
        return moves

    def more_start(field, recv, got):
        move = pltpu.make_async_remote_copy(
            src_ref=got[recv].at[:, pl.ds(6 - 3 * core, HALO), pl.ds(BASE, ROWS)],
            dst_ref=got[recv].at[:, pl.ds(9 * core, HALO), pl.ds(BASE, ROWS)],
            send_sem=more_send.at[field, recv], recv_sem=more_recv.at[field, recv],
            device_id=mate, device_id_type=MESH,
        )
        move.start()
        return move

    def sum_start(sweep, stage, value):
        sums_mine[sweep, stage] = value
        group = SUM_ORDER[sweep][stage]
        first = group * len(place_peers)
        moves = []
        for i, peer in enumerate((place_peers, shot_peers)[group]):
            moves.append(pltpu.make_async_remote_copy(
                src_ref=sums_mine.at[sweep, stage], dst_ref=sums_got.at[sweep, first + i],
                send_sem=sum_send.at[sweep, first + i], recv_sem=sum_recv.at[sweep, first + i],
                device_id=peer, device_id_type=MESH,
            ))
            moves[-1].start()
        return moves

    def sum_end(sweep, stage, value, moves):
        first = SUM_ORDER[sweep][stage] * len(place_peers)
        for i, move in enumerate(moves):
            move.wait_recv()
            value = value + sums_got[sweep, first + i]
        return value

    def ratio(value):
        return jnp.sum(value[:4], keepdims=True) / jnp.sum(value[4:], keepdims=True)

    lane = lax.broadcasted_iota(jnp.int32, (ROWS, 128), 1)

    def blend_near(recv, got, put, after=None):
        def shots(block, _):
            for i in (block * 2, block * 2 + 1):
                terms = shift_terms(lane, rows_near, rests_near, i)
                traces = [traces_near[j, i] for j in range(PARTNERS)]
                for source in range(groups):
                    own = got[recv][source, HALO + i, pl.ds(BASE, ROWS), :]

                    def load(j, row):
                        return got[recv][source, traces[j], pl.ds(row, ROWS), :]

                    put(i, source, blended_record(own, load, terms))
            if after is not None:
                after(block)
            return 0

        lax.fori_loop(0, 3, shots, 0)

    ahead = (tables.at[0], tables.at[1], mix_hi, mix_lo, y, v)
    behind = (kept, tables.at[2], tables.at[3], mix_hi, mix_lo, y, w, back)

    zero = jnp.zeros((ROWS, 128), F32)
    shifts = (rows_all, rests_all)
    sums = (zero, zero)
    bulk1 = []
    for recv in range(2):
        own[recv].wait()
        for copy in copies[recv]:
            copy.wait()
        forward(res.at[recv], u0.at[recv], *ahead)
        inverse(u0.at[recv], 0, q.at[recv], *behind)
        fill(sent1.at[recv], lambda at: q[recv, at, :])
        if recv == 0:
            bulk1.append(bulk_start(0, 0, sent1, got1))
        sums = blend(shifts, [(q.at[recv], image.at[recv])], res.at[recv], sums)
    value = fold(sums)
    stage0 = sum_start(0, 0, value)
    bulk1.append(bulk_start(0, 1, sent1, got1))

    for recv in range(2):
        inverse(u0.at[recv], 1, q.at[recv], *behind)
        forward(image.at[recv], u1.at[recv], *ahead)
        inverse(u1.at[recv], 1, other.at[recv], *behind)
    fill(raw_a, lambda at: q[0, at, :])
    fill(raw_b, lambda at: other[0, at, :])
    pairs = ((q, image_a), (other, image_b))
    value = sum_end(0, 0, value, stage0)
    stage1 = sum_start(0, 1, value)
    raw = raw_start()
    blend(shifts, [(f.at[recv], g.at[recv]) for f, g in pairs for recv in range(2)], chunk=4)
    value = sum_end(0, 1, value, stage1)
    step1 = ratio(value)

    def second(block, sums):
        num, den = sums
        for i in range(8):
            at = pl.ds(pl.multiple_of((block * 8 + i) * ROWS, ROWS), ROWS)
            for r in range(2):
                g = image_a[r, at, :] - step1 * image_b[r, at, :]
                num = num + (res[r, at, :] - step1 * image[r, at, :]) * g
                den = den + g * g
        return num, den

    value = fold(lax.fori_loop(0, SHOTS // 8, second, (zero, zero)))
    stage2 = sum_start(1, 0, value)
    bulk2 = []
    for recv in range(2):
        fill(sent2.at[recv], lambda at: q[recv, at, :] - step1 * other[recv, at, :])
        if recv == 1:
            bulk2_mate = bulk_start(1, 1, sent2, got2, 1)
        bulk2.append(bulk_start(1, recv, sent2, got2, 2))

    for move in raw:
        move.wait()
    for source in range(groups):
        for i in range(HALO):
            got20[source, 6 - 3 * core + i, BASE:BASE + ROWS, :] = (
                got_a[source, i] - step1 * got_b[source, i]
            )
    more2 = more_start(1, 0, got2)

    more1 = []
    for recv in range(2):
        for move in bulk1[recv]:
            move.wait()
        more1.append(more_start(0, recv, got1))
    for recv in range(2):
        more1[recv].wait()

        def put_left(i, source, g):
            old = staged[pl.ds(pl.multiple_of((source * 2 + recv) * 96 + i * ROWS, 8), ROWS), :]
            left[recv, i, source] = old - step1 * g

        blend_near(recv, got1, put_left)
        if recv == 0:
            value = sum_end(1, 0, value, stage2)
            stage3 = sum_start(1, 1, value)

    for move in bulk2[0]:
        move.wait()
    more2.wait()

    def put_late(i, source, g):
        late[i, source] = g

    blend_near(0, got2, put_late)
    for move in bulk2_mate:
        move.wait()
    more = more_start(1, 1, got2)
    value = sum_end(1, 1, value, stage3)
    step2 = ratio(value)

    def rows_of(recv, source):
        return slice((source * 2 + recv) * ROWS, (source * 2 + recv + 1) * ROWS)

    def combine(i, _):
        data = pl.ds(BASE, ROWS)
        for source in range(groups):
            at = rows_of(0, source)
            rows_d[i, at, :] = (
                step1 * got10[source, HALO + i, data, :] + step2 * got20[source, HALO + i, data, :]
            )
            rows_r[i, at, :] = left[0, i, source] - step2 * late[i, source]
        return 0

    def natural(source, target, i):
        for half in range(2):
            for n1 in range(ROWS):
                target[i, half * 8:(half + 1) * 8, n1 * 128:(n1 + 1) * 128] = source[
                    i, pl.ds(half * 128 + n1, 8, stride=ROWS), :
                ]

    def writes(block):
        two = pl.ds(block * 2, 2)
        return (
            pltpu.make_async_copy(done_d.at[two], out_d.at[two], out_sem.at[block]),
            pltpu.make_async_copy(done_r.at[two], out_r.at[two], out_sem.at[3 + block]),
        )

    def put_rest(i, source, g):
        at = rows_of(1, source)
        data = pl.ds(BASE, ROWS)
        rows_r[i, at, :] = left[1, i, source] - step2 * g
        rows_d[i, at, :] = (
            step1 * got11[source, HALO + i, data, :] + step2 * got21[source, HALO + i, data, :]
        )

    def finish_two(block):
        for i in (block * 2, block * 2 + 1):
            natural(rows_d, done_d, i)
            natural(rows_r, done_r, i)
        for write in writes(block):
            write.start()

    lax.fori_loop(0, 6, combine, 0)
    for move in bulk2[1]:
        move.wait()
    more.wait()
    blend_near(1, got2, put_rest, finish_two)
    for block in range(3):
        for write in writes(block):
            write.wait()

    for move in stage0 + stage1 + stage2 + stage3:
        move.wait_send()


def write_out(d, r, out_d, out_r, held_d, held_r, sem):
    parts = [
        (source.at[i], held.at[i], target.at[i])
        for source, held, target in ((d, held_d, out_d), (r, held_r, out_r))
        for i in range(6)
    ]
    loads = [pltpu.make_async_copy(p[0], p[1], sem.at[0, i]) for i, p in enumerate(parts)]
    stores = [pltpu.make_async_copy(p[1], p[2], sem.at[1, i]) for i, p in enumerate(parts)]
    for load in loads:
        load.start()
    for load, store in zip(loads, stores):
        load.wait()
        store.start()
    for store in stores:
        store.wait()


def solution(mesh):
    groups = mesh.shape["shot"]
    peers = groups - 1 + mesh.shape["rcv"] - 1
    table_hi, table_lo = time_tables()
    tables = np.stack([table_hi, table_lo, table_hi.swapaxes(1, 2), table_lo.swapaxes(1, 2)])
    mix_hi, mix_lo = shot_operands()
    order = mask_order()

    def body(blended, partners, offsets, fk_mask):
        hbm = pl.BlockSpec(memory_space=pltpu.HBM)
        out = jax.ShapeDtypeStruct(blended.shape, F32)
        dma = pltpu.SemaphoreType.DMA
        d, r = pl.pallas_call(
            lambda *refs: kernel(groups, *refs),
            out_shape=(out, out),
            in_specs=[hbm] * 8,
            out_specs=(hbm, hbm),
            scratch_shapes=[
                *[pltpu.SMEM((PARTNERS, SHOTS), jnp.int32)] * 4,
                *[pltpu.SMEM((PARTNERS, 6), jnp.int32)] * 3,
                pltpu.VMEM(mix_hi.shape, BF16),
                pltpu.VMEM(mix_lo.shape, BF16),
                pltpu.VMEM(blended.shape, F32),
                pltpu.VMEM((ITERATIONS * SHOTS, FREQS), jnp.int32),
                pltpu.VMEM((16 * 96, 128), F32),
                pltpu.VMEM((2, SHOTS * ROWS, 128), F32),
                pltpu.VMEM((2, (SHOTS + 1) * PITCH, 128), F32),
                pltpu.VMEM((2, (SHOTS + 1) * PITCH, 128), F32),
                pltpu.VMEM((2, SHOTS * ROWS, 128), F32),
                pltpu.VMEM((2, SHOTS * ROWS, 128), F32),
                pltpu.VMEM((2, SHOTS * ROWS, 128), F32),
                pltpu.VMEM((2, SHOTS + 2 * HALO, ROWS, 128), F32),
                pltpu.VMEM((2, SHOTS + 2 * HALO, ROWS, 128), F32),
                *[pltpu.VMEM((SHOTS + 2 * HALO, ROWS, 128), F32)] * 2,
                *[pltpu.VMEM((groups, HALO, ROWS, 128), F32)] * 2,
                *[pltpu.VMEM((groups, NEAR + 1, PITCH, 128), F32)] * 4,
                pltpu.VMEM((2, 6, groups, ROWS, 128), F32),
                pltpu.VMEM((6, groups, ROWS, 128), F32),
                pltpu.VMEM((6, 16 * ROWS, 128), F32),
                pltpu.VMEM((6, 16 * ROWS, 128), F32),
                pltpu.VMEM(blended.shape, F32),
                pltpu.VMEM(blended.shape, F32),
                pltpu.VMEM((GROUPS, TRACES, 256), BF16),
                pltpu.VMEM((192, FREQS), BF16),
                pltpu.VMEM((192, FREQS), BF16),
                pltpu.VMEM((GROUPS, SHOTS, 256), F32),
                pltpu.VMEM((2, 96, FREQS), F32),
                pltpu.VMEM((2, 96, FREQS), F32),
                pltpu.VMEM((4, GROUPS, 256, 256), BF16),
                pltpu.VMEM((FREQS, FREQS), BF16),
                pltpu.VMEM((ITERATIONS * SHOTS, FREQS), F32),
                pltpu.VMEM((ITERATIONS, 2, 8, 128), F32),
                pltpu.VMEM((ITERATIONS, peers, 8, 128), F32),
                dma((8,)),
                dma((groups - 1, 2)),
                dma((groups - 1, 2)),
                dma((ITERATIONS, groups - 1, 3)),
                dma((ITERATIONS, groups - 1, 3)),
                dma((2, groups - 1)),
                dma((2, groups - 1)),
                dma((ITERATIONS, 2)),
                dma((ITERATIONS, 2)),
                dma((10,)),
                dma((6,)),
                dma((ITERATIONS, peers)),
                dma((ITERATIONS, peers)),
            ],
            compiler_params=pltpu.CompilerParams(
                collective_id=0, has_side_effects=True, vmem_limit_bytes=56 * 2**20
            ),
            name="deblend",
        )(
            partners.T, offsets.T, blended, fk_mask.reshape(ITERATIONS * SHOTS, FREQS),
            jnp.asarray(order), jnp.asarray(tables), jnp.asarray(mix_hi), jnp.asarray(mix_lo),
        )
        return pl.pallas_call(
            write_out,
            out_shape=(out, out),
            in_specs=[hbm, hbm],
            out_specs=(hbm, hbm),
            scratch_shapes=[pltpu.VMEM(blended.shape, F32), pltpu.VMEM(blended.shape, F32), dma((2, 12))],
            compiler_params=pltpu.CompilerParams(vmem_limit_bytes=56 * 2**20),
            name="write_out",
        )(d, r)

    in_specs = (P("shot", "rcv", None), P(), P(), P())
    out_specs = (P("shot", "rcv", None), P("shot", "rcv", None))
    return jax.shard_map(body, mesh=mesh, in_specs=in_specs, out_specs=out_specs, check_vma=False)
```
